32 devices in a mesh: dp: 16 (over z, y, x), tensor: 2 (over core).
Axes of the slice: x: 2, y: 2, z: 4, core: 2. Of those that a mesh axis runs over, the one named last changes fastest.
Arguments:
- frames: bfloat16 [32768, 768], P('dp')
- cotangent: bfloat16 [32768, 768], P('dp'), may hold values from -6 to 6
- segment_ids: int32 [32768], P('dp'), may hold values from 0 to 9, as said below
- pad_mask: int32 [32768], P('dp'), may hold values from 0 to 1, as said below
- attention_weight: bfloat16 [4, 768, 768], P(None, None, 'tensor')
- feedforward_weight: bfloat16 [2, 768, 3072], P(None, None, 'tensor')
- head_bias: float32 [2, 2, 384], P(None, 'tensor'), may hold values from -3 to 3
- hidden_bias: float32 [2, 1536], P('tensor'), may hold values from -3 to 3
- norm_vectors: float32 [6, 768], replicated
- attention_first: float32 [4, 768, 768], P(None, 'dp', 'tensor')
- attention_second: float32 [4, 768, 768], P(None, 'dp', 'tensor')
- feedforward_first: float32 [2, 768, 3072], P(None, 'dp', 'tensor')
- feedforward_second: float32 [2, 768, 3072], P(None, 'dp', 'tensor')
- head_first: float32 [2, 2, 384], P(None, 'tensor', 'dp')
- head_second: float32 [2, 2, 384], P(None, 'tensor', 'dp')
- hidden_first: float32 [2, 1536], P('tensor', 'dp')
- hidden_second: float32 [2, 1536], P('tensor', 'dp')
- vector_first: float32 [6, 768], P(None, 'dp')
- vector_second: float32 [6, 768], P(None, 'dp')
Outputs:
- layer_output: bfloat16 [32768, 768], P('dp')
- input_gradient: float32 [32768, 768], P('dp')
- gradient_norm: float32 [], replicated
- new_attention_first: float32 [4, 768, 768], P(None, 'dp', 'tensor')
- new_attention_second: float32 [4, 768, 768], P(None, 'dp', 'tensor')
- new_attention: float32 [4, 768, 768], P(None, 'dp', 'tensor')
- new_feedforward_first: float32 [2, 768, 3072], P(None, 'dp', 'tensor')
- new_feedforward_second: float32 [2, 768, 3072], P(None, 'dp', 'tensor')
- new_feedforward: float32 [2, 768, 3072], P(None, 'dp', 'tensor')
- new_head_first: float32 [2, 2, 384], P(None, 'tensor', 'dp')
- new_head_second: float32 [2, 2, 384], P(None, 'tensor', 'dp')
- new_head_bias: float32 [2, 2, 384], P(None, 'tensor', 'dp')
- new_hidden_first: float32 [2, 1536], P('tensor', 'dp')
- new_hidden_second: float32 [2, 1536], P('tensor', 'dp')
- new_hidden_bias: float32 [2, 1536], P('tensor', 'dp')
- new_vector_first: float32 [6, 768], P(None, 'dp')
- new_vector_second: float32 [6, 768], P(None, 'dp')
- new_vectors: float32 [6, 768], P(None, 'dp')
The draws below stay inside these ranges and needn't reach their ends.
Inputs may be any that keep to these rules, and one draw needn't show every extreme that they name: `segment_ids`: within each row of 1024 frames the ids start at 0 and never fall; each id covers one whole clip of 100 to 400 frames, and the padding at a row's end carries the id of the row's last clip; in every draw some row is packed with clips of exactly 100 frames. `pad_mask`: 1 on a row's frames up to the end of its last whole clip, 0 on the padding after it.
All inputs are finite; a program needn't handle non-finite values.
Results may differ from the reference program's by a relative error of at most 0.02.
Values may be sent and summed in bfloat16 or wider, within the bound.
No kernel may reach another device: no remote copies, remote signals or barrier semaphores. Data moves between devices by JAX's collectives and lax.ppermute only.
A program may use at most 192 MiB of HBM per device.

```python
import math
import jax
import jax.numpy as jnp
from jax import lax

D = 768
H = 12
HD = 64
FF = 3072
SEQ = 1024
CLIP_MIN = 100
CLIP_MAX = 400
STEP = 10
HEAD_COLS = 384
UNIT_COLS = 1536
TOKENS = 32768
N_TENSOR = 2


def base_draw(key, shape):
    return jax.random.normal(key, shape, jnp.float32)


def rising(key, shape, width, ratio):
    place = jnp.arange(width, dtype=jnp.float32) / width
    return jnp.power(ratio, place) * jax.random.uniform(key, shape, jnp.float32, 0.8, 1.25)


def draw_frames(key, part):
    key = jax.random.fold_in(key, 11)
    first_key, second_key = jax.random.split(key)
    ramp = 0.6 * rising(second_key, (D,), D, 3.0)
    return (base_draw(first_key, (TOKENS, D)) * ramp).astype(jnp.bfloat16)


def draw_attention_weight(key, part):
    key = jax.random.fold_in(key, 12)
    first_key, second_key = jax.random.split(key)
    ramp = 0.75 * rising(second_key, (4, 1, D), D, 2.0)
    factor = jnp.array([1.0, 1.0, 1.0, 6.0], jnp.float32).reshape(4, 1, 1) / jnp.sqrt(jnp.float32(D))
    return (base_draw(first_key, (4, D, D)) * ramp * factor).astype(jnp.bfloat16)


def draw_feedforward_weight(key, part):
    key = jax.random.fold_in(key, 13)
    first_key, second_key = jax.random.split(key)
    ramp = 0.75 * rising(second_key, (2, 1, FF), FF, 2.0)
    factor = jnp.stack([1.0 / jnp.sqrt(jnp.float32(D)), 1.0 / jnp.sqrt(jnp.float32(FF))]).reshape(2, 1, 1)
    return (base_draw(first_key, (2, D, FF)) * ramp * factor).astype(jnp.bfloat16)


def draw_norm_vectors(key, part):
    key = jax.random.fold_in(key, 14)
    first_key, second_key = jax.random.split(key)
    shifts = 0.3 * base_draw(first_key, (6, D))
    gains = 0.6 * jnp.power(3.0, jnp.arange(D, dtype=jnp.float32) / D) * jax.random.uniform(second_key, (6, D), jnp.float32, 0.85, 1.15)
    is_gain = jnp.array([0.0, 1.0, 0.0, 0.0, 1.0, 0.0], jnp.float32).reshape(6, 1)
    return is_gain * gains + (1.0 - is_gain) * shifts


def pack_rows(key):
    key = jax.random.fold_in(key, 40)
    length_key, row_key = jax.random.split(key)
    rows = TOKENS // SEQ
    count = SEQ // CLIP_MIN + 1
    lengths = jax.random.randint(length_key, (rows, count), CLIP_MIN, CLIP_MAX + 1, dtype=jnp.int32)
    packed_row = jax.random.randint(row_key, (), 0, rows, dtype=jnp.int32)
    row_place = jnp.arange(rows, dtype=jnp.int32)
    lengths = jnp.where(row_place[:, None] == packed_row, jnp.int32(CLIP_MIN), lengths)
    ends = jnp.cumsum(lengths, axis=1)
    inside = ends <= SEQ
    whole = jnp.sum(inside.astype(jnp.int32), axis=1)
    filled = jnp.max(jnp.where(inside, ends, 0), axis=1)
    place = jnp.arange(SEQ, dtype=jnp.int32)
    numbers = jnp.sum((ends[:, None, :] <= place[None, :, None]).astype(jnp.int32), axis=2)
    numbers = jnp.minimum(numbers, whole[:, None] - 1)
    valid = (place[None, :] < filled[:, None]).astype(jnp.int32)
    return (numbers.reshape(-1), valid.reshape(-1))


def draw_segment_ids(key, part):
    return pack_rows(key)[0]


def draw_pad_mask(key, part):
    return pack_rows(key)[1]


def grad_size(strength):
    count = 4.0 * D * D + 2.0 * D * FF + 8.0 * D + FF
    return strength / jnp.sqrt(jnp.float32(count))


def first_draw(key, shape, strength):
    return jax.random.normal(key, shape, jnp.float32) * (0.1 / 0.9) * grad_size(strength)


def second_draw(key, shape, strength):
    spread = jnp.exp(jax.random.uniform(key, shape, jnp.float32, 0.0, 1.3862944))
    size = grad_size(strength)
    return spread * (0.001 / 0.999) * size * size


def draw_attention_first(key, part):
    key = jax.random.fold_in(key, 21)
    return first_draw(key, (4, D, D), 1.0)


def draw_attention_second(key, part):
    key = jax.random.fold_in(key, 22)
    return second_draw(key, (4, D, D), 1.0)


def draw_feedforward_first(key, part):
    key = jax.random.fold_in(key, 23)
    return first_draw(key, (2, D, FF), 1.0)


def draw_feedforward_second(key, part):
    key = jax.random.fold_in(key, 24)
    return second_draw(key, (2, D, FF), 1.0)


def draw_head_first(key, part):
    key = jax.random.fold_in(key, 25)
    return first_draw(key, (2, N_TENSOR, D // N_TENSOR), 3.0)


def draw_head_second(key, part):
    key = jax.random.fold_in(key, 26)
    return second_draw(key, (2, N_TENSOR, D // N_TENSOR), 3.0)


def draw_hidden_first(key, part):
    key = jax.random.fold_in(key, 27)
    return first_draw(key, (N_TENSOR, FF // N_TENSOR), 0.75)


def draw_hidden_second(key, part):
    key = jax.random.fold_in(key, 28)
    return second_draw(key, (N_TENSOR, FF // N_TENSOR), 0.75)


def draw_vector_first(key, part):
    key = jax.random.fold_in(key, 29)
    return first_draw(key, (6, D), 3.0)


def draw_vector_second(key, part):
    key = jax.random.fold_in(key, 30)
    return second_draw(key, (6, D), 3.0)


def block_levels(rng, dims, cuts, least, high):
    loudness = 1.0
    for axis_at, shards_of in cuts:
        heights = jax.random.uniform(jax.random.fold_in(jax.random.fold_in(rng, 6), axis_at), (shards_of,), jnp.float32, least / len(cuts), high / len(cuts))
        loudness = loudness * jnp.repeat(jnp.exp(heights), dims[axis_at] // shards_of).reshape((-1,) + (1,) * (len(dims) - 1 - axis_at))
    return loudness


def centred(rng, shape, scale, reach, shards=(), kind=jnp.bfloat16):
    values = jax.random.normal(rng, shape, jnp.float32) * scale
    if len(shards) > 0:
        values = block_levels(rng, shape, shards, -0.22, 0.18) * values
    return jnp.clip(values, min=-reach, max=reach).astype(kind)


def setup_inputs(seed: int = 0) -> dict:
    arg_keys = jax.random.split(jax.random.key(seed), 20)
    return {
        "frames": draw_frames(jax.random.fold_in(arg_keys[19], 71), 0),
        "cotangent": centred(arg_keys[1], (TOKENS, D), 1.0, 6.0, ((0, 16),)),
        "segment_ids": draw_segment_ids(jax.random.fold_in(arg_keys[19], 71), 0),
        "pad_mask": draw_pad_mask(jax.random.fold_in(arg_keys[19], 71), 0),
        "attention_weight": draw_attention_weight(jax.random.fold_in(arg_keys[19], 71), 0),
        "feedforward_weight": draw_feedforward_weight(jax.random.fold_in(arg_keys[19], 71), 0),
        "head_bias": centred(arg_keys[6], (2, N_TENSOR, HEAD_COLS), 0.5, 3.0, ((1, 2),), jnp.float32),
        "hidden_bias": centred(arg_keys[7], (N_TENSOR, UNIT_COLS), 0.5, 3.0, ((0, 2),), jnp.float32),
        "norm_vectors": draw_norm_vectors(jax.random.fold_in(arg_keys[19], 71), 0),
        "attention_first": draw_attention_first(jax.random.fold_in(arg_keys[19], 71), 0),
        "attention_second": draw_attention_second(jax.random.fold_in(arg_keys[19], 71), 0),
        "feedforward_first": draw_feedforward_first(jax.random.fold_in(arg_keys[19], 71), 0),
        "feedforward_second": draw_feedforward_second(jax.random.fold_in(arg_keys[19], 71), 0),
        "head_first": draw_head_first(jax.random.fold_in(arg_keys[19], 71), 0),
        "head_second": draw_head_second(jax.random.fold_in(arg_keys[19], 71), 0),
        "hidden_first": draw_hidden_first(jax.random.fold_in(arg_keys[19], 71), 0),
        "hidden_second": draw_hidden_second(jax.random.fold_in(arg_keys[19], 71), 0),
        "vector_first": draw_vector_first(jax.random.fold_in(arg_keys[19], 71), 0),
        "vector_second": draw_vector_second(jax.random.fold_in(arg_keys[19], 71), 0),
    }


@jax.custom_vjp
def low(v):
    return lax.optimization_barrier(v.astype(jnp.bfloat16)).astype(jnp.float32)

@jax.custom_vjp
def low_back(v):
    return v

def low_keep(v):
    return (low(v), None)

def low_pass(kept, grad):
    return (grad,)

def back_keep(v):
    return (v, None)

def back_low(kept, grad):
    return (low(grad),)
low.defvjp(low_keep, low_pass)
low_back.defvjp(back_keep, back_low)

def product(pattern, left, right):
    return jnp.einsum(pattern, left, right, precision=lax.Precision.HIGHEST)

def layer_norm(value, gain, shift):
    center = value - lax.optimization_barrier(jnp.mean(value, axis=-1, keepdims=True))
    inv_std = lax.rsqrt(lax.optimization_barrier(jnp.mean(center * center, axis=-1, keepdims=True)) + 1e-05)
    return center * inv_std * gain + shift

def layer_rows(params, rows, segments, valid):
    attention, feedforward, head_vec, hidden_vec, vectors = params
    group = rows.shape[0]
    scale = HD ** (-0.5)
    head_flat = head_vec.reshape(2, D)
    split_shape = (group, SEQ, H, HD)
    query = low(low_back(product('rsd,de->rse', rows, attention[0]) + head_flat[0]))
    keys = low(low_back(product('rsd,de->rse', rows, attention[1])))
    values = low(low_back(product('rsd,de->rse', rows, attention[2]) + head_flat[1]))
    scores = low_back(product('rqhd,rkhd->rhqk', query.reshape(split_shape), keys.reshape(split_shape)) * scale)
    allowed = (segments[:, :, None] == segments[:, None, :]) & (valid[:, None, :] == 1)
    scores = jnp.where(allowed[:, None], scores, -1000000000.0)
    probs = low(jax.nn.softmax(scores, axis=-1))
    mixed = low(low_back(product('rhqk,rkhd->rqhd', probs, values.reshape(split_shape))))
    mixed = mixed.reshape(group, SEQ, N_TENSOR, D // N_TENSOR)
    out_weight = attention[3].reshape(D, N_TENSOR, D // N_TENSOR)
    parts = low(product('rstc,dtc->trsd', mixed, out_weight))
    first = rows + low_back(lax.optimization_barrier(jnp.sum(parts, axis=0))) + vectors[0]
    first_norm = layer_norm(first, vectors[1], vectors[2])
    first_low = low(first_norm)
    up_pre = low_back(product('rsd,dh->rsh', first_low, feedforward[0]) + hidden_vec.reshape(FF))
    act = low(jax.nn.gelu(up_pre, approximate=False))
    act_split = act.reshape(group, SEQ, N_TENSOR, FF // N_TENSOR)
    down_weight = feedforward[1].reshape(D, N_TENSOR, FF // N_TENSOR)
    parts_two = low(product('rsth,dth->trsd', act_split, down_weight))
    second = first_norm + low_back(lax.optimization_barrier(jnp.sum(parts_two, axis=0))) + vectors[3]
    return layer_norm(second, vectors[4], vectors[5])

def adam_step(grad, first, second, weight, factor, rate, decay):
    clipped = grad * factor
    first_new = 0.9 * first + 0.1 * clipped
    second_new = 0.999 * second + 0.001 * clipped * clipped
    mean_hat = first_new / (1.0 - 0.9 ** STEP)
    var_hat = second_new / (1.0 - 0.999 ** STEP)
    weight_new = weight - rate * (mean_hat / (jnp.sqrt(var_hat) + 1e-08) + decay * weight)
    return (first_new, second_new, weight_new)

def reference(frames, cotangent, segment_ids, pad_mask, attention_weight, feedforward_weight, head_bias, hidden_bias, norm_vectors, attention_first, attention_second, feedforward_first, feedforward_second, head_first, head_second, hidden_first, hidden_second, vector_first, vector_second):
    params = (attention_weight.astype(jnp.float32), feedforward_weight.astype(jnp.float32), head_bias, hidden_bias, norm_vectors)
    frames32 = frames.astype(jnp.float32)
    rows_total = TOKENS // SEQ
    group = math.gcd(rows_total, max(1, 4096 // SEQ))
    blocks_seg = segment_ids.reshape(rows_total // group, group, SEQ)
    blocks_valid = pad_mask.reshape(rows_total // group, group, SEQ)

    def forward(weights, inputs):

        def group_fn(block):
            return layer_rows(weights, block[0], block[1], block[2])
        blocks = (inputs.reshape(rows_total // group, group, SEQ, D), blocks_seg, blocks_valid)
        return lax.map(jax.checkpoint(group_fn), blocks).reshape(TOKENS, D)
    output, pullback = jax.vjp(forward, params, frames32)
    weight_grads, input_gradient = pullback(cotangent.astype(jnp.float32) * pad_mask[:, None].astype(jnp.float32))
    total = jnp.float32(0.0)
    for grad in weight_grads:
        total = total + jnp.sum(grad * grad)
    gradient_norm = jnp.sqrt(total)
    factor = jnp.minimum(1.0, 1.0 / (gradient_norm + 1e-06))
    att = adam_step(weight_grads[0], attention_first, attention_second, params[0], factor, 0.05, 0.01)
    ffw = adam_step(weight_grads[1], feedforward_first, feedforward_second, params[1], factor, 0.05, 0.01)
    hed = adam_step(weight_grads[2], head_first, head_second, params[2], factor, 0.5, 0.0)
    hid = adam_step(weight_grads[3], hidden_first, hidden_second, params[3], factor, 0.5, 0.0)
    vec = adam_step(weight_grads[4], vector_first, vector_second, params[4], factor, 0.5, 0.0)
    return (output.astype(jnp.bfloat16), input_gradient, gradient_norm, att[0], att[1], att[2], ffw[0], ffw[1], ffw[2], hed[0], hed[1], hed[2], hid[0], hid[1], hid[2], vec[0], vec[1], vec[2])
```

```python
import functools

import jax
import jax.numpy as jnp
from jax import lax
from jax.experimental import pallas as pl
from jax.experimental.pallas import tpu as pltpu
from jax.sharding import PartitionSpec as P

HD = 64
SEQ = 1024
STEP = 10
LANES = 128
QB = 256
BIG = 1e30
LOG2E = 1.4426950408889634
LN2 = 0.6931471805599453
WINDOWS = (512, 640, 768, 1024)
VMEM_LIMIT = 60 * 2**20
BF = jnp.bfloat16
F32 = jnp.float32


def nn(a, b):
    return jnp.dot(a, b, preferred_element_type=F32)


def nt(a, b):
    return lax.dot_general(a, b, (((1,), (1,)), ((), ())), preferred_element_type=F32)


def ds(start, size, step):
    return pl.ds(pl.multiple_of(start, step), size)


def params(**extra):
    return pltpu.CompilerParams(vmem_limit_bytes=VMEM_LIMIT, **extra)


def cost(flops, bytes_accessed, transcendentals=0):
    return pl.CostEstimate(
        flops=int(flops), bytes_accessed=int(bytes_accessed), transcendentals=int(transcendentals)
    )


def vmem(count):
    return [pl.BlockSpec(memory_space=pltpu.VMEM)] * count


SMEM = pl.BlockSpec(memory_space=pltpu.SMEM)
ANY = pl.BlockSpec(memory_space=pl.ANY)


def lane_row(dtype=jnp.int32):
    return lax.broadcasted_iota(jnp.int32, (1, LANES), 1)


def half_masks():
    lane = lane_row()
    low = jnp.where(lane < HD, 1.0, 0.0)
    return (low.astype(BF), (1.0 - low).astype(BF))


def norm_rows(value):
    center = value - jnp.mean(value, axis=-1, keepdims=True)
    inv_std = lax.rsqrt(jnp.mean(center * center, axis=-1, keepdims=True) + 1e-05)
    return center * inv_std, inv_std


def norm_back(grad, normed, inv_std, gain):
    scaled = grad * gain
    mean_one = jnp.mean(scaled, axis=-1, keepdims=True)
    mean_two = jnp.mean(scaled * normed, axis=-1, keepdims=True)
    return inv_std * (scaled - mean_one - normed * mean_two)


def col_sum(value):
    return jnp.sum(value, axis=0, keepdims=True)


def attention_kernel(
    win_ref, x_ref, wm_ref, wo_ref, bm_ref, bo_ref, augq_ref, augk_ref, vec_ref,
    q_ref, k_ref, v_ref, augl_ref, mixed_ref, n1_ref, inv_ref, low_ref,
    w_s, vt_s, mt_s, lse_s, sem,
):
    cols = wm_ref.shape[2]
    copies = []
    for j in range(4):
        for side, ref in enumerate((wm_ref, wo_ref)):
            copies.append(
                pltpu.make_async_copy(
                    ref.at[j], w_s.at[j, :, side * cols : (side + 1) * cols], sem.at[2 * j + side]
                )
            )
    for copy in copies:
        copy.start()
    bias = [
        jnp.concatenate([bm_ref[j : j + 1, :], bo_ref[j : j + 1, :]], axis=1) for j in range(2)
    ]
    copies[0].wait()
    copies[1].wait()
    q_ref[...] = ((nn(x_ref[...], w_s[0]) + bias[0]) * (HD ** (-0.5) * LOG2E)).astype(BF)
    copies[2].wait()
    copies[3].wait()
    k_ref[...] = nn(x_ref[...], w_s[1]).astype(BF)
    copies[4].wait()
    copies[5].wait()
    v_ref[...] = (nn(x_ref[...], w_s[2]) + bias[1]).astype(BF)
    vt_s[...] = v_ref[...].T
    lse_s[...] = jnp.zeros_like(lse_s)
    pairs = q_ref.shape[1] // LANES

    def block(i, carry):
        rows = ds(i * QB, QB, QB)
        begin = win_ref[0, i]
        kind = win_ref[1, i]

        def heads(width):
            span = ds(begin, width, LANES)

            def pair(p, c):
                tile = ds(p * LANES, LANES, LANES)
                right = jnp.concatenate([q_ref[rows, tile], augq_ref[rows, :]], axis=1)
                key = k_ref[span, tile]
                aug = augk_ref[span, :]
                ones = jnp.ones((16, width), BF)
                for a, mask in enumerate(half_masks()):
                    scores = nt(jnp.concatenate([key * mask, aug], axis=1), right)
                    top = jnp.max(scores, axis=0, keepdims=True)
                    probs = jnp.exp2(scores - top).astype(BF)
                    part = ds(p * LANES + a * HD, HD, HD)
                    out = nn(jnp.concatenate([vt_s[part, span], ones], axis=0), probs)
                    total = out[HD : HD + 1, :]
                    mt_s[part, rows] = (out[:HD, :] * (1.0 / total)).astype(BF)
                    lse = top + jnp.log2(total)
                    for piece in range(3):
                        lse_s[pl.ds(16 * (piece + 1) + 2 * p + a, 1), rows] = lse
                return c

            lax.fori_loop(0, pairs, pair, 0)

        for index, width in enumerate(WINDOWS):
            pl.when(kind == index)(functools.partial(heads, width))
        return carry

    lax.fori_loop(0, SEQ // QB, block, 0)
    mixed_ref[...] = mt_s[...].T
    lse = lse_s[...].T
    high = lse.astype(BF).astype(F32)
    mid = (lse - high).astype(BF).astype(F32)
    lane = lane_row()
    piece = jnp.where(lane < 32, high, jnp.where(lane < 48, mid, lse - high - mid))
    augl_ref[...] = (augq_ref[...].astype(F32) - piece).astype(BF)
    copies[6].wait()
    copies[7].wait()

    def finish(r, carry):
        rows = ds(r * QB, QB, QB)
        first = x_ref[rows, :].astype(F32) + nt(mixed_ref[rows, :], w_s[3]) + vec_ref[0:1, :]
        normed, inv_std = norm_rows(first)
        n1_ref[rows, :] = normed
        inv_ref[rows, :] = jnp.broadcast_to(inv_std, (QB, LANES))
        low_ref[rows, :] = (normed * vec_ref[1:2, :] + vec_ref[2:3, :]).astype(BF)
        return carry

    lax.fori_loop(0, SEQ // QB, finish, 0)


def attention_forward(win, x, att_m, att_o, bias_m, bias_o, augq, augk, vectors):
    width = x.shape[1]
    wide = jax.ShapeDtypeStruct((SEQ, width), BF)
    thin = jax.ShapeDtypeStruct((SEQ, LANES), BF)
    return pl.pallas_call(
        attention_kernel,
        out_shape=[
            wide, wide, wide, thin, wide,
            jax.ShapeDtypeStruct((SEQ, width), F32),
            jax.ShapeDtypeStruct((SEQ, LANES), F32),
            wide,
        ],
        in_specs=[SMEM] + vmem(1) + [ANY, ANY] + vmem(5),
        out_specs=vmem(8),
        scratch_shapes=[
            pltpu.VMEM((4, width, width), BF),
            pltpu.VMEM((width, SEQ), BF),
            pltpu.VMEM((width, SEQ), BF),
            pltpu.VMEM((LANES, SEQ), F32),
            pltpu.SemaphoreType.DMA((8,)),
        ],
        compiler_params=params(),
        cost_estimate=cost(15e9, 20e6, 10e6),
        name="attention_forward",
    )(win, x, att_m, att_o, bias_m, bias_o, augq, augk, vectors)


def gelu_pair(value):
    phi = 0.5 + 0.5 * lax.erf(value * 0.7071067811865476)
    low = value.astype(BF)
    density = jnp.exp2(low * low * BF(-0.5 * LOG2E)) * BF(0.3989422804014327)
    return (value * phi).astype(BF), phi.astype(BF) + low * density


def weight_copies(sources, target, sem, base):
    units = sources[0].shape[-1]
    return [
        pltpu.make_async_copy(
            ref, target.at[:, side * units : (side + 1) * units], sem.at[base + side]
        )
        for side, ref in enumerate(sources)
    ]


def forward_kernel(
    low_ref, n1_ref, fm_ref, fo_ref, hm_ref, ho_ref, cot_ref, augk_ref, vec_ref,
    out_ref, g2_ref, slope_ref, dm_ref, do_ref, sum_ref,
    w1_s, w2_s, act_s, glow_s, glt_s, sem,
):
    units = fm_ref.shape[2]
    copies = weight_copies((fm_ref.at[0], fo_ref.at[0]), w1_s, sem, 0)
    copies += weight_copies((fm_ref.at[1], fo_ref.at[1]), w2_s, sem, 2)
    for copy in copies:
        copy.start()
    sum_ref[...] = jnp.zeros_like(sum_ref)
    for side, bias in enumerate((hm_ref, ho_ref)):
        copies[side].wait()

        def up(c, carry, side=side, bias=bias):
            here = ds(c * QB, QB, QB)
            there = ds(side * units + c * QB, QB, QB)
            act, slope = gelu_pair(nn(low_ref[...], w1_s[:, there]) + bias[0:1, here])
            act_s[:, there] = act
            slope_ref[:, there] = slope
            return carry

        lax.fori_loop(0, units // QB, up, 0)
    copies[2].wait()
    copies[3].wait()

    def rows_step(r, carry):
        rows = ds(r * QB, QB, QB)
        ffn = nt(act_s[rows, :], w2_s[...])
        first_norm = n1_ref[rows, :] * vec_ref[1:2, :] + vec_ref[2:3, :]
        n2, inv_std = norm_rows(first_norm + ffn + vec_ref[3:4, :])
        out_ref[rows, :] = (n2 * vec_ref[4:5, :] + vec_ref[5:6, :]).astype(BF)
        valid = 1.0 - augk_ref[rows, 10:11].astype(F32)
        grad = cot_ref[rows, :].astype(F32) * valid
        back = norm_back(grad, n2, inv_std, vec_ref[4:5, :])
        g2_ref[rows, :] = back
        glow_s[rows, :] = back.astype(BF)
        sum_ref[3:4, :] += col_sum(back)
        sum_ref[4:5, :] += col_sum(grad * n2)
        sum_ref[5:6, :] += col_sum(grad)
        return carry

    lax.fori_loop(0, SEQ // QB, rows_step, 0)
    glt_s[...] = glow_s[...].T
    for side, target in ((1, do_ref), (0, dm_ref)):

        def down(c, carry, side=side, target=target):
            there = ds(side * units + c * QB, QB, QB)
            target[:, ds(c * QB, QB, QB)] = nn(glt_s[...], act_s[:, there]).astype(BF)
            return carry

        lax.fori_loop(0, units // QB, down, 0)


def ffn_forward(low, n1, ffw_m, ffw_o, hid_m, hid_o, cot, augk, vectors):
    width = low.shape[1]
    units = ffw_m.shape[2]
    shape = jax.ShapeDtypeStruct
    return pl.pallas_call(
        forward_kernel,
        out_shape=[
            shape((SEQ, width), BF),
            shape((SEQ, width), F32),
            shape((SEQ, 2 * units), BF),
            shape((width, units), BF),
            shape((width, units), BF),
            shape((8, width), F32),
        ],
        in_specs=vmem(2) + [ANY, ANY] + vmem(5),
        out_specs=vmem(6),
        scratch_shapes=[
            pltpu.VMEM((width, 2 * units), BF),
            pltpu.VMEM((width, 2 * units), BF),
            pltpu.VMEM((SEQ, 2 * units), BF),
            pltpu.VMEM((SEQ, width), BF),
            pltpu.VMEM((width, SEQ), BF),
            pltpu.SemaphoreType.DMA((4,)),
        ],
        compiler_params=params(),
        cost_estimate=cost(14.5e9, 30e6, 6e6),
        name="ffn_forward",
    )(low, n1, ffw_m, ffw_o, hid_m, hid_o, cot, augk, vectors)


def backward_kernel(
    g2_ref, slope_ref, n1_ref, inv_ref, low_ref, mixed_ref, fm_ref, fo_ref, am_ref, ao_ref,
    vec_ref, pick_ref,
    um_ref, uo_ref, hm_ref, ho_ref, g1_ref, om_ref, oo_ref, gm_ref, augd_ref, sum_ref,
    w1_s, w2_s, wo_s, gup_s, glow_s, lowt_s, sem,
):
    units = fm_ref.shape[2]
    cols = am_ref.shape[2]
    copies = weight_copies((fm_ref.at[1], fo_ref.at[1]), w2_s, sem, 0)
    copies += weight_copies((fm_ref.at[0], fo_ref.at[0]), w1_s, sem, 2)
    copies += weight_copies((am_ref.at[3], ao_ref.at[3]), wo_s, sem, 4)
    for copy in copies:
        copy.start()
    sum_ref[...] = jnp.zeros_like(sum_ref)
    glow_s[...] = g2_ref[...].astype(BF)
    lowt_s[...] = low_ref[...].T
    copies[0].wait()
    copies[1].wait()
    for side, target, bias in ((1, uo_ref, ho_ref), (0, um_ref, hm_ref)):

        def up(c, carry, side=side, target=target, bias=bias):
            here = ds(c * QB, QB, QB)
            there = ds(side * units + c * QB, QB, QB)
            grad = (nn(glow_s[...], w2_s[:, there]) * slope_ref[:, there].astype(F32)).astype(BF)
            gup_s[:, there] = grad
            bias[0:1, here] = col_sum(grad.astype(F32))
            target[:, here] = nn(lowt_s[...], grad).astype(BF)
            return carry

        lax.fori_loop(0, units // QB, up, 0)
    copies[2].wait()
    copies[3].wait()

    def rows_step(r, carry):
        rows = ds(r * QB, QB, QB)
        grad = nt(gup_s[rows, :], w1_s[...]) + g2_ref[rows, :]
        n1 = n1_ref[rows, :]
        back = norm_back(grad, n1, inv_ref[rows, 0:1], vec_ref[1:2, :])
        g1_ref[rows, :] = back
        glow_s[rows, :] = back.astype(BF)
        sum_ref[0:1, :] += col_sum(back)
        sum_ref[1:2, :] += col_sum(grad * n1)
        sum_ref[2:3, :] += col_sum(grad)
        return carry

    lax.fori_loop(0, SEQ // QB, rows_step, 0)
    copies[4].wait()
    copies[5].wait()
    mixed = mixed_ref[...]
    lowt_s[...] = glow_s[...].T
    product = nn(lowt_s[...], mixed).astype(BF)
    om_ref[...] = product[:, :cols]
    oo_ref[...] = product[:, cols:]
    gm_ref[...] = nn(glow_s[...], wo_s[...]).astype(BF)
    lane = lane_row()
    for r in range(SEQ // QB):
        rows = slice(r * QB, (r + 1) * QB)
        both = gm_ref[rows, :].astype(F32) * mixed_ref[rows, :].astype(F32)
        high = both.astype(BF)
        dots = nn(high, pick_ref[...]) + nn((both - high.astype(F32)).astype(BF), pick_ref[...])
        dot_high = dots.astype(BF).astype(F32)
        augd_ref[rows, :] = (-jnp.where(lane < 32, dot_high, dots - dot_high)).astype(BF)


def ffn_backward(g2, slope, n1, inv, low, mixed, ffw_m, ffw_o, att_m, att_o, vectors, pick):
    width = low.shape[1]
    units = ffw_m.shape[2]
    cols = att_m.shape[2]
    shape = jax.ShapeDtypeStruct
    return pl.pallas_call(
        backward_kernel,
        out_shape=[
            shape((width, units), BF),
            shape((width, units), BF),
            shape((1, units), F32),
            shape((1, units), F32),
            shape((SEQ, width), F32),
            shape((width, cols), BF),
            shape((width, cols), BF),
            shape((SEQ, width), BF),
            shape((SEQ, LANES), BF),
            shape((8, width), F32),
        ],
        in_specs=vmem(6) + [ANY] * 4 + vmem(2),
        out_specs=vmem(10),
        scratch_shapes=[
            pltpu.VMEM((width, 2 * units), BF),
            pltpu.VMEM((width, 2 * units), BF),
            pltpu.VMEM((width, 2 * cols), BF),
            pltpu.VMEM((SEQ, 2 * units), BF),
            pltpu.VMEM((SEQ, width), BF),
            pltpu.VMEM((width, SEQ), BF),
            pltpu.SemaphoreType.DMA((6,)),
        ],
        compiler_params=params(),
        cost_estimate=cost(17e9, 40e6),
        name="ffn_backward",
    )(g2, slope, n1, inv, low, mixed, ffw_m, ffw_o, att_m, att_o, vectors, pick)


def heads_kernel(
    first_head,
    win_ref, q_ref, k_ref, v_ref, gm_ref, augl_ref, augd_ref, augk_ref, x_ref,
    dq_ref, dk_ref, dv_ref, wq_ref, wk_ref, wv_ref, bias_ref,
    kt_s, dqt_s, dk_s, dv_s, xt_s,
):
    cols = q_ref.shape[1]
    kt_s[...] = k_ref[...].T
    xt_s[...] = x_ref[...].T
    dk_s[...] = jnp.zeros_like(dk_s)
    dv_s[...] = jnp.zeros_like(dv_s)

    def block(i, carry):
        rows = ds(i * QB, QB, QB)
        begin = win_ref[0, i]
        kind = win_ref[1, i]

        def heads(width):
            span = ds(begin, width, LANES)

            def pair(p, c):
                tile = ds(p * LANES, LANES, LANES)
                query = q_ref[rows, tile]
                out_grad = gm_ref[rows, tile]
                query_right = jnp.concatenate([query, augl_ref[rows, :]], axis=1)
                grad_right = jnp.concatenate([out_grad, augd_ref[rows, :]], axis=1)
                key = k_ref[span, tile]
                value = v_ref[span, tile]
                aug = augk_ref[span, :]
                lane = lane_row()
                probs_all, grads_all, query_all, out_all = [], [], [], []
                for a, mask in enumerate(half_masks()):
                    head = first_head + 2 * p + a
                    spot = (lane == head + 16) | (lane == head + 32)
                    ones = jnp.where(spot, 1.0, 0.0).astype(BF)
                    more = jnp.where(lane == head + 48, 1.0, 0.0).astype(BF)
                    probs = jnp.exp2(
                        nt(jnp.concatenate([key * mask, aug + (ones + more)], axis=1), query_right)
                    )
                    grads = nt(
                        jnp.concatenate(
                            [value * mask, jnp.broadcast_to(ones, (width, LANES))], axis=1
                        ),
                        grad_right,
                    )
                    grads = (probs * grads).astype(BF)
                    probs_all.append(probs.astype(BF))
                    grads_all.append(grads)
                    query_all.append(query * mask)
                    out_all.append(out_grad * mask)
                    part = ds(p * LANES + a * HD, HD, HD)
                    dqt_s[part, rows] = nn(kt_s[part, span], grads)
                dv_s[span, tile] += nn(
                    jnp.concatenate(probs_all, axis=1), jnp.concatenate(out_all, axis=0)
                )
                dk_s[span, tile] += nn(
                    jnp.concatenate(grads_all, axis=1), jnp.concatenate(query_all, axis=0)
                )
                return c

            lax.fori_loop(0, cols // LANES, pair, 0)

        for index, width in enumerate(WINDOWS):
            pl.when(kind == index)(functools.partial(heads, width))
        return carry

    lax.fori_loop(0, SEQ // QB, block, 0)
    query_grad = (dqt_s[...] * HD ** (-0.5)).T.astype(BF)
    key_grad = (dk_s[...] * LN2).astype(BF)
    value_grad = dv_s[...].astype(BF)
    dq_ref[...] = query_grad
    dk_ref[...] = key_grad
    dv_ref[...] = value_grad
    bias_ref[...] = jnp.zeros_like(bias_ref)
    bias_ref[0:1, :] = col_sum(query_grad.astype(F32))
    bias_ref[1:2, :] = col_sum(value_grad.astype(F32))
    wq_ref[...] = nn(xt_s[...], dq_ref[...]).astype(BF)
    wk_ref[...] = nn(xt_s[...], dk_ref[...]).astype(BF)
    wv_ref[...] = nn(xt_s[...], dv_ref[...]).astype(BF)


def heads_backward(side, cols, win, q, k, v, gm, augl, augd, augk, x):
    width = x.shape[1]
    shape = jax.ShapeDtypeStruct
    part = pl.BlockSpec((SEQ, cols), lambda i: (0, side))
    thin = pl.BlockSpec((SEQ, LANES), lambda i: (0, 0))
    row = pl.BlockSpec((SEQ, cols), lambda i: (0, 0))
    grad = pl.BlockSpec((width, cols), lambda i: (0, 0))
    return pl.pallas_call(
        functools.partial(heads_kernel, side * (cols // HD)),
        grid=(1,),
        out_shape=[shape((SEQ, cols), BF)] * 3
        + [shape((width, cols), BF)] * 3
        + [shape((8, cols), F32)],
        in_specs=[SMEM]
        + [part] * 4
        + [thin] * 3
        + [pl.BlockSpec((SEQ, width), lambda i: (0, 0))],
        out_specs=[row] * 3 + [grad] * 3 + [pl.BlockSpec((8, cols), lambda i: (0, 0))],
        scratch_shapes=[
            pltpu.VMEM((cols, SEQ), BF),
            pltpu.VMEM((cols, SEQ), F32),
            pltpu.VMEM((SEQ, cols), F32),
            pltpu.VMEM((SEQ, cols), F32),
            pltpu.VMEM((width, SEQ), BF),
        ],
        compiler_params=params(),
        cost_estimate=cost(12e9, 15e6, 5e6),
        name="heads_backward",
    )(win, q, k, v, gm, augl, augd, augk, x)


def input_kernel(
    qm_ref, km_ref, vm_ref, qo_ref, ko_ref, vo_ref, g1_ref, wm_ref, wo_ref, out_ref, w_s, sem
):
    cols = wm_ref.shape[2]
    copies = []
    for j in range(3):
        for side, ref in enumerate((wm_ref, wo_ref)):
            at = (2 * j + side) * cols
            copies.append(
                pltpu.make_async_copy(
                    ref.at[j], w_s.at[:, at : at + cols], sem.at[2 * j + side]
                )
            )
    for copy in copies:
        copy.start()
    for copy in copies:
        copy.wait()

    def rows_step(r, carry):
        rows = ds(r * QB, QB, QB)
        left = jnp.concatenate(
            [ref[rows, :] for ref in (qm_ref, qo_ref, km_ref, ko_ref, vm_ref, vo_ref)], axis=1
        )
        out_ref[rows, :] = (nt(left, w_s[...]) + g1_ref[rows, :]).astype(BF)
        return carry

    lax.fori_loop(0, SEQ // QB, rows_step, 0)


def input_gradient(mine, other, g1, att_m, att_o):
    width = g1.shape[1]
    return pl.pallas_call(
        input_kernel,
        out_shape=jax.ShapeDtypeStruct((SEQ, width), BF),
        in_specs=vmem(7) + [ANY, ANY],
        out_specs=pl.BlockSpec(memory_space=pltpu.VMEM),
        scratch_shapes=[
            pltpu.VMEM((width, 3 * width), BF),
            pltpu.SemaphoreType.DMA((6,)),
        ],
        compiler_params=params(),
        cost_estimate=cost(3.6e9, 15e6),
        name="input_gradient",
    )(*mine, *other, g1, att_m, att_o)


def fold_kernel(axes, last, place_ref, *refs):
    count = len(axes)
    keeps, arrived = refs[:count], refs[count : 2 * count]
    outs = refs[2 * count :]
    for n, axis in enumerate(axes):
        if last:
            total = keeps[n][...].astype(F32) + arrived[n][...].astype(F32)
            outs[n][...] = total
            square = jnp.sum(total * total, axis=0, keepdims=True)
            outs[count + n][...] = square
            continue
        dim, bit = axis
        mine = place_ref[bit]
        lead = (slice(None),) * dim
        for out, at in ((outs[n], mine), (outs[count + n], 1 - mine)):
            index = lead + (at,)
            out[...] = (keeps[n][index].astype(F32) + arrived[n][index].astype(F32)).astype(BF)


def fold(place, axes, last, keeps, arrived):
    shape = jax.ShapeDtypeStruct
    if last:
        out = [shape(k.shape, F32) for k in keeps]
        out += [shape((1, k.shape[-1]), F32) for k in keeps]
    else:
        out = [
            shape(k.shape[: axis[0]] + k.shape[axis[0] + 1 :], BF) for k, axis in zip(keeps, axes)
        ] * 2
    size = sum(k.size for k in keeps)
    res = pl.pallas_call(
        functools.partial(fold_kernel, axes, last),
        out_shape=out,
        in_specs=[SMEM] + vmem(2 * len(keeps)),
        out_specs=vmem(len(out)),
        compiler_params=params(),
        cost_estimate=cost(2 * size, 6 * size),
        name="fold",
    )(place, *keeps, *arrived)
    return res[: len(keeps)], res[len(keeps) :]


def swap_cores(value):
    return lax.ppermute(value, "tensor", [(0, 1), (1, 0)])


def swap_bit(value, bit, count):
    return lax.ppermute(value, "dp", [(i, i ^ (1 << bit)) for i in range(count)])


def reduce_parts(place, mine, other, count):
    bits = count.bit_length() - 1
    rows = mine[0].shape[0] // count
    orders = []
    for n in range(len(mine)):
        turn = min(bits, 3)
        orders.append([(n + s) % turn for s in range(turn)] + list(range(turn, bits)))
    left = [list(range(bits - 1, -1, -1)) for _ in mine]
    keeps = [m.reshape((2,) * bits + (rows, m.shape[1])) for m in mine]
    arrived = [swap_cores(o).reshape(k.shape) for o, k in zip(other, keeps)]
    for step in range(bits):
        axes = []
        for n in range(len(mine)):
            bit = orders[n][step]
            axes.append((left[n].index(bit), bit))
            left[n].remove(bit)
        keeps, sends = fold(place, axes, False, keeps, arrived)
        arrived = [swap_bit(s, axis[1], count) for s, axis in zip(sends, axes)]
    totals, squares = fold(place, [None] * len(mine), True, keeps, arrived)
    return totals, squares


def adam_step(grad, first, second, weight, factor, rate, decay):
    clipped = grad * factor
    first_new = 0.9 * first + 0.1 * clipped
    second_new = 0.999 * second + 0.001 * clipped * clipped
    mean_hat = first_new / (1.0 - 0.9**STEP)
    var_hat = second_new / (1.0 - 0.999**STEP)
    weight_new = weight - rate * (mean_hat / (jnp.sqrt(var_hat) + 1e-08) + decay * weight)
    return (first_new, second_new, weight_new)


def windows(seg, valid):
    blocks = SEQ // QB
    begin = seg[::QB]
    end = seg[QB - 1 :: QB]
    start = jnp.sum((seg[None, :] < begin[:, None]).astype(jnp.int32), axis=1)
    real = jnp.sum(valid)
    stop = jnp.minimum(jnp.sum((seg[None, :] <= end[:, None]).astype(jnp.int32), axis=1), real)
    start = (start // LANES) * LANES
    need = stop - start
    kind = jnp.zeros((blocks,), jnp.int32)
    for width in WINDOWS[:-1]:
        kind = kind + (need > width).astype(jnp.int32)
    sizes = jnp.array(WINDOWS, jnp.int32)
    size = jnp.sum(jnp.where(kind[:, None] == jnp.arange(len(WINDOWS))[None, :], sizes, 0), axis=1)
    return jnp.stack([jnp.minimum(start, SEQ - size), kind])


def mask_columns(seg, valid):
    lane = lax.broadcasted_iota(jnp.int32, (SEQ, LANES), 1)
    same = lane == seg[:, None]
    augk = jnp.where(lane == 10, (1 - valid)[:, None], same.astype(jnp.int32)).astype(BF)
    augq = jnp.where((lane < 10) & ~same | (lane == 10), -BIG, 0.0).astype(BF)
    return augq, augk


def local(
    frames,
    cotangent,
    segment_ids,
    pad_mask,
    attention_weight,
    feedforward_weight,
    head_bias,
    hidden_bias,
    norm_vectors,
    attention_first,
    attention_second,
    feedforward_first,
    feedforward_second,
    head_first,
    head_second,
    hidden_first,
    hidden_second,
    vector_first,
    vector_second,
):
    width = frames.shape[1]
    cols = attention_weight.shape[2]
    units = feedforward_weight.shape[2]
    count = lax.axis_size("dp")
    core = lax.axis_index("tensor")
    dp_index = lax.axis_index("dp")
    bits = count.bit_length() - 1
    place = jnp.stack([(dp_index >> b) & 1 for b in range(bits)]).astype(jnp.int32)

    att_o = swap_cores(attention_weight)
    head_m = head_bias.reshape(2, cols)
    head_o = swap_cores(head_m)
    hidden_o = swap_cores(hidden_bias)
    ffw_o = swap_cores(feedforward_weight)

    x = lax.dynamic_slice_in_dim(frames, core * SEQ, SEQ, 0)
    cot = lax.dynamic_slice_in_dim(cotangent, core * SEQ, SEQ, 0)
    seg = lax.dynamic_slice_in_dim(segment_ids, core * SEQ, SEQ, 0)
    valid = lax.dynamic_slice_in_dim(pad_mask, core * SEQ, SEQ, 0)
    win = windows(seg, valid)
    augq, augk = mask_columns(seg, valid)
    heads = 2 * cols // HD
    head_of = lax.broadcasted_iota(jnp.int32, (width, LANES), 0) // HD
    lane = lax.broadcasted_iota(jnp.int32, (width, LANES), 1)
    pick = ((lane == head_of + 16) | (lane == head_of + 32)).astype(BF)

    q, k, v, augl, mixed, n1, inv, low = attention_forward(
        win, x, attention_weight, att_o, head_m, head_o, augq, augk, norm_vectors
    )
    out_row, g2, slope, down_m, down_o, sums_two = ffn_forward(
        low, n1, feedforward_weight, ffw_o, hidden_bias, hidden_o, cot, augk, norm_vectors
    )

    def thirds(value):
        size = value.shape[1] // 3
        return [value[:, n * size : (n + 1) * size] for n in range(3)]

    down, down_sq = reduce_parts(place, thirds(down_m), thirds(down_o), count)
    up_m, up_o, hid_m, hid_o, g1, om, oo, gm, augd, sums_one = ffn_backward(
        g2, slope, n1, inv, low, mixed, feedforward_weight, ffw_o, attention_weight, att_o,
        norm_vectors, pick,
    )
    up, up_sq = reduce_parts(place, thirds(up_m), thirds(up_o), count)
    outp, outp_sq = reduce_parts(place, thirds(om), thirds(oo), count)
    back = functools.partial(heads_backward, cols=cols, win=win, q=q, k=k, v=v, gm=gm, augl=augl,
                             augd=augd, augk=augk, x=x)
    other = back(1)
    mine = back(0)
    qkv, qkv_sq = reduce_parts(place, mine[3:6], other[3:6], count)
    grad_row = input_gradient(mine[:3], other[:3], g1, attention_weight, att_o)

    side_sums = jnp.concatenate(
        [hid_m.reshape(-1), mine[6][:2].reshape(-1)]
    ) + swap_cores(jnp.concatenate([hid_o.reshape(-1), other[6][:2].reshape(-1)]))
    vector_sums = jnp.concatenate([sums_one[0:3], sums_two[3:6]], axis=0)
    vector_sums = vector_sums + swap_cores(vector_sums)
    small = jnp.concatenate([side_sums, vector_sums.reshape(-1)])
    for bit in range(bits):
        small = small + swap_bit(small, bit, count)
    hidden_sum = small[:units]
    head_sum = small[units : units + 2 * cols]
    vector_sum = small[units + 2 * cols :]

    squares = sum(jnp.sum(s) for s in down_sq + up_sq + outp_sq + qkv_sq)
    squares = squares + (jnp.sum(hidden_sum * hidden_sum) + jnp.sum(head_sum * head_sum)) / count
    squares = squares + jnp.sum(vector_sum * vector_sum) / (2 * count)
    squares = squares + swap_cores(squares)
    for bit in range(bits):
        squares = squares + swap_bit(squares, bit, count)
    gradient_norm = jnp.sqrt(squares)
    factor = jnp.minimum(1.0, 1.0 / (gradient_norm + 1e-06))

    attention_shard = jnp.stack(list(qkv) + [jnp.concatenate(outp, axis=1)])
    feedforward_shard = jnp.stack([jnp.concatenate(up, axis=1), jnp.concatenate(down, axis=1)])
    rows_owned = attention_shard.shape[1]
    old_attention = lax.dynamic_slice_in_dim(
        attention_weight, dp_index * rows_owned, rows_owned, 1
    ).astype(F32)
    old_feedforward = lax.dynamic_slice_in_dim(
        feedforward_weight, dp_index * rows_owned, rows_owned, 1
    ).astype(F32)
    head_owned = cols // count
    hidden_owned = units // count

    def own(value, size, axis):
        return lax.dynamic_slice_in_dim(value, dp_index * size, size, axis)

    att = adam_step(
        attention_shard, attention_first, attention_second, old_attention, factor, 0.05, 0.01
    )
    ffw = adam_step(
        feedforward_shard, feedforward_first, feedforward_second, old_feedforward, factor, 0.05,
        0.01,
    )
    hed = adam_step(
        own(head_sum.reshape(2, 1, cols), head_owned, 2), head_first, head_second,
        own(head_bias, head_owned, 2), factor, 0.5, 0.0,
    )
    hid = adam_step(
        own(hidden_sum.reshape(1, units), hidden_owned, 1), hidden_first, hidden_second,
        own(hidden_bias, hidden_owned, 1), factor, 0.5, 0.0,
    )
    vec = adam_step(
        own(vector_sum.reshape(6, width), rows_owned, 1), vector_first, vector_second,
        own(norm_vectors, rows_owned, 1), factor, 0.5, 0.0,
    )

    def both_rows(row):
        partner = swap_cores(row)
        lower = jnp.where(core == 0, row, partner)
        upper = jnp.where(core == 0, partner, row)
        return jnp.concatenate([lower, upper], axis=0)

    return (
        both_rows(out_row),
        both_rows(grad_row).astype(F32),
        gradient_norm,
        *att,
        *ffw,
        *hed,
        *hid,
        *vec,
    )


def solution(mesh):
    weight_spec = P(None, None, "tensor")
    shard = P(None, "dp", "tensor")
    head = P(None, "tensor", "dp")
    hidden = P("tensor", "dp")
    vector = P(None, "dp")
    row = P("dp", None)
    return jax.shard_map(
        local,
        mesh=mesh,
        in_specs=(
            row, row, P("dp"), P("dp"),
            weight_spec, weight_spec,
            P(None, "tensor", None), P("tensor", None), P(),
            shard, shard, shard, shard,
            head, head, hidden, hidden, vector, vector,
        ),
        out_specs=(
            row, row, P(),
            shard, shard, shard, shard, shard, shard,
            head, head, head, hidden, hidden, hidden, vector, vector, vector,
        ),
        check_vma=False,
    )
```

```python
import functools

import jax
import jax.numpy as jnp
from jax import lax
from jax.experimental import pallas as pl
from jax.experimental.pallas import tpu as pltpu
from jax.sharding import PartitionSpec as P

HD = 64
SEQ = 1024
STEP = 10
LANES = 128
QB = 256
BLOCKS = SEQ // QB
BIG = 1e30
LOG2E = 1.4426950408889634
LN2 = 0.6931471805599453
WINDOWS = (512, 640, 768, 1024)
BF = jnp.bfloat16
F32 = jnp.float32
I32 = jnp.int32


def nn(a, b):
    return jnp.dot(a, b, preferred_element_type=F32)


def nt(a, b):
    return lax.dot_general(a, b, (((1,), (1,)), ((), ())), preferred_element_type=F32)


def ds(start, size, step):
    return pl.ds(pl.multiple_of(start, step), size)


def shape(dims, dtype):
    return jax.ShapeDtypeStruct(dims, dtype)


def cost(flops, bytes_accessed, transcendentals=0):
    return pl.CostEstimate(
        flops=int(flops), bytes_accessed=int(bytes_accessed), transcendentals=int(transcendentals)
    )


SMEM = "smem"
HBM = "hbm"
OUT = "out"
SPACES = {SMEM: pltpu.SMEM, HBM: pltpu.HBM, OUT: pltpu.VMEM}
WHOLE = 63


def call(kernel, name, ins, outs, scratch, copies, estimate, mib=WHOLE):
    args = [
        pltpu.with_memory_space_constraint(array, pltpu.HBM) if space == HBM else array
        for space, array in ins
    ]
    return pl.pallas_call(
        kernel,
        out_shape=[
            pltpu.HBM(dims, dtype) if space == HBM else shape(dims, dtype)
            for space, dims, dtype in outs
        ],
        in_specs=[pl.BlockSpec(memory_space=SPACES[space]) for space, _ in ins],
        out_specs=[pl.BlockSpec(memory_space=SPACES[space]) for space, _, _ in outs],
        scratch_shapes=[pltpu.VMEM(dims, dtype) for dims, dtype in scratch]
        + [pltpu.SemaphoreType.DMA((max(copies, 1),))],
        compiler_params=pltpu.CompilerParams(vmem_limit_bytes=mib * 2**20),
        cost_estimate=estimate,
        name=name,
    )(*args)


class Copies:
    def __init__(self, sem):
        self.sem = sem
        self.used = 0
        self.pending = {}

    def start(self, name, *pairs):
        made = []
        for source, target in pairs:
            made.append(pltpu.make_async_copy(source, target, self.sem.at[self.used]))
            made[-1].start()
            self.used += 1
        self.pending[name] = made

    def wait(self, *names):
        for name in names:
            for copy in self.pending.pop(name):
                copy.wait()

    def finish(self):
        self.wait(*list(self.pending))


def lane_row():
    return lax.broadcasted_iota(I32, (1, LANES), 1)


def half_masks():
    low = jnp.where(lane_row() < HD, 1.0, 0.0)
    return (low.astype(BF), (1.0 - low).astype(BF))


def norm_rows(value):
    center = value - jnp.mean(value, axis=-1, keepdims=True)
    inv_std = lax.rsqrt(jnp.mean(center * center, axis=-1, keepdims=True) + 1e-05)
    return center * inv_std, inv_std


def norm_back(grad, normed, inv_std, gain):
    scaled = grad * gain
    mean_one = jnp.mean(scaled, axis=-1, keepdims=True)
    mean_two = jnp.mean(scaled * normed, axis=-1, keepdims=True)
    return inv_std * (scaled - mean_one - normed * mean_two)


def col_sum(value):
    return jnp.sum(value, axis=0, keepdims=True)


def sides(refs, target, index=None):
    size = target.shape[-1] // len(refs)
    picked = [ref if index is None else ref.at[index] for ref in refs]
    return [
        (ref, target.at[:, n * size : (n + 1) * size]) for n, ref in enumerate(picked)
    ]


def staged(count, *stages):
    for step in range(count + len(stages) - 1):
        for n, stage in enumerate(stages):
            if 0 <= step - n < count:
                stage(step - n)


def window_of(seg, real, i):
    begin = jnp.min(seg[2 * i : 2 * i + 1, :])
    end = jnp.max(seg[2 * i + 1 : 2 * i + 2, :])
    start = jnp.sum(jnp.where(seg < begin, 1, 0))
    stop = jnp.minimum(jnp.sum(jnp.where(seg <= end, 1, 0)), real)
    start = (start // LANES) * LANES
    need = stop - start
    kind = jnp.int32(0)
    size = jnp.int32(WINDOWS[0])
    for index, width in enumerate(WINDOWS[:-1]):
        kind = jnp.where(need > width, index + 1, kind)
        size = jnp.where(need > width, WINDOWS[index + 1], size)
    return jnp.minimum(start, SEQ - size), kind


def attention_kernel(
    core_ref, frames_ref, seg_ref, pad_ref, wm_ref, wo_ref, bm_ref, bo_ref,
    q_ref, k_ref, v_ref, augq_out, augk_out, mixed_ref, win_ref,
    x_s, w_s, q_s, k_s, v_s, vt_s, mt_s, lse_s, score_s, prob_s, mixed_s, augq_ref, augk_ref,
    small_s, seg_s, pad_s, sem,
):
    moves = Copies(sem)
    core = core_ref[0]
    lines = ds(core * (SEQ // LANES), SEQ // LANES, SEQ // LANES)
    moves.start("seg", (seg_ref.at[lines, :], seg_s), (pad_ref.at[lines, :], pad_s))
    moves.start("x", (frames_ref.at[ds(core * SEQ, SEQ, SEQ), :], x_s))
    moves.start("bias", *sides((bm_ref, bo_ref), small_s))
    moves.start(0, *sides((wm_ref, wo_ref), w_s.at[0], 0))
    lane = lane_row()
    moves.wait("seg")
    seg = seg_s[...]
    pad = pad_s[...]
    real = jnp.sum(pad)
    for i in range(BLOCKS):
        begin, kind = window_of(seg, real, i)
        win_ref[0, i] = begin
        win_ref[1, i] = kind
    for b in range(SEQ // LANES):
        rows = slice(b * LANES, (b + 1) * LANES)
        ids = jnp.broadcast_to(seg[b : b + 1, :].astype(F32), (LANES, LANES)).T
        shown = jnp.broadcast_to(pad[b : b + 1, :].astype(F32), (LANES, LANES)).T
        same = lane.astype(F32) == ids
        augk_ref[rows, :] = jnp.where(
            lane == 10, 1.0 - shown, jnp.where(same, 1.0, 0.0)
        ).astype(BF)
        off = jnp.where(same, 0.0, -BIG)
        augq_ref[rows, :] = jnp.where(
            lane < 10, off, jnp.where(lane == 10, -BIG, 0.0)
        ).astype(BF)
    moves.start("augk", (augk_ref, augk_out))
    moves.wait("bias", "x", 0)
    for j in (1, 2):
        moves.start(j, *sides((wm_ref, wo_ref), w_s.at[j], j))
    bias = [small_s[j : j + 1, :] for j in range(2)]
    q_s[...] = ((nn(x_s[...], w_s[0]) + bias[0]) * (HD ** (-0.5) * LOG2E)).astype(BF)
    moves.start("q", (q_s, q_ref))
    moves.wait(1)
    k_s[...] = nn(x_s[...], w_s[1]).astype(BF)
    moves.start("k", (k_s, k_ref))
    moves.wait(2)
    v_s[...] = (nn(x_s[...], w_s[2]) + bias[1]).astype(BF)
    moves.start("v", (v_s, v_ref))
    vt_s[...] = v_s[...].T
    lse_s[...] = jnp.zeros_like(lse_s)
    heads = q_s.shape[1] // HD
    masks = half_masks()

    def block(i, carry):
        rows = ds(i * QB, QB, QB)
        begin = win_ref[0, i]
        kind = win_ref[1, i]

        def run(width):
            span = ds(begin, width, LANES)
            ones = jnp.ones((16, width), BF)

            def score(h):
                tile = slice(h // 2 * LANES, (h // 2 + 1) * LANES)
                right = jnp.concatenate([q_s[rows, tile], augq_ref[rows, :]], axis=1)
                left = jnp.concatenate([k_s[span, tile] * masks[h % 2], augk_ref[span, :]], axis=1)
                score_s[h % 2, :width] = nt(left, right)

            def soften(h):
                top = jnp.max(score_s[h % 2, :width], axis=0, keepdims=True)
                prob_s[h % 2, :width] = jnp.exp2(score_s[h % 2, :width] - top).astype(BF)
                return top

            def mix(h, top):
                part = slice(h * HD, (h + 1) * HD)
                out = nn(jnp.concatenate([vt_s[part, span], ones], axis=0), prob_s[h % 2, :width])
                total = out[HD : HD + 1, :]
                mt_s[part, rows] = (out[:HD, :] * (1.0 / total)).astype(BF)
                lse = top + jnp.log2(total)
                for piece in range(3):
                    lse_s[16 * (piece + 1) + h : 16 * (piece + 1) + h + 1, rows] = lse

            tops = {}
            for step in range(heads + 2):
                if step < heads:
                    score(step)
                if step >= 2:
                    mix(step - 2, tops.pop(step - 2))
                if 1 <= step <= heads:
                    tops[step - 1] = soften(step - 1)

        for index, width in enumerate(WINDOWS):
            pl.when(kind == index)(functools.partial(run, width))
        mixed_s[rows, :] = mt_s[:, rows].T
        return carry

    lax.fori_loop(0, BLOCKS, block, 0)
    moves.start("mixed", (mixed_s, mixed_ref))
    lse = lse_s[...].T
    high = lse.astype(BF).astype(F32)
    mid = (lse - high).astype(BF).astype(F32)
    piece = jnp.where(lane < 32, high, jnp.where(lane < 48, mid, lse - high - mid))
    augq_ref[...] = (augq_ref[...].astype(F32) - piece).astype(BF)
    moves.start("augq", (augq_ref, augq_out))
    moves.finish()


def attention_forward(core, frames, seg, pad, att_m, att_o, bias_m, bias_o):
    width = frames.shape[1]
    wide = ((SEQ, width), BF)
    thin = ((SEQ, LANES), BF)
    line = ((SEQ // LANES, LANES), I32)
    return call(
        attention_kernel,
        "attention_forward",
        [(SMEM, core)]
        + [(HBM, a) for a in (frames, seg, pad, att_m, att_o, bias_m, bias_o)],
        [(HBM, *wide)] * 3 + [(HBM, *thin)] * 2 + [(HBM, *wide), (SMEM, (2, BLOCKS), I32)],
        [
            wide, ((3, width, width), BF), wide, wide, wide, ((width, SEQ), BF),
            ((width, SEQ), BF), ((LANES, SEQ), F32), ((2, SEQ, QB), F32), ((2, SEQ, QB), BF),
            wide, thin, thin, ((2, width), F32), line, line,
        ],
        17,
        cost(15e9, 20e6, 10e6),
    )


def gelu_pair(value):
    phi = 0.5 + 0.5 * lax.erf(value * 0.7071067811865476)
    low = value.astype(BF)
    density = jnp.exp2(low * low * BF(-0.5 * LOG2E)) * BF(0.3989422804014327)
    return (value * phi).astype(BF), phi.astype(BF) + low * density


def chunk_of(c, size):
    each = size // QB
    return c // each, ds(c % each * QB, QB, QB)


def forward_kernel(
    core_ref, frames_ref, cot_ref, mixed_ref, am_ref, ao_ref, fm_ref, fo_ref, hm_ref, ho_ref,
    augk_out, vec_out,
    n1_ref, inv_out, low_ref, out_ref, g2_ref, glow_ref, slope_ref, dm_ref, do_ref, sum_ref,
    x_s, mixed_s, wo_s, w1_s, w2_s, cot_s, n1_s, inv_ref, low_s, g2_s, glow_s, slope_s, act_s,
    glt_s, stage_s, unit_s, ffn_s, bias_s, augk_ref, vec_ref, sem,
):
    units = fm_ref.shape[2]
    moves = Copies(sem)
    own = ds(core_ref[0] * SEQ, SEQ, SEQ)
    moves.start("wo", *sides((am_ref, ao_ref), wo_s, 3))
    moves.start("in", (vec_out, vec_ref), (mixed_ref, mixed_s), (frames_ref.at[own, :], x_s))
    moves.start("bias", *sides((hm_ref, ho_ref), bias_s))
    moves.wait("wo", "in")
    moves.start("w1", *sides((fm_ref, fo_ref), w1_s, 0))
    sum_ref[...] = jnp.zeros_like(sum_ref)

    def project(r):
        rows = slice(r * QB, (r + 1) * QB)
        ffn_s[r % 2] = nt(mixed_s[rows, :], wo_s[...])

    def first_rows(r):
        rows = slice(r * QB, (r + 1) * QB)
        first = x_s[rows, :].astype(F32) + ffn_s[r % 2] + vec_ref[0:1, :]
        normed, inv_std = norm_rows(first)
        n1_s[rows, :] = normed
        inv_ref[rows, :] = jnp.broadcast_to(inv_std, (QB, LANES))
        low_s[rows, :] = (normed * vec_ref[1:2, :] + vec_ref[2:3, :]).astype(BF)

    staged(BLOCKS, project, first_rows)
    moves.wait("bias", "w1")
    moves.start("first", (n1_s, n1_ref), (inv_ref, inv_out), (low_s, low_ref))
    moves.start("cot", (cot_ref.at[own, :], cot_s), (augk_out, augk_ref))
    moves.start("w2", *sides((fm_ref, fo_ref), w2_s, 1))
    each = units // QB

    def up(c):
        unit_s[c % 2] = nn(low_s[...], w1_s[:, c * QB : (c + 1) * QB])

    def bend(c):
        spot = slice(c * QB, (c + 1) * QB)
        act, slope = gelu_pair(unit_s[c % 2] + bias_s[0:1, spot])
        act_s[:, c * QB : (c + 1) * QB] = act
        slope_s[:, c * QB : (c + 1) * QB] = slope

    staged(2 * each, up, bend)
    moves.start("slope", (slope_s, slope_ref))
    moves.wait("cot", "w2")

    def contract(r):
        rows = slice(r * QB, (r + 1) * QB)
        ffn_s[r % 2] = nt(act_s[rows, :], w2_s[...])

    def second(r):
        rows = slice(r * QB, (r + 1) * QB)
        first_norm = n1_s[rows, :] * vec_ref[1:2, :] + vec_ref[2:3, :]
        n2, inv_std = norm_rows(first_norm + ffn_s[r % 2] + vec_ref[3:4, :])
        valid = 1.0 - augk_ref[rows, 10:11].astype(F32)
        grad = cot_s[rows, :].astype(F32) * valid
        cot_s[rows, :] = (n2 * vec_ref[4:5, :] + vec_ref[5:6, :]).astype(BF)
        back = norm_back(grad, n2, inv_std, vec_ref[4:5, :])
        g2_s[rows, :] = back
        glow_s[rows, :] = back.astype(BF)
        sum_ref[3:4, :] += col_sum(back)
        sum_ref[4:5, :] += col_sum(grad * n2)
        sum_ref[5:6, :] += col_sum(grad)

    staged(BLOCKS, contract, second)
    moves.start("second", (cot_s, out_ref), (g2_s, g2_ref), (glow_s, glow_ref))
    glt_s[...] = glow_s[...].T
    size = stage_s.shape[2]
    spots = [(side, part) for side in (1, 0) for part in range(3)]
    for n, (side, part) in enumerate(spots):
        if n >= 2:
            moves.wait(n - 2)
        for c in range(size // QB):
            at = side * units + part * size + c * QB
            grad = nn(glt_s[...], act_s[:, at : at + QB])
            stage_s[n % 2, :, c * QB : (c + 1) * QB] = grad.astype(BF)
        moves.start(n, (stage_s.at[n % 2], (dm_ref, do_ref)[side].at[part]))
    moves.finish()


def ffn_forward(
    core, frames, cot, mixed, att_m, att_o, ffw_m, ffw_o, hid_m, hid_o, augk, vectors
):
    width = frames.shape[1]
    units = ffw_m.shape[2]
    wide = ((SEQ, width), BF)
    full = ((SEQ, width), F32)
    thin = ((SEQ, LANES), F32)
    inner = ((width, 2 * units), BF)
    outer = ((SEQ, 2 * units), BF)
    grads = ((3, width, units // 3), BF)
    ins = (frames, cot, mixed, att_m, att_o, ffw_m, ffw_o, hid_m, hid_o, augk, vectors)
    return call(
        forward_kernel,
        "ffn_forward",
        [(SMEM, core)] + [(HBM, a) for a in ins],
        [(HBM, *out) for out in (full, thin, wide, wide, full, wide, outer, grads, grads)]
        + [(OUT, (8, width), F32)],
        [
            wide, wide, ((width, width), BF), inner, inner, wide, full, thin, wide, full, wide,
            outer, outer, ((width, SEQ), BF), ((2, width, units // 3), BF), ((2, SEQ, QB), F32),
            ((2, QB, width), F32), ((1, 2 * units), F32), ((SEQ, LANES), BF),
            (vectors.shape, F32),
        ],
        26,
        cost(15.7e9, 40e6, 6e6),
    )


def hidden_kernel(
    glow_ref, slope_ref, low_ref, fm_ref, fo_ref,
    gup_ref, um_ref, uo_ref, hm_ref, ho_ref,
    glow_s, slope_s, low_s, w2_s, lowt_s, um_s, uo_s, unit_s, sem,
):
    units = fm_ref.shape[2]
    half = [slice(side * units, (side + 1) * units) for side in range(2)]
    moves = Copies(sem)

    def weight(side):
        return (fm_ref, fo_ref)[side].at[1], w2_s.at[:, half[side]]

    def slope(side):
        return slope_ref.at[:, half[side]], slope_s.at[:, half[side]]

    moves.start("first", (glow_ref, glow_s), weight(1))
    moves.wait("first")
    moves.start("low", (low_ref, low_s), slope(1))
    gup_s = slope_s
    each = units // QB
    targets = ((um_s, um_ref, hm_ref), (uo_s, uo_ref, ho_ref))
    order = [(side, c) for side in (1, 0) for c in range(each)]

    def place(n):
        side, c = order[n]
        at = side * units + c * QB
        return side, c, slice(at, at + QB), slice(c * QB, (c + 1) * QB)

    def pull(n):
        side, c, there, here = place(n)
        if n == each:
            moves.wait("rest")
        unit_s[n % 2] = nn(glow_s[...], w2_s[:, there])
        if n == 0:
            moves.wait("low")
            moves.start("rest", weight(0), slope(0))
            lowt_s[...] = low_s[...].T

    def bend(n):
        side, c, there, here = place(n)
        grad = (unit_s[n % 2] * slope_s[:, there].astype(F32)).astype(BF)
        gup_s[:, there] = grad
        targets[side][2][0:1, here] = col_sum(grad.astype(F32))

    def push(n):
        side, c, there, here = place(n)
        target, result, bias = targets[side]
        part, spot = divmod(c * QB, target.shape[2])
        target[part, :, spot : spot + QB] = nn(lowt_s[...], gup_s[:, there]).astype(BF)
        if c == each - 1:
            moves.start(
                side,
                (target, result),
                (gup_s.at[:, half[side]], gup_ref.at[:, half[side]]),
            )

    staged(2 * each, pull, bend, push)
    moves.finish()


def hidden_backward(glow, slope, low, ffw_m, ffw_o):
    width = low.shape[1]
    units = ffw_m.shape[2]
    wide = ((SEQ, width), BF)
    outer = ((SEQ, 2 * units), BF)
    grads = ((3, width, units // 3), BF)
    return call(
        hidden_kernel,
        "hidden_backward",
        [(HBM, a) for a in (glow, slope, low, ffw_m, ffw_o)],
        [
            (HBM, *outer), (HBM, *grads), (HBM, *grads),
            (OUT, (1, units), F32), (OUT, (1, units), F32),
        ],
        [
            wide, outer, wide, ((width, 2 * units), BF), ((width, SEQ), BF), grads, grads,
            ((2, SEQ, QB), F32),
        ],
        10,
        cost(9.7e9, 30e6),
    )


def norm_kernel(
    gup_ref, g2_ref, n1_ref, inv_out, mixed_ref, fm_ref, fo_ref, am_ref, ao_ref, vec_out,
    g1_ref, om_ref, oo_ref, gm_ref, augd_out, sum_ref,
    gup_s, g2_s, n1_s, inv_ref, mixed_s, w1_s, wo_s, vec_ref,
    glow_s, glt_s, gm_s, augd_ref, om_s, oo_s, gfn_s, sem,
):
    moves = Copies(sem)
    g1_s = g2_s
    moves.start("w1", *sides((fm_ref, fo_ref), w1_s, 0))

    def fetch(r):
        rows = slice(r * QB, (r + 1) * QB)
        moves.start(("gup", r), (gup_ref.at[rows, :], gup_s.at[rows, :]))
        moves.start(
            ("first", r),
            (g2_ref.at[rows, :], g2_s.at[rows, :]),
            (n1_ref.at[rows, :], n1_s.at[rows, :]),
        )

    moves.start("vec", (vec_out, vec_ref), (inv_out, inv_ref))
    fetch(0)
    sum_ref[...] = jnp.zeros_like(sum_ref)
    moves.wait("w1", "vec")
    fetch(1)

    def pull(r):
        rows = slice(r * QB, (r + 1) * QB)
        moves.wait(("gup", r))
        if 0 < r < BLOCKS - 1:
            fetch(r + 1)
        gfn_s[r % 2] = nt(gup_s[rows, :], w1_s[...])
        if r == BLOCKS - 1:
            moves.start("wo", *sides((am_ref, ao_ref), wo_s, 3))
            moves.start("mixed", (mixed_ref, mixed_s))

    def first_rows(r):
        rows = slice(r * QB, (r + 1) * QB)
        moves.wait(("first", r))
        grad = gfn_s[r % 2] + g2_s[rows, :]
        n1 = n1_s[rows, :]
        back = norm_back(grad, n1, inv_ref[rows, 0:1], vec_ref[1:2, :])
        g1_s[rows, :] = back
        glow_s[rows, :] = back.astype(BF)
        sum_ref[0:1, :] += col_sum(back)
        sum_ref[1:2, :] += col_sum(grad * n1)
        sum_ref[2:3, :] += col_sum(grad)

    staged(BLOCKS, pull, first_rows)
    moves.start("g1", (g1_s, g1_ref))
    moves.wait("wo", "mixed")
    lane = lane_row()
    width = wo_s.shape[0]
    head = lax.broadcasted_iota(I32, (width, LANES), 0) // HD
    spot = lax.broadcasted_iota(I32, (width, LANES), 1)
    pick = jnp.where((spot == head + 16) | (spot == head + 32), 1.0, 0.0).astype(BF)
    for r in range(BLOCKS):
        rows = slice(r * QB, (r + 1) * QB)
        gm = nn(glow_s[rows, :], wo_s[...]).astype(BF)
        gm_s[rows, :] = gm
        both = gm.astype(F32) * mixed_s[rows, :].astype(F32)
        high = both.astype(BF)
        dots = nn(high, pick) + nn((both - high.astype(F32)).astype(BF), pick)
        dot_high = dots.astype(BF).astype(F32)
        augd_ref[rows, :] = (-jnp.where(lane < 32, dot_high, dots - dot_high)).astype(BF)
    moves.start("gm", (gm_s, gm_ref), (augd_ref, augd_out))
    glt_s[...] = glow_s[...].T
    size = om_s.shape[2]
    for side, target, result in ((1, oo_s, oo_ref), (0, om_s, om_ref)):
        cols = slice(side * 3 * size, (side + 1) * 3 * size)
        product = nn(glt_s[...], mixed_s[:, cols]).astype(BF)
        for part in range(3):
            target[part] = product[:, part * size : (part + 1) * size]
        moves.start(("o", side), (target, result))
    moves.finish()


def norm_backward(gup, g2, n1, inv, mixed, ffw_m, ffw_o, att_m, att_o, vectors):
    width = n1.shape[1]
    units = ffw_m.shape[2]
    cols = att_m.shape[2]
    wide = ((SEQ, width), BF)
    full = ((SEQ, width), F32)
    thin = ((SEQ, LANES), BF)
    grads = ((3, width, cols // 3), BF)
    ins = (gup, g2, n1, inv, mixed, ffw_m, ffw_o, att_m, att_o, vectors)
    return call(
        norm_kernel,
        "norm_backward",
        [(HBM, a) for a in ins],
        [(HBM, *out) for out in (full, grads, grads, wide, thin)] + [(OUT, (8, width), F32)],
        [
            ((SEQ, 2 * units), BF), full, full, ((SEQ, LANES), F32), wide,
            ((width, 2 * units), BF), ((width, width), BF), (vectors.shape, F32),
            wide, ((width, SEQ), BF), wide, thin, grads, grads, ((2, QB, width), F32),
        ],
        27,
        cost(7.5e9, 30e6),
    )


def heads_kernel(
    side,
    win_ref, core_ref, q_ref, k_ref, v_ref, gm_ref, augq_out, augd_out, augk_out, frames_ref,
    dq_ref, dk_ref, dv_ref, grad_ref, bias_ref,
    q_s, k_s, v_s, gm_s, augq_ref, augd_ref, augk_ref, x_s,
    kt_s, dqt_s, dk_s, dv_s, xt_s, score_s, slope_s, prob_s, back_s, outs_s, grad_s, sem,
):
    cols = dk_s.shape[1]
    heads = cols // HD
    moves = Copies(sem)
    own = slice(side * cols, (side + 1) * cols)
    moves.start(
        "in",
        *[
            (ref.at[:, own], to)
            for ref, to in ((k_ref, k_s), (q_ref, q_s), (v_ref, v_s), (gm_ref, gm_s))
        ],
        (augq_out, augq_ref), (augd_out, augd_ref), (augk_out, augk_ref),
    )
    dk_s[...] = jnp.zeros_like(dk_s)
    dv_s[...] = jnp.zeros_like(dv_s)
    moves.wait("in")
    moves.start("x", (frames_ref.at[ds(core_ref[0] * SEQ, SEQ, SEQ), :], x_s))
    kt_s[...] = k_s[...].T
    masks = half_masks()
    lane = lane_row()

    def block(i, carry):
        rows = ds(i * QB, QB, QB)
        begin = win_ref[0, i]
        kind = win_ref[1, i]

        def run(width):
            span = ds(begin, width, LANES)

            def scores(h):
                tile = slice(h // 2 * LANES, (h // 2 + 1) * LANES)
                at = side * heads + h
                ones = jnp.where((lane == at + 16) | (lane == at + 32), 1.0, 0.0)
                more = jnp.where(lane == at + 48, 1.0, ones).astype(BF)
                ones = ones.astype(BF)
                mask = masks[h % 2]
                score_s[h % 2, :width] = nt(
                    jnp.concatenate([k_s[span, tile] * mask, augk_ref[span, :] + more], axis=1),
                    jnp.concatenate([q_s[rows, tile], augq_ref[rows, :]], axis=1),
                )
                slope_s[h % 2, :width] = nt(
                    jnp.concatenate(
                        [v_s[span, tile] * mask, jnp.broadcast_to(ones, (width, LANES))], axis=1
                    ),
                    jnp.concatenate([gm_s[rows, tile], augd_ref[rows, :]], axis=1),
                )

            def soften(h):
                probs = jnp.exp2(score_s[h % 2, :width])
                prob_s[h % 2, :width] = probs.astype(BF)
                back_s[h % 2, :width] = (probs * slope_s[h % 2, :width]).astype(BF)

            def collect(h):
                tile = slice(h // 2 * LANES, (h // 2 + 1) * LANES)
                mask = masks[h % 2]
                dv_s[span, tile] += nn(prob_s[h % 2, :width], gm_s[rows, tile] * mask)
                dk_s[span, tile] += nn(back_s[h % 2, :width], q_s[rows, tile] * mask)
                here = slice(h * HD, (h + 1) * HD)
                dqt_s[here, rows] = nn(kt_s[here, span], back_s[h % 2, :width])

            for step in range(heads + 2):
                if step < heads:
                    scores(step)
                if step >= 2:
                    collect(step - 2)
                if 1 <= step <= heads:
                    soften(step - 1)

        for index, width in enumerate(WINDOWS):
            pl.when(kind == index)(functools.partial(run, width))
        return carry

    lax.fori_loop(0, BLOCKS, block, 0)
    bias_ref[...] = jnp.zeros_like(bias_ref)
    bias_ref[...] = jnp.zeros_like(bias_ref)
    outs_s[0] = (dqt_s[...] * HD ** (-0.5)).T.astype(BF)
    outs_s[1] = (dk_s[...] * LN2).astype(BF)
    outs_s[2] = dv_s[...].astype(BF)
    moves.start("out", *[(outs_s.at[j], ref) for j, ref in enumerate((dq_ref, dk_ref, dv_ref))])
    bias_ref[0:1, :] = col_sum(outs_s[0].astype(F32))
    bias_ref[1:2, :] = col_sum(outs_s[2].astype(F32))
    moves.wait("x")
    xt_s[...] = x_s[...].T
    for j in range(3):
        grad_s[j] = nn(xt_s[...], outs_s[j]).astype(BF)
        moves.start(j, (grad_s.at[j], grad_ref.at[j]))
    moves.finish()


def heads_backward(side, cols, win, core, q, k, v, gm, augq, augd, augk, frames):
    width = frames.shape[1]
    part = ((SEQ, cols), BF)
    thin = ((SEQ, LANES), BF)
    sums = ((SEQ, cols), F32)
    grads = ((3, width, cols), BF)
    return call(
        functools.partial(heads_kernel, side),
        "heads_backward",
        [(SMEM, win), (SMEM, core)]
        + [(HBM, a) for a in (q, k, v, gm, augq, augd, augk, frames)],
        [(HBM, *out) for out in (part, part, part, grads)] + [(OUT, (8, cols), F32)],
        [
            part, part, part, part, thin, thin, thin, ((SEQ, width), BF),
            ((cols, SEQ), BF), ((cols, SEQ), F32), sums, sums, ((width, SEQ), BF),
            ((2, SEQ, QB), F32), ((2, SEQ, QB), F32), ((2, SEQ, QB), BF), ((2, SEQ, QB), BF),
            ((3, SEQ, cols), BF), grads,
        ],
        14,
        cost(12e9, 15e6, 5e6),
    )


def input_kernel(
    qm_ref, km_ref, vm_ref, qo_ref, ko_ref, vo_ref, g1_ref, wm_ref, wo_ref, out_ref,
    w_s, left_s, g1_s, out_s, sem,
):
    cols = wm_ref.shape[2]
    moves = Copies(sem)
    for j in range(3):
        at = slice(2 * j * cols, 2 * (j + 1) * cols)
        moves.start(("w", j), *sides((wm_ref, wo_ref), w_s.at[:, at], j))
    refs = (qm_ref, qo_ref, km_ref, ko_ref, vm_ref, vo_ref)

    def fetch(r):
        rows = slice(r * QB, (r + 1) * QB)
        moves.start(
            r,
            (g1_ref.at[rows, :], g1_s.at[rows, :]),
            *[
                (ref.at[rows, :], left_s.at[rows, n * cols : (n + 1) * cols])
                for n, ref in enumerate(refs)
            ],
        )

    fetch(0)
    moves.wait(*[("w", j) for j in range(3)])
    fetch(1)
    for r in range(BLOCKS):
        rows = slice(r * QB, (r + 1) * QB)
        moves.wait(r)
        if 0 < r < BLOCKS - 1:
            fetch(r + 1)
        out_s[rows, :] = (nt(left_s[rows, :], w_s[...]) + g1_s[rows, :]).astype(BF)
        moves.start(("out", r), (out_s.at[rows, :], out_ref.at[rows, :]))
    moves.finish()


def input_gradient(mine, other, g1, att_m, att_o):
    width = g1.shape[1]
    return call(
        input_kernel,
        "input_gradient",
        [(HBM, a) for a in (*mine, *other, g1, att_m, att_o)],
        [(HBM, (SEQ, width), BF)],
        [
            ((width, 3 * width), BF), ((SEQ, 3 * width), BF), ((SEQ, width), F32),
            ((SEQ, width), BF),
        ],
        6 + 8 * BLOCKS,
        cost(3.6e9, 15e6),
    )[0]


def swap_cores(value):
    return lax.ppermute(value, "tensor", [(0, 1), (1, 0)])


def swap_bit(value, bit, count):
    return lax.ppermute(value, "dp", [(i, i ^ (1 << bit)) for i in range(count)])


class Reduction:
    def __init__(self, count):
        self.count = count
        self.bits = count.bit_length() - 1
        self.step = 0
        self.regions = []
        turn = min(self.bits, 3)
        self.orders = [
            [(n + s) % turn for s in range(turn)] + list(range(turn, self.bits)) for n in range(3)
        ]
        self.sources = [[] for _ in range(3)]

    @property
    def columns(self):
        return sum(width for _, width in self.regions)

    def add(self, mine, other):
        self.rows = mine.shape[1] // self.count
        width = mine.shape[2]
        view = (3,) + (2,) * self.bits + (self.rows, width)
        every = list(range(self.bits - 1, -1, -1))
        at = self.columns
        for value in (mine.reshape(view), swap_cores(other).reshape(view)):
            for part in range(3):
                self.sources[part].append((value, part, every, at, width))
        self.regions.append((at, width))

    def left(self, part, step):
        gone = self.orders[part][:step]
        return [b for b in range(self.bits - 1, -1, -1) if b not in gone]

    def jobs(self, final):
        step = self.bits if final else self.step + 1
        sent = [None if final else order[self.step] for order in self.orders]
        joined = len(set(sent)) == 1
        outs = []
        jobs = []
        for part in range(3):
            bits = self.left(part, step)
            dims = (2,) * len(bits) + (self.rows, self.columns)
            if joined:
                if part == 0:
                    outs.append(((3,) + dims, F32 if final else BF))
                jobs.append((0, part, bits, sent[part], self.sources[part], self.regions))
            else:
                outs.append((dims, BF))
                jobs.append((part, None, bits, sent[part], self.sources[part], self.regions))
        return outs, jobs

    def launch(self, sends):
        turn = [order[self.step] for order in self.orders]
        if len(sends) == 1:
            got = swap_bit(sends[0], turn[0], self.count)
            moved = [(got, n) for n in range(3)]
        else:
            moved = [(swap_bit(s, b, self.count), None) for s, b in zip(sends, turn)]
        self.step += 1
        for part, (value, lead) in enumerate(moved):
            bits = self.left(part, self.step)
            self.sources[part].append((value, lead, bits, 0, self.columns))


def fold_kernel(jobs, inputs, outputs, final, place_ref, *refs):
    ins, refs = refs[:inputs], refs[inputs:]
    results, refs = refs[:outputs], refs[outputs:]
    if final:
        squares_ref, refs = refs[0], refs[1:]
    scratch, outs = refs[: -1 - outputs], refs[-1 - outputs : -1]
    moves = Copies(refs[-1])
    spot = 0
    for output, lead, bits, sent, sources, regions in jobs:
        for which, part, own_bits, at, width in sources:
            index = [] if part is None else [part]
            for bit in own_bits:
                if bit in bits:
                    index.append(slice(None))
                else:
                    index.append(1 - place_ref[bit] if bit == sent else place_ref[bit])
            moves.start(spot, (ins[which].at[tuple(index)], scratch[spot]))
            spot += 1
    squares = jnp.float32(0.0)
    spot = 0
    for number, (output, lead, bits, sent, sources, regions) in enumerate(jobs):
        target = outs[output] if lead is None else outs[output].at[lead]
        for n in range(len(sources)):
            moves.wait(spot + n)
        for at, width in regions:
            total = None
            for n, (which, part, own_bits, first, size) in enumerate(sources):
                if first <= at < first + size:
                    value = scratch[spot + n][..., at - first : at - first + width].astype(F32)
                    total = value if total is None else total + value
            target[..., at : at + width] = total.astype(target.dtype)
            if final:
                squares = squares + jnp.sum(total * total)
        spot += len(sources)
        if output not in [job[0] for job in jobs[number + 1 :]]:
            moves.start(("out", output), (outs[output], results[output]))
    moves.finish()
    if final:
        squares_ref[0, 0] = squares


def fold(place, reductions, final=False):
    arrays = []
    outs = []
    jobs = []
    counts = []
    for reduction in reductions:
        shapes, todo = reduction.jobs(final)
        for output, lead, bits, sent, sources, regions in todo:
            listed = []
            for array, part, own_bits, at, width in sources:
                known = [n for n, a in enumerate(arrays) if a is array]
                if not known:
                    arrays.append(array)
                listed.append((known[0] if known else len(arrays) - 1, part, own_bits, at, width))
            jobs.append((len(outs) + output, lead, bits, sent, listed, regions))
        outs += shapes
        counts.append(len(shapes))
    scratch = []
    for output, lead, bits, sent, sources, regions in jobs:
        for which, part, own_bits, at, width in sources:
            rows = arrays[which].shape[-2]
            scratch.append(((2,) * len(bits) + (rows, width), BF))
    size = sum(functools.reduce(lambda a, b: a * b, dims) for dims, _ in scratch)
    res = call(
        functools.partial(fold_kernel, jobs, len(arrays), len(outs), final),
        "fold",
        [(SMEM, place)] + [(HBM, a) for a in arrays],
        [(HBM, *out) for out in outs] + ([(SMEM, (1, 1), F32)] if final else []),
        scratch + [out for out in outs],
        len(scratch) + len(outs),
        cost(2 * size, 6 * size),
    )
    grouped = []
    at = 0
    for n in counts:
        grouped.append(res[at : at + n])
        at += n
    return grouped + ([res[-1]] if final else [])


def advance(place, reductions, *held):
    sends = fold(place, reductions)
    sends, held = lax.optimization_barrier((sends, held))
    for reduction, send in zip(reductions, sends):
        reduction.launch(send)
    return held


def update_kernel(
    factor_ref, down_ref, up_ref, qkv_ref, aw, am, av, fw, fm, fv, *refs
):
    factor = factor_ref[0, 0]
    small, outs = refs[:12], refs[12:]

    def adam(grad, weight, first, second, results, index, rate, decay):
        clipped = grad * factor
        first_new = 0.9 * first[index] + 0.1 * clipped
        second_new = 0.999 * second[index] + 0.001 * clipped * clipped
        mean_hat = first_new / (1.0 - 0.9**STEP)
        var_hat = second_new / (1.0 - 0.999**STEP)
        old = weight[index].astype(F32)
        results[0][index] = first_new
        results[1][index] = second_new
        results[2][index] = old - rate * (mean_hat / (jnp.sqrt(var_hat) + 1e-08) + decay * old)

    every = slice(None)
    each = down_ref.shape[2]
    rest = up_ref.shape[2] - each
    for j in range(3):
        adam(qkv_ref[j], aw, am, av, outs[0:3], (j,), 0.05, 0.01)
        cols = slice(j * rest, (j + 1) * rest)
        adam(up_ref[j, :, each:], aw, am, av, outs[0:3], (3, every, cols), 0.05, 0.01)
        cols = slice(j * each, (j + 1) * each)
        adam(up_ref[j, :, :each], fw, fm, fv, outs[3:6], (0, every, cols), 0.05, 0.01)
        adam(down_ref[j], fw, fm, fv, outs[3:6], (1, every, cols), 0.05, 0.01)
    for n in range(3):
        grad, weight, first, second = small[4 * n : 4 * n + 4]
        results = outs[6 + 3 * n : 9 + 3 * n]
        adam(grad[...], weight, first, second, results, (every, every), 0.5, 0.0)


def update(factor, down, up, qkv, attention, feedforward, small):
    arrays = [down, up, qkv, *attention, *feedforward]
    outs = [attention[1].shape] * 3 + [feedforward[1].shape] * 3
    for group in small:
        arrays += group
        outs += [group[0].shape] * 3
    return call(
        update_kernel,
        "update",
        [(SMEM, factor)] + [(OUT, a) for a in arrays],
        [(OUT, dims, F32) for dims in outs],
        [],
        0,
        cost(5e6, 6e6),
        mib=16,
    )


def local(
    frames,
    cotangent,
    segment_ids,
    pad_mask,
    attention_weight,
    feedforward_weight,
    head_bias,
    hidden_bias,
    norm_vectors,
    attention_first,
    attention_second,
    feedforward_first,
    feedforward_second,
    head_first,
    head_second,
    hidden_first,
    hidden_second,
    vector_first,
    vector_second,
):
    width = frames.shape[1]
    cols = attention_weight.shape[2]
    units = feedforward_weight.shape[2]
    count = lax.axis_size("dp")
    bits = count.bit_length() - 1
    rows = width // count
    core = lax.axis_index("tensor")
    dp_index = lax.axis_index("dp")
    core_ref = core.reshape(1).astype(I32)
    place = jnp.stack([(dp_index >> b) & 1 for b in range(bits)]).astype(I32)

    att_m, ffw_m, hid_m = attention_weight, feedforward_weight, hidden_bias
    head_m = head_bias.reshape(2, cols)
    att_o = swap_cores(att_m)
    head_o = swap_cores(head_m)
    hid_o = swap_cores(hid_m)
    ffw_late, att_o = lax.optimization_barrier((ffw_m, att_o))
    ffw_o = swap_cores(ffw_late)
    lines = (frames.shape[0] // LANES, LANES)

    q, k, v, augq, augk, mixed, win = attention_forward(
        core_ref, frames, segment_ids.reshape(lines), pad_mask.reshape(lines), att_m, att_o,
        head_m, head_o,
    )
    n1, inv, low, out_row, g2, glow, slope, down_m, down_o, sums_two = ffn_forward(
        core_ref, frames, cotangent, mixed, att_m, att_o, ffw_m, ffw_o, hid_m, hid_o, augk,
        norm_vectors,
    )
    down = Reduction(count)
    down.add(down_m, down_o)
    gup, up_m, up_o, hidden_m, hidden_o = hidden_backward(glow, slope, low, ffw_m, ffw_o)
    up = Reduction(count)
    up.add(up_m, up_o)
    (gup,) = advance(place, [down], gup)
    g1, om, oo, gm, augd, sums_one = norm_backward(
        gup, g2, n1, inv, mixed, ffw_m, ffw_o, att_m, att_o, norm_vectors
    )
    up.add(om, oo)
    (gm,) = advance(place, [down, up], gm)

    def back(side, gm):
        return heads_backward(
            side, cols, win, core_ref, q, k, v, gm, augq, augd, augk, frames
        )

    *other, other_grad, other_bias = back(1, gm)
    gm, other_grad = advance(place, [down, up], gm, other_grad)
    *mine, mine_grad, mine_bias = back(0, gm)
    qkv = Reduction(count)
    qkv.add(mine_grad, other_grad)

    side_sums = jnp.concatenate(
        [hidden_m.reshape(-1), mine_bias[:2].reshape(-1)]
    ) + swap_cores(jnp.concatenate([hidden_o.reshape(-1), other_bias[:2].reshape(-1)]))
    vector_sums = jnp.concatenate([sums_one[0:3], sums_two[3:6]], axis=0)
    vector_sums = vector_sums + swap_cores(vector_sums)
    small = jnp.concatenate([side_sums, vector_sums.reshape(-1)])
    for bit in range(bits):
        active = [r for r in (qkv, up, down) if r.step < bits]
        advance(place, active)
        small = small + swap_bit(small, bit, count)
    hidden_sum = small[:units]
    head_sum = small[units : units + 2 * cols]
    vector_sum = small[units + 2 * cols :]
    grad_row = input_gradient(mine, other, g1, att_m, att_o)

    (down_sum,), (up_sum,), early = fold(place, [down, up], final=True)
    (qkv_sum,), late = fold(place, [qkv], final=True)
    squares = (jnp.sum(hidden_sum * hidden_sum) + jnp.sum(head_sum * head_sum)) / count
    squares = squares + jnp.sum(vector_sum * vector_sum) / (2 * count)
    squares = squares + early + late
    squares = squares + swap_cores(squares)
    for bit in range(bits):
        squares = squares + swap_bit(squares, bit, count)
    gradient_norm = jnp.sqrt(squares)
    factor = jnp.minimum(1.0, 1.0 / (gradient_norm + 1e-06))

    def own(value, size, axis):
        return lax.dynamic_slice_in_dim(value, dp_index * size, size, axis)

    def flat(value):
        return value.reshape(-1, value.shape[-1])

    new = update(
        factor, down_sum, up_sum, qkv_sum,
        (own(att_m, rows, 1), attention_first, attention_second),
        (own(ffw_m, rows, 1), feedforward_first, feedforward_second),
        (
            (
                own(head_sum.reshape(2, cols), cols // count, 1), own(head_m, cols // count, 1),
                flat(head_first), flat(head_second),
            ),
            (
                own(hidden_sum.reshape(1, units), units // count, 1),
                own(hidden_bias, units // count, 1), hidden_first, hidden_second,
            ),
            (
                own(vector_sum.reshape(6, width), rows, 1), own(norm_vectors, rows, 1),
                vector_first, vector_second,
            ),
        ),
    )

    def both_rows(row):
        partner = swap_cores(row)
        lower = jnp.where(core == 0, row, partner)
        upper = jnp.where(core == 0, partner, row)
        return jnp.concatenate([lower, upper], axis=0)

    return (
        both_rows(out_row),
        both_rows(grad_row).astype(F32),
        gradient_norm.reshape(()),
        *new[:6],
        *[value.reshape(head_first.shape) for value in new[6:9]],
        *new[9:],
    )


def solution(mesh):
    weight_spec = P(None, None, "tensor")
    shard = P(None, "dp", "tensor")
    head = P(None, "tensor", "dp")
    hidden = P("tensor", "dp")
    vector = P(None, "dp")
    row = P("dp", None)
    return jax.shard_map(
        local,
        mesh=mesh,
        in_specs=(
            row, row, P("dp"), P("dp"),
            weight_spec, weight_spec,
            P(None, "tensor", None), P("tensor", None), P(),
            shard, shard, shard, shard,
            head, head, hidden, hidden, vector, vector,
        ),
        out_specs=(
            row, row, P(),
            shard, shard, shard, shard, shard, shard,
            head, head, head, hidden, hidden, hidden, vector, vector, vector,
        ),
        check_vma=False,
    )
```

```python
import functools

import jax
import jax.numpy as jnp
from jax import lax
from jax.experimental import pallas as pl
from jax.experimental.pallas import tpu as pltpu
from jax.sharding import PartitionSpec as P

HD = 64
SEQ = 1024
STEP = 10
LANES = 128
QB = 256
BLOCKS = SEQ // QB
BIG = 1e30
LOG2E = 1.4426950408889634
LN2 = 0.6931471805599453
WINDOWS = (384, 512, 640, 768, 1024)
BF = jnp.bfloat16
F32 = jnp.float32
I32 = jnp.int32


def nn(a, b):
    return jnp.dot(a, b, preferred_element_type=F32)


def nt(a, b):
    return lax.dot_general(a, b, (((1,), (1,)), ((), ())), preferred_element_type=F32)


def ds(start, size, step):
    return pl.ds(pl.multiple_of(start, step), size)


def shape(dims, dtype):
    return jax.ShapeDtypeStruct(dims, dtype)


def cost(micros):
    return pl.CostEstimate(flops=int(1.1e9 * micros), bytes_accessed=2**20, transcendentals=0)


SMEM = "smem"
HBM = "hbm"
OUT = "out"
SPACES = {SMEM: pltpu.SMEM, HBM: pltpu.HBM, OUT: pltpu.VMEM}
WHOLE = 63


def call(kernel, name, ins, outs, scratch, copies, estimate, mib=WHOLE):
    args = [
        pltpu.with_memory_space_constraint(array, pltpu.HBM) if space == HBM else array
        for space, array in ins
    ]
    return pl.pallas_call(
        kernel,
        out_shape=[
            pltpu.HBM(dims, dtype) if space == HBM else shape(dims, dtype)
            for space, dims, dtype in outs
        ],
        in_specs=[pl.BlockSpec(memory_space=SPACES[space]) for space, _ in ins],
        out_specs=[pl.BlockSpec(memory_space=SPACES[space]) for space, _, _ in outs],
        scratch_shapes=[pltpu.VMEM(dims, dtype) for dims, dtype in scratch]
        + [pltpu.SemaphoreType.DMA((max(copies, 1),))],
        compiler_params=pltpu.CompilerParams(vmem_limit_bytes=mib * 2**20),
        cost_estimate=estimate,
        name=name,
    )(*args)


class Copies:
    def __init__(self, sem):
        self.sem = sem
        self.used = 0
        self.pending = {}

    def start(self, name, *pairs):
        made = []
        for source, target in pairs:
            made.append(pltpu.make_async_copy(source, target, self.sem.at[self.used]))
            made[-1].start()
            self.used += 1
        self.pending[name] = made

    def wait(self, *names):
        for name in names:
            for copy in self.pending.pop(name):
                copy.wait()

    def finish(self):
        self.wait(*list(self.pending))


def lane_row():
    return lax.broadcasted_iota(I32, (1, LANES), 1)


def half_masks():
    low = jnp.where(lane_row() < HD, 1.0, 0.0)
    return (low.astype(BF), (1.0 - low).astype(BF))


def norm_rows(value):
    center = value - jnp.mean(value, axis=-1, keepdims=True)
    inv_std = lax.rsqrt(jnp.mean(center * center, axis=-1, keepdims=True) + 1e-05)
    return center * inv_std, inv_std


def norm_back(grad, normed, inv_std, gain):
    scaled = grad * gain
    mean_one = jnp.mean(scaled, axis=-1, keepdims=True)
    mean_two = jnp.mean(scaled * normed, axis=-1, keepdims=True)
    return inv_std * (scaled - mean_one - normed * mean_two)


def col_sum(value):
    return jnp.sum(value, axis=0, keepdims=True)


def sides(refs, target, index=None):
    size = target.shape[-1] // len(refs)
    picked = [ref if index is None else ref.at[index] for ref in refs]
    return [
        (ref, target.at[:, n * size : (n + 1) * size]) for n, ref in enumerate(picked)
    ]


def by_block(vectors, width, first, lines, each, spread):
    size = vectors.shape[1]
    count = size // (each * spread)
    rows = width // count
    row = lax.broadcasted_iota(I32, (width, size), 0)
    col = lax.broadcasted_iota(I32, (width, size), 1)
    line = row - row // rows * rows
    block = row // rows
    if spread > 1:
        hit = (col // each == spread * block + line) & (line < lines)
        value = jnp.broadcast_to(vectors[0:1, :], (width, size))
    else:
        hit = (col // each == block) & (line < lines)
        pick = lax.broadcasted_iota(I32, (width, 8), 0)
        pick = pick - pick // rows * rows == lax.broadcasted_iota(I32, (width, 8), 1)
        value = nn(jnp.where(pick, 1.0, 0.0).astype(BF), vectors.astype(BF))
    picked = jnp.where(hit, value, 0.0).astype(BF)
    source = lax.broadcasted_iota(I32, (size, LANES), 0)
    lane = lax.broadcasted_iota(I32, (size, LANES), 1)
    move = jnp.where(source - source // each * each + first == lane, 1.0, 0.0).astype(BF)
    return nn(picked, move)


def staged(count, *stages):
    for step in range(count + len(stages) - 1):
        for n, stage in enumerate(stages):
            if 0 <= step - n < count:
                stage(step - n)


def window_of(seg, real, i):
    begin = jnp.min(seg[2 * i : 2 * i + 1, :])
    end = jnp.max(seg[2 * i + 1 : 2 * i + 2, :])
    start = jnp.sum(jnp.where(seg < begin, 1, 0))
    stop = jnp.minimum(jnp.sum(jnp.where(seg <= end, 1, 0)), real)
    start = (start // LANES) * LANES
    need = stop - start
    kind = jnp.int32(0)
    size = jnp.int32(WINDOWS[0])
    for index, width in enumerate(WINDOWS[:-1]):
        kind = jnp.where(need > width, index + 1, kind)
        size = jnp.where(need > width, WINDOWS[index + 1], size)
    return jnp.minimum(start, SEQ - size), kind


def attention_kernel(
    core_ref, frames_ref, seg_ref, pad_ref, wm_ref, wo_ref, bm_ref, bo_ref,
    q_ref, k_ref, v_ref, augq_out, augk_out, mixed_ref, win_ref,
    x_s, w_s, q_s, k_s, v_s, vt_s, mt_s, lse_s, score_s, prob_s, mixed_s, augq_ref, augk_ref,
    small_s, seg_s, pad_s, sem,
):
    moves = Copies(sem)
    core = core_ref[0]
    lines = ds(core * (SEQ // LANES), SEQ // LANES, SEQ // LANES)
    moves.start("seg", (seg_ref.at[lines, :], seg_s), (pad_ref.at[lines, :], pad_s))
    moves.start("x", (frames_ref.at[ds(core * SEQ, SEQ, SEQ), :], x_s))
    for j in range(2):
        moves.start(("bias", j), *sides((bm_ref, bo_ref), small_s.at[j], j))
    moves.start(0, *sides((wm_ref, wo_ref), w_s.at[0], 0))
    lane = lane_row()
    moves.wait("seg")
    seg = seg_s[...]
    pad = pad_s[...]
    real = jnp.sum(pad)
    for i in range(BLOCKS):
        begin, kind = window_of(seg, real, i)
        win_ref[0, i] = begin
        win_ref[1, i] = kind
    for b in range(SEQ // LANES):
        rows = slice(b * LANES, (b + 1) * LANES)
        ids = jnp.broadcast_to(seg[b : b + 1, :].astype(F32), (LANES, LANES)).T
        shown = jnp.broadcast_to(pad[b : b + 1, :].astype(F32), (LANES, LANES)).T
        same = lane.astype(F32) == ids
        augk_ref[rows, :] = jnp.where(
            lane == 10, 1.0 - shown, jnp.where(same, 1.0, 0.0)
        ).astype(BF)
        off = jnp.where(same, 0.0, -BIG)
        augq_ref[rows, :] = jnp.where(
            lane < 10, off, jnp.where(lane == 10, -BIG, 0.0)
        ).astype(BF)
    moves.start("augk", (augk_ref, augk_out))
    moves.wait(("bias", 0), ("bias", 1), "x", 0)
    for j in (1, 2):
        moves.start(j, *sides((wm_ref, wo_ref), w_s.at[j], j))
    bias = [small_s[j] for j in range(2)]
    q_s[...] = ((nn(x_s[...], w_s[0]) + bias[0]) * (HD ** (-0.5) * LOG2E)).astype(BF)
    moves.start("q", (q_s, q_ref))
    moves.wait(1)
    k_s[...] = nn(x_s[...], w_s[1]).astype(BF)
    moves.start("k", (k_s, k_ref))
    moves.wait(2)
    v_s[...] = (nn(x_s[...], w_s[2]) + bias[1]).astype(BF)
    moves.start("v", (v_s, v_ref))
    vt_s[...] = v_s[...].T
    lse_s[...] = jnp.zeros_like(lse_s)
    heads = q_s.shape[1] // HD
    masks = half_masks()

    def block(i, carry):
        rows = ds(i * QB, QB, QB)
        begin = win_ref[0, i]
        kind = win_ref[1, i]

        def run(width):
            span = ds(begin, width, LANES)
            ones = jnp.ones((16, width), BF)

            def score(h):
                tile = slice(h // 2 * LANES, (h // 2 + 1) * LANES)
                right = jnp.concatenate([q_s[rows, tile], augq_ref[rows, :]], axis=1)
                left = jnp.concatenate([k_s[span, tile] * masks[h % 2], augk_ref[span, :]], axis=1)
                score_s[h % 2, :width] = nt(left, right)

            def soften(h):
                top = jnp.max(score_s[h % 2, :width], axis=0, keepdims=True)
                prob_s[h % 2, :width] = jnp.exp2(score_s[h % 2, :width] - top).astype(BF)
                return top

            def mix(h, top):
                part = slice(h * HD, (h + 1) * HD)
                out = nn(jnp.concatenate([vt_s[part, span], ones], axis=0), prob_s[h % 2, :width])
                total = out[HD : HD + 1, :]
                mt_s[part, rows] = (out[:HD, :] * (1.0 / total)).astype(BF)
                lse = top + jnp.log2(total)
                for piece in range(3):
                    lse_s[16 * (piece + 1) + h : 16 * (piece + 1) + h + 1, rows] = lse

            tops = {}
            for step in range(heads + 2):
                if step < heads:
                    score(step)
                if step >= 2:
                    mix(step - 2, tops.pop(step - 2))
                if 1 <= step <= heads:
                    tops[step - 1] = soften(step - 1)

        for index, width in enumerate(WINDOWS):
            pl.when(kind == index)(functools.partial(run, width))
        mixed_s[rows, :] = mt_s[:, rows].T
        return carry

    lax.fori_loop(0, BLOCKS, block, 0)
    moves.start("mixed", (mixed_s, mixed_ref))
    lse = lse_s[...].T
    high = lse.astype(BF).astype(F32)
    mid = (lse - high).astype(BF).astype(F32)
    piece = jnp.where(lane < 32, high, jnp.where(lane < 48, mid, lse - high - mid))
    augq_ref[...] = (augq_ref[...].astype(F32) - piece).astype(BF)
    moves.start("augq", (augq_ref, augq_out))
    moves.finish()


def attention_forward(core, frames, seg, pad, att_m, att_o, bias_m, bias_o):
    width = frames.shape[1]
    wide = ((SEQ, width), BF)
    thin = ((SEQ, LANES), BF)
    line = ((SEQ // LANES, LANES), I32)
    return call(
        attention_kernel,
        "attention_forward",
        [(SMEM, core)]
        + [(HBM, a) for a in (frames, seg, pad, att_m, att_o, bias_m, bias_o)],
        [(HBM, *wide)] * 3 + [(HBM, *thin)] * 2 + [(HBM, *wide), (SMEM, (2, BLOCKS), I32)],
        [
            wide, ((3, width, width), BF), wide, wide, wide, ((width, SEQ), BF),
            ((width, SEQ), BF), ((LANES, SEQ), F32), ((2, SEQ, QB), F32), ((2, SEQ, QB), BF),
            wide, thin, thin, ((2, 1, width), F32), line, line,
        ],
        19,
        cost(21),
    )


def gelu_pair(value):
    phi = 0.5 + 0.5 * lax.erf(value * 0.7071067811865476)
    low = value.astype(BF)
    density = jnp.exp2(low * low * BF(-0.5 * LOG2E)) * BF(0.3989422804014327)
    return (value * phi).astype(BF), phi.astype(BF) + low * density


def chunk_of(c, size):
    each = size // QB
    return c // each, ds(c % each * QB, QB, QB)


def middle_kernel(
    core_ref, frames_ref, cot_ref, mixed_ref, am_ref, ao_ref, fm_ref, fo_ref, hm_ref, ho_ref,
    augk_out, vec_out,
    n1_ref, inv_out, out_ref, gfn_ref, dm_ref, do_ref, sums_out, hsum_out,
    x_s, mixed_s, wo_s, w1_s, w2_s, cot_s, n1_s, inv_ref, low_s, g2_s, glow_s, slope_s, act_s,
    turn_s, stage_s, unit_s, ffn_s, bias_s, augk_ref, vec_ref, sum_ref, hsum_ref, sem,
):
    units = fm_ref.shape[2]
    moves = Copies(sem)
    own = ds(core_ref[0] * SEQ, SEQ, SEQ)
    moves.start("wo", *sides((am_ref, ao_ref), wo_s, 3))
    moves.start("in", (vec_out, vec_ref), (mixed_ref, mixed_s), (frames_ref.at[own, :], x_s))
    moves.start("bias", *sides((hm_ref, ho_ref), bias_s))
    moves.wait("wo", "in")
    moves.start("w1", *sides((fm_ref, fo_ref), w1_s, 0))
    sum_ref[...] = jnp.zeros_like(sum_ref)

    def project(r):
        rows = slice(r * QB, (r + 1) * QB)
        ffn_s[r % 2] = nt(mixed_s[rows, :], wo_s[...])

    def first_rows(r):
        rows = slice(r * QB, (r + 1) * QB)
        first = x_s[rows, :].astype(F32) + ffn_s[r % 2] + vec_ref[0:1, :]
        normed, inv_std = norm_rows(first)
        n1_s[rows, :] = normed
        inv_ref[rows, :] = jnp.broadcast_to(inv_std, (QB, LANES))
        low_s[rows, :] = (normed * vec_ref[1:2, :] + vec_ref[2:3, :]).astype(BF)

    staged(BLOCKS, project, first_rows)
    moves.wait("bias", "w1")
    moves.start("first", (n1_s, n1_ref), (inv_ref, inv_out))
    moves.start("cot", (cot_ref.at[own, :], cot_s), (augk_out, augk_ref))
    moves.start("w2", *sides((fm_ref, fo_ref), w2_s, 1))
    each = units // QB

    def up(c):
        unit_s[c % 2] = nn(low_s[...], w1_s[:, c * QB : (c + 1) * QB])

    def bend(c):
        spot = slice(c * QB, (c + 1) * QB)
        act, slope = gelu_pair(unit_s[c % 2] + bias_s[0:1, spot])
        act_s[:, c * QB : (c + 1) * QB] = act
        slope_s[:, c * QB : (c + 1) * QB] = slope

    staged(2 * each, up, bend)
    moves.wait("cot", "w2")

    def contract(r):
        rows = slice(r * QB, (r + 1) * QB)
        ffn_s[r % 2] = nt(act_s[rows, :], w2_s[...])

    def second(r):
        rows = slice(r * QB, (r + 1) * QB)
        first_norm = n1_s[rows, :] * vec_ref[1:2, :] + vec_ref[2:3, :]
        n2, inv_std = norm_rows(first_norm + ffn_s[r % 2] + vec_ref[3:4, :])
        valid = 1.0 - augk_ref[rows, 10:11].astype(F32)
        grad = cot_s[rows, :].astype(F32) * valid
        cot_s[rows, :] = (n2 * vec_ref[4:5, :] + vec_ref[5:6, :]).astype(BF)
        back = norm_back(grad, n2, inv_std, vec_ref[4:5, :])
        g2_s[rows, :] = back
        glow_s[rows, :] = back.astype(BF)
        sum_ref[3:4, :] += col_sum(back)
        sum_ref[4:5, :] += col_sum(grad * n2)
        sum_ref[5:6, :] += col_sum(grad)

    staged(BLOCKS, contract, second)
    moves.start("second", (cot_s, out_ref))
    size = stage_s.shape[2]
    stages = []

    def put(side, part, column, value):
        slot = len(stages) % 2
        if column == 0 and len(stages) >= 2:
            moves.wait(stages[-2])
        stage_s[slot, :, column : column + QB] = value
        if column + QB == size:
            stages.append(("part", side, part))
            moves.start(stages[-1], (stage_s.at[slot], (dm_ref, do_ref)[side].at[part]))

    turn_s[...] = glow_s[...].T
    for side in (1, 0):
        for c in range(each):
            at = side * units + c * QB
            part, column = divmod(c * QB, size)
            put(side, part, column, nn(turn_s[...], act_s[:, at : at + QB]).astype(BF))
    turn_s[...] = low_s[...].T
    order = [(side, c) for side in (1, 0) for c in range(each)]

    def columns(n):
        side, c = order[n]
        return slice(side * units + c * QB, side * units + (c + 1) * QB)

    def pull(n):
        unit_s[n % 2] = nn(glow_s[...], w2_s[:, columns(n)])

    def lean(n):
        grad = (unit_s[n % 2] * slope_s[:, columns(n)].astype(F32)).astype(BF)
        slope_s[:, columns(n)] = grad
        hsum_ref[0:1, columns(n)] = col_sum(grad.astype(F32))

    def push(n):
        side, c = order[n]
        part, column = divmod(c * QB, size)
        put(side, 3 + part, column, nn(turn_s[...], slope_s[:, columns(n)]).astype(BF))

    staged(2 * each, pull, lean, push)
    moves.start("sums", (sum_ref, sums_out), (hsum_ref, hsum_out))
    for r in range(BLOCKS):
        rows = slice(r * QB, (r + 1) * QB)
        g2_s[rows, :] += nt(slope_s[rows, :], w1_s[...])
        moves.start(("gfn", r), (g2_s.at[rows, :], gfn_ref.at[rows, :]))
    moves.finish()


def middle(core, frames, cot, mixed, att_m, att_o, ffw_m, ffw_o, hid_m, hid_o, augk, vectors):
    width = frames.shape[1]
    units = ffw_m.shape[2]
    wide = ((SEQ, width), BF)
    full = ((SEQ, width), F32)
    thin = ((SEQ, LANES), F32)
    inner = ((width, 2 * units), BF)
    outer = ((SEQ, 2 * units), BF)
    grads = ((6, width, units // 3), BF)
    ins = (frames, cot, mixed, att_m, att_o, ffw_m, ffw_o, hid_m, hid_o, augk, vectors)
    return call(
        middle_kernel,
        "middle",
        [(SMEM, core)] + [(HBM, a) for a in ins],
        [(HBM, *out) for out in (full, thin, wide, full, grads, grads)]
        + [(HBM, (8, width), F32), (HBM, (1, 2 * units), F32)],
        [
            wide, wide, ((width, width), BF), inner, inner, wide, full, thin, wide, full, wide,
            outer, outer, ((width, SEQ), BF), ((2, width, units // 3), BF), ((2, SEQ, QB), F32),
            ((2, QB, width), F32), ((1, 2 * units), F32), ((SEQ, LANES), BF),
            (vectors.shape, F32), ((8, width), F32), ((1, 2 * units), F32),
        ],
        36,
        cost(47),
    )


def norm_kernel(
    count, gfn_ref, n1_ref, inv_out, mixed_ref, am_ref, ao_ref, vec_out, sums_out, hsum_out,
    g1_ref, om_ref, oo_ref, gm_ref, augd_out,
    gfn_s, n1_s, inv_ref, mixed_s, wo_s, vec_ref,
    glow_s, glt_s, gm_s, augd_ref, om_s, oo_s, sum_ref, hsum_ref, sem,
):
    moves = Copies(sem)
    g1_s = gfn_s
    moves.start("sums", (sums_out, sum_ref), (hsum_out, hsum_ref))
    moves.start("vec", (vec_out, vec_ref), (inv_out, inv_ref))
    for r in range(BLOCKS):
        rows = slice(r * QB, (r + 1) * QB)
        moves.start(
            r, (gfn_ref.at[rows, :], gfn_s.at[rows, :]), (n1_ref.at[rows, :], n1_s.at[rows, :])
        )
        if r == 0:
            moves.wait("vec", "sums", 0)
    moves.start("wo", *sides((am_ref, ao_ref), wo_s, 3))
    moves.start("mixed", (mixed_ref, mixed_s))
    for r in range(BLOCKS):
        rows = slice(r * QB, (r + 1) * QB)
        if r > 0:
            moves.wait(r)
        grad = gfn_s[rows, :]
        n1 = n1_s[rows, :]
        back = norm_back(grad, n1, inv_ref[rows, 0:1], vec_ref[1:2, :])
        g1_s[rows, :] = back
        glow_s[rows, :] = back.astype(BF)
        sum_ref[0:1, :] += col_sum(back)
        sum_ref[1:2, :] += col_sum(grad * n1)
        sum_ref[2:3, :] += col_sum(grad)
    moves.start("g1", (g1_s, g1_ref))
    moves.wait("wo", "mixed")
    lane = lane_row()
    width = wo_s.shape[0]
    head = lax.broadcasted_iota(I32, (width, LANES), 0) // HD
    spot = lax.broadcasted_iota(I32, (width, LANES), 1)
    pick = jnp.where((spot == head + 16) | (spot == head + 32), 1.0, 0.0).astype(BF)
    for r in range(BLOCKS):
        rows = slice(r * QB, (r + 1) * QB)
        gm = nn(glow_s[rows, :], wo_s[...]).astype(BF)
        gm_s[rows, :] = gm
        both = gm.astype(F32) * mixed_s[rows, :].astype(F32)
        high = both.astype(BF)
        dots = nn(high, pick) + nn((both - high.astype(F32)).astype(BF), pick)
        dot_high = dots.astype(BF).astype(F32)
        augd_ref[rows, :] = (-jnp.where(lane < 32, dot_high, dots - dot_high)).astype(BF)
    moves.start("gm", (gm_s, gm_ref), (augd_ref, augd_out))
    glt_s[...] = glow_s[...].T
    size = om_s.shape[2]
    vectors = by_block(sum_ref[...], width, 0, 6, width // count, 1)
    units = hsum_ref.shape[1] // 2
    for side, target, result in ((1, oo_s, oo_ref), (0, om_s, om_ref)):
        cols = slice(side * 3 * size, (side + 1) * 3 * size)
        product = nn(glt_s[...], mixed_s[:, cols]).astype(BF)
        for part in range(3):
            target[part] = product[:, part * size : (part + 1) * size]
        hidden = hsum_ref[:, side * units : (side + 1) * units]
        hidden = by_block(hidden, width, LANES // 2, 2, units // count // 2, 2)
        target[3] = (vectors + hidden).astype(BF)
        moves.start(("o", side), (target, result))
    moves.finish()


def norm_backward(count, gfn, n1, inv, mixed, att_m, att_o, vectors, sums, hidden_sums):
    width = n1.shape[1]
    cols = att_m.shape[2]
    wide = ((SEQ, width), BF)
    full = ((SEQ, width), F32)
    thin = ((SEQ, LANES), BF)
    grads = ((4, width, cols // 3), BF)
    ins = (gfn, n1, inv, mixed, att_m, att_o, vectors, sums, hidden_sums)
    return call(
        functools.partial(norm_kernel, count),
        "norm_backward",
        [(HBM, a) for a in ins],
        [(HBM, *out) for out in (full, grads, grads, wide, thin)],
        [
            full, full, ((SEQ, LANES), F32), wide, ((width, width), BF), (vectors.shape, F32),
            wide, ((width, SEQ), BF), wide, thin, grads, grads, (sums.shape, F32),
            (hidden_sums.shape, F32),
        ],
        21,
        cost(11),
    )


def heads_kernel(
    side, count,
    win_ref, core_ref, q_ref, k_ref, v_ref, gm_ref, augq_out, augd_out, augk_out, frames_ref,
    dq_ref, dk_ref, dv_ref, grad_ref,
    q_s, k_s, v_s, gm_s, augq_ref, augd_ref, augk_ref, x_s,
    kt_s, dqt_s, dk_s, dv_s, xt_s, score_s, slope_s, prob_s, back_s, outs_s, grad_s, bias_ref, block_s, sem,
):
    cols = dk_s.shape[1]
    heads = cols // HD
    moves = Copies(sem)
    own = slice(side * cols, (side + 1) * cols)
    moves.start(
        "in",
        *[
            (ref.at[:, own], to)
            for ref, to in ((k_ref, k_s), (q_ref, q_s), (v_ref, v_s), (gm_ref, gm_s))
        ],
        (augq_out, augq_ref), (augd_out, augd_ref), (augk_out, augk_ref),
    )
    dk_s[...] = jnp.zeros_like(dk_s)
    dv_s[...] = jnp.zeros_like(dv_s)
    moves.wait("in")
    moves.start("x", (frames_ref.at[ds(core_ref[0] * SEQ, SEQ, SEQ), :], x_s))
    kt_s[...] = k_s[...].T
    masks = half_masks()
    lane = lane_row()

    def block(i, carry):
        rows = ds(i * QB, QB, QB)
        begin = win_ref[0, i]
        kind = win_ref[1, i]

        def run(width):
            span = ds(begin, width, LANES)

            def scores(h):
                tile = slice(h // 2 * LANES, (h // 2 + 1) * LANES)
                at = side * heads + h
                ones = jnp.where((lane == at + 16) | (lane == at + 32), 1.0, 0.0)
                more = jnp.where(lane == at + 48, 1.0, ones).astype(BF)
                ones = ones.astype(BF)
                mask = masks[h % 2]
                score_s[h % 2, :width] = nt(
                    jnp.concatenate([k_s[span, tile] * mask, augk_ref[span, :] + more], axis=1),
                    jnp.concatenate([q_s[rows, tile], augq_ref[rows, :]], axis=1),
                )
                slope_s[h % 2, :width] = nt(
                    jnp.concatenate(
                        [v_s[span, tile] * mask, jnp.broadcast_to(ones, (width, LANES))], axis=1
                    ),
                    jnp.concatenate([gm_s[rows, tile], augd_ref[rows, :]], axis=1),
                )

            def soften(h):
                probs = jnp.exp2(score_s[h % 2, :width])
                prob_s[h % 2, :width] = probs.astype(BF)
                back_s[h % 2, :width] = (probs * slope_s[h % 2, :width]).astype(BF)

            def collect(h):
                tile = slice(h // 2 * LANES, (h // 2 + 1) * LANES)
                mask = masks[h % 2]
                dv_s[span, tile] += nn(prob_s[h % 2, :width], gm_s[rows, tile] * mask)
                dk_s[span, tile] += nn(back_s[h % 2, :width], q_s[rows, tile] * mask)
                here = slice(h * HD, (h + 1) * HD)
                dqt_s[here, rows] = nn(kt_s[here, span], back_s[h % 2, :width])

            for step in range(heads + 2):
                if step < heads:
                    scores(step)
                if step >= 2:
                    collect(step - 2)
                if 1 <= step <= heads:
                    soften(step - 1)

        for index, width in enumerate(WINDOWS):
            pl.when(kind == index)(functools.partial(run, width))
        return carry

    lax.fori_loop(0, BLOCKS, block, 0)
    bias_ref[...] = jnp.zeros_like(bias_ref)
    bias_ref[...] = jnp.zeros_like(bias_ref)
    outs_s[0] = (dqt_s[...] * HD ** (-0.5)).T.astype(BF)
    outs_s[1] = (dk_s[...] * LN2).astype(BF)
    outs_s[2] = dv_s[...].astype(BF)
    moves.start("out", *[(outs_s.at[j], ref) for j, ref in enumerate((dq_ref, dk_ref, dv_ref))])
    bias_ref[0:1, :] = col_sum(outs_s[0].astype(F32))
    bias_ref[1:2, :] = col_sum(outs_s[2].astype(F32))
    width = grad_s.shape[1]
    block_s[...] = by_block(bias_ref[...], width, 0, 2, cols // count, 1).astype(BF)
    moves.start("bias", (block_s, grad_ref.at[3, :, :LANES]))
    moves.wait("x")
    xt_s[...] = x_s[...].T
    for j in range(3):
        grad_s[j] = nn(xt_s[...], outs_s[j]).astype(BF)
        moves.start(j, (grad_s.at[j], grad_ref.at[j]))
    moves.finish()


def heads_backward(side, count, cols, win, core, q, k, v, gm, augq, augd, augk, frames):
    width = frames.shape[1]
    part = ((SEQ, cols), BF)
    thin = ((SEQ, LANES), BF)
    sums = ((SEQ, cols), F32)
    grads = ((3, width, cols), BF)
    blocks = ((4, width, cols), BF)
    return call(
        functools.partial(heads_kernel, side, count),
        "heads_backward",
        [(SMEM, win), (SMEM, core)]
        + [(HBM, a) for a in (q, k, v, gm, augq, augd, augk, frames)],
        [(HBM, *out) for out in (part, part, part, blocks)],
        [
            part, part, part, part, thin, thin, thin, ((SEQ, width), BF),
            ((cols, SEQ), BF), ((cols, SEQ), F32), sums, sums, ((width, SEQ), BF),
            ((2, SEQ, QB), F32), ((2, SEQ, QB), F32), ((2, SEQ, QB), BF), ((2, SEQ, QB), BF),
            ((3, SEQ, cols), BF), grads, ((8, cols), F32), ((width, LANES), BF),
        ],
        15,
        cost(19),
    )


def input_kernel(
    core_ref, qm_ref, km_ref, vm_ref, qo_ref, ko_ref, vo_ref, g1_ref, wm_ref, wo_ref,
    row_ref, partner_ref, out_ref, both_ref,
    w_s, left_s, g1_s, out_s, rows_s, sem,
):
    cols = wm_ref.shape[2]
    moves = Copies(sem)
    core = core_ref[0]
    for j in range(3):
        at = slice(2 * j * cols, 2 * (j + 1) * cols)
        moves.start(("w", j), *sides((wm_ref, wo_ref), w_s.at[:, at], j))
    refs = (qm_ref, qo_ref, km_ref, ko_ref, vm_ref, vo_ref)

    def fetch(r):
        rows = slice(r * QB, (r + 1) * QB)
        moves.start(
            r,
            (g1_ref.at[rows, :], g1_s.at[rows, :]),
            *[
                (ref.at[rows, :], left_s.at[rows, n * cols : (n + 1) * cols])
                for n, ref in enumerate(refs)
            ],
        )

    fetch(0)
    moves.wait(*[("w", j) for j in range(3)])
    fetch(1)
    for r in range(BLOCKS):
        rows = slice(r * QB, (r + 1) * QB)
        moves.wait(r)
        if 0 < r < BLOCKS - 1:
            fetch(r + 1)
        out_s[rows, :] = (nt(left_s[rows, :], w_s[...]) + g1_s[rows, :]).astype(BF)
        moves.start(("out", r), (out_s.at[rows, :], out_ref.at[rows, :]))
        if r == 0:
            moves.start("rows", (row_ref, rows_s.at[0]), (partner_ref, rows_s.at[1]))
    moves.wait("rows")
    moves.start(
        "both",
        (rows_s.at[0], both_ref.at[ds(core * SEQ, SEQ, SEQ), :]),
        (rows_s.at[1], both_ref.at[ds((1 - core) * SEQ, SEQ, SEQ), :]),
    )
    moves.finish()


def input_gradient(core, mine, other, g1, att_m, att_o, row, partner):
    width = g1.shape[1]
    return call(
        input_kernel,
        "input_gradient",
        [(SMEM, core)] + [(HBM, a) for a in (*mine, *other, g1, att_m, att_o, row, partner)],
        [(HBM, (SEQ, width), BF), (HBM, (2 * SEQ, width), BF)],
        [
            ((width, 3 * width), BF), ((SEQ, 3 * width), BF), ((SEQ, width), F32),
            ((SEQ, width), BF), ((2, SEQ, width), BF),
        ],
        10 + 8 * BLOCKS,
        cost(10),
        mib=30,
    )


def widen_kernel(core_ref, row_ref, partner_ref, out_ref, low_s, high_s, sem):
    core = core_ref[0]
    moves = Copies(sem)
    spots = [(half, r) for half in range(2) for r in range(2)]
    size = SEQ // 2
    for half, r in spots:
        rows = slice(r * size, (r + 1) * size)
        ref = (row_ref, partner_ref)[half]
        moves.start((half, r), (ref.at[rows, :], low_s.at[half, rows, :]))
    for half, r in spots:
        rows = slice(r * size, (r + 1) * size)
        moves.wait((half, r))
        high_s[half, rows, :] = low_s[half, rows, :].astype(F32)
        place = core if half == 0 else 1 - core
        moves.start(
            ("out", half, r),
            (high_s.at[half, rows, :], out_ref.at[ds(place * SEQ + r * size, size, size), :]),
        )
    moves.finish()


def widen(core, row, partner):
    return call(
        widen_kernel,
        "widen",
        [(SMEM, core), (HBM, row), (HBM, partner)],
        [(HBM, (2 * SEQ, row.shape[1]), F32)],
        [((2, *row.shape), BF), ((2, *row.shape), F32)],
        8,
        cost(4),
        mib=16,
    )[0]


def swap_cores(value):
    return lax.ppermute(value, "tensor", [(0, 1), (1, 0)])


def swap_bit(value, bit, count):
    return lax.ppermute(value, "dp", [(i, i ^ (1 << bit)) for i in range(count)])


class Reduction:
    def __init__(self, count):
        self.count = count
        self.memory = HBM
        self.bits = count.bit_length() - 1
        self.step = 0
        self.widths = [[], [], []]
        turn = min(self.bits, 3)
        self.orders = [
            [(n + s) % turn for s in range(turn)] + list(range(turn, self.bits)) for n in range(3)
        ]
        self.sources = [[], [], []]

    def columns(self, part):
        return sum(self.widths[part])

    def starts(self):
        return [sum(self.columns(p) for p in range(part)) for part in range(4)]

    def add(self, mine, other, leads, width):
        self.rows = mine.shape[1] // self.count
        view = (mine.shape[0],) + (2,) * self.bits + (self.rows, mine.shape[2])
        every = list(range(self.bits - 1, -1, -1))
        pair = (mine.reshape(view), other.reshape(view))
        for part, lead in enumerate(leads):
            for value in pair:
                at = self.columns(part)
                self.sources[part].append((HBM, value, lead, every, 0, at, width))
            self.widths[part].append(width)

    def left(self, part, step):
        gone = self.orders[part][:step]
        return [b for b in range(self.bits - 1, -1, -1) if b not in gone]

    def jobs(self, final):
        step = self.bits if final else self.step + 1
        sent = [None if final else order[self.step] for order in self.orders]
        joined = len(set(sent)) == 1
        starts = self.starts()
        outs = []
        jobs = []
        for part in range(3):
            bits = self.left(part, step)
            dims = (2,) * len(bits) + (self.rows,)
            if joined:
                if part == 0:
                    memory = OUT if final else self.memory
                    outs.append((memory, dims + (starts[3],), F32 if final else BF))
                spot = (0, starts[part])
            else:
                outs.append((self.memory, dims + (self.columns(part),), BF))
                spot = (part, 0)
            jobs.append((*spot, bits, sent[part], self.sources[part], self.widths[part]))
        if self.step > 0 and not final:
            for part in range(3):
                bits = self.left(part, step)
                dims = (2,) * len(bits) + (self.rows, self.columns(part))
                outs.append((self.memory, dims, F32))
                jobs.append(
                    (len(outs) - 1, 0, bits, None, self.sources[part], self.widths[part])
                )
        return outs, jobs

    def launch(self, values):
        turn = [order[self.step] for order in self.orders]
        kept = self.step > 0
        sends = values[:-3] if kept else values
        if len(sends) == 1:
            got = swap_bit(sends[0], turn[0], self.count)
            moved = [(got, at) for at in self.starts()[:3]]
        else:
            moved = [(swap_bit(s, b, self.count), 0) for s, b in zip(sends, turn)]
        self.step += 1
        for part, (value, skip) in enumerate(moved):
            bits = self.left(part, self.step)
            columns = self.columns(part)
            if kept:
                own = values[part - 3]
                self.sources[part] = [(self.memory, own, None, bits, 0, 0, columns)]
            self.sources[part].append((self.memory, value, None, bits, skip, 0, columns))


def fold_kernel(jobs, spaces, spans, final, extra, place_ref, *refs):
    ins, refs = refs[: len(spaces)], refs[len(spaces) :]
    if extra:
        early_ref, refs = refs[0], refs[1:]
    results, refs = refs[: len(spans)], refs[len(spans) :]
    if final:
        squares_ref, refs = refs[0], refs[1:]
    moves = Copies(refs[-1])
    scratch = list(refs[:-1])
    outs = [scratch.pop() if space == HBM else ref for space, ref in zip(spans, results)]
    values = []
    for number, (output, column, bits, sent, sources, widths) in enumerate(jobs):
        found = []
        for which, lead, own_bits, skip, at, width in sources:
            index = [] if lead is None else [lead]
            for bit in own_bits:
                if bit in bits:
                    index.append(slice(None))
                else:
                    index.append(1 - place_ref[bit] if bit == sent else place_ref[bit])
            if spaces[which] == HBM:
                target = scratch.pop(0)
                index += [slice(None), slice(skip, skip + width)]
                moves.start((number, len(found)), (ins[which].at[tuple(index)], target))
                found.append((target, (), 0))
            else:
                found.append((ins[which], tuple(index), skip))
        values.append(found)
    squares = jnp.float32(0.0)
    for number, (output, column, bits, sent, sources, widths) in enumerate(jobs):
        total = [None for _ in widths]
        starts = [sum(widths[:n]) for n in range(len(widths))]
        for n, (which, lead, own_bits, skip, first, size) in enumerate(sources):
            if spaces[which] == HBM:
                moves.wait((number, n))
            ref, index, skip = values[number][n]
            for spot, (at, width) in enumerate(zip(starts, widths)):
                if first <= at < first + size:
                    cols = slice(skip + at - first, skip + at - first + width)
                    value = ref[(*index, Ellipsis, cols)].astype(F32)
                    total[spot] = value if total[spot] is None else total[spot] + value
        for at, width, value in zip(starts, widths, total):
            outs[output][..., column + at : column + at + width] = value.astype(
                outs[output].dtype
            )
            if final:
                squares = squares + jnp.sum(value * value)
                if number == 0 and final == "shared" and at == starts[-1]:
                    lane = lax.broadcasted_iota(I32, value.shape, 1)
                    line = lax.broadcasted_iota(I32, value.shape, 0)
                    both = jnp.where((lane < LANES // 2) & (line < 6), value, 0.0)
                    squares = squares - 0.5 * jnp.sum(both * both)
        if spans[output] == HBM:
            if output not in [job[0] for job in jobs[number + 1 :]]:
                moves.start(("out", output), (outs[output], results[output]))
    if extra:
        squares_ref[...] = jnp.full(squares_ref.shape, squares + early_ref[0, 0], F32)
    elif final:
        squares_ref[0, 0] = squares
    moves.finish()


def fold(place, reductions, final=False, extra=None):
    arrays = []
    outs = []
    jobs = []
    counts = []
    for reduction in reductions:
        shapes, todo = reduction.jobs(final)
        for output, column, bits, sent, sources, widths in todo:
            listed = []
            for space, array, *rest in sources:
                known = [n for n, (_, a) in enumerate(arrays) if a is array]
                if not known:
                    arrays.append((space, array))
                listed.append((known[0] if known else len(arrays) - 1, *rest))
            jobs.append((len(outs) + output, column, bits, sent, listed, widths))
        outs += shapes
        counts.append(len(shapes))
    scratch = []
    for output, column, bits, sent, sources, widths in jobs:
        for which, lead, own_bits, skip, at, width in sources:
            if arrays[which][0] == HBM:
                array = arrays[which][1]
                scratch.append(((2,) * len(bits) + (array.shape[-2], width), array.dtype))
    copies = len(scratch)
    for space, dims, dtype in reversed(outs):
        if space == HBM:
            scratch.append((dims, dtype))
            copies += 1

    def volume(dims):
        return 4 * functools.reduce(lambda a, b: a * b, dims)

    last = []
    if extra:
        last = [(OUT, (2 * extra[1], LANES), F32)]
    elif final:
        last = [(SMEM, (1, 1), F32)]
    size = sum(volume(dims) for dims, _ in scratch)
    size += sum(volume(a.shape) for space, a in arrays if space == OUT)
    size += sum(volume(dims) for space, dims, _ in outs if space == OUT)
    res = call(
        functools.partial(
            fold_kernel, jobs, [space for space, _ in arrays], [out[0] for out in outs], final,
            bool(extra),
        ),
        "fold",
        [(SMEM, place)] + arrays + ([(SMEM, extra[0])] if extra else []),
        outs + last,
        scratch,
        copies,
        cost(2),
        mib=4 + size // 2**20,
    )
    grouped = []
    at = 0
    for n in counts:
        grouped.append(list(res[at : at + n]))
        at += n
    return grouped + ([res[-1]] if final else [])


def tie(value, *others):
    return lax.optimization_barrier((value, others))[0]


def advance(place, reductions, after):
    values = fold(tie(place, after), reductions)
    values = lax.optimization_barrier(values)
    for reduction, value in zip(reductions, values):
        reduction.launch(value)
    return values


def update_kernel(
    squares_ref, ffn_ref, qkv_ref, aw, am, av, fw, fm, fv, *refs
):
    small, outs, norm_ref = refs[:9], refs[9:-2], refs[-2]
    norm = jnp.sqrt(col_sum(squares_ref[...])[:, 0:1])
    norm_ref[...] = norm
    factor = jnp.minimum(1.0, 1.0 / (norm + 1e-06))

    def adam(grad, weight, first, second, results, index, rate, decay):
        clipped = grad * factor
        first_new = 0.9 * first[index] + 0.1 * clipped
        second_new = 0.999 * second[index] + 0.001 * clipped * clipped
        mean_hat = first_new / (1.0 - 0.9**STEP)
        var_hat = second_new / (1.0 - 0.999**STEP)
        old = weight[index].astype(F32)
        results[0][index] = first_new
        results[1][index] = second_new
        results[2][index] = old - rate * (mean_hat / (jnp.sqrt(var_hat) + 1e-08) + decay * old)

    every = slice(None)
    each = fw.shape[2] // 3
    wide = aw.shape[2]
    rest = wide // 3
    ends = [small[3 * n].shape[1] for n in range(3)]
    here = 2 * each + rest
    lines = ffn_ref[0:6, here : here + ends[2]]
    half = ends[1] // 2
    spot = here + LANES // 2
    hidden = jnp.concatenate(
        [ffn_ref[0:1, spot : spot + half], ffn_ref[1:2, spot : spot + half]], axis=1
    )
    tails = (qkv_ref[0:2, wide : wide + ends[0]], hidden, lines)
    for j in range(3):
        at = 0 if j == 0 else LANES + j * wide
        adam(qkv_ref[:, at : at + wide], aw, am, av, outs[0:3], (j,), 0.05, 0.01)
        at = 0 if j == 0 else LANES + j * here
        cols = slice(j * rest, (j + 1) * rest)
        grad = ffn_ref[:, at + 2 * each : at + here]
        adam(grad, aw, am, av, outs[0:3], (3, every, cols), 0.05, 0.01)
        cols = slice(j * each, (j + 1) * each)
        grad = ffn_ref[:, at + each : at + 2 * each]
        adam(grad, fw, fm, fv, outs[3:6], (0, every, cols), 0.05, 0.01)
        adam(ffn_ref[:, at : at + each], fw, fm, fv, outs[3:6], (1, every, cols), 0.05, 0.01)
    for n in range(3):
        weight, first, second = small[3 * n : 3 * n + 3]
        results = outs[6 + 3 * n : 9 + 3 * n]
        adam(tails[n], weight, first, second, results, (every, every), 0.5, 0.0)


def update(squares, ffn, qkv, attention, feedforward, small):
    arrays = [squares, ffn, qkv, *attention, *feedforward]
    outs = [attention[1].shape] * 3 + [feedforward[1].shape] * 3
    for group in small:
        arrays += group
        outs += [group[0].shape] * 3
    return call(
        update_kernel,
        "update",
        [(OUT, a) for a in arrays],
        [(OUT, dims, F32) for dims in outs] + [(OUT, (1, 1), F32)],
        [],
        0,
        cost(2),
        mib=16,
    )


def local(
    frames,
    cotangent,
    segment_ids,
    pad_mask,
    attention_weight,
    feedforward_weight,
    head_bias,
    hidden_bias,
    norm_vectors,
    attention_first,
    attention_second,
    feedforward_first,
    feedforward_second,
    head_first,
    head_second,
    hidden_first,
    hidden_second,
    vector_first,
    vector_second,
):
    width = frames.shape[1]
    cols = attention_weight.shape[2]
    units = feedforward_weight.shape[2]
    count = lax.axis_size("dp")
    bits = count.bit_length() - 1
    rows = width // count
    core = lax.axis_index("tensor")
    dp_index = lax.axis_index("dp")
    core_ref = core.reshape(1).astype(I32)
    place = jnp.stack([(dp_index >> b) & 1 for b in range(bits)]).astype(I32)

    att_m, ffw_m, hid_m = attention_weight, feedforward_weight, hidden_bias
    att_o = swap_cores(att_m)
    head_o = swap_cores(head_bias)
    hid_o = swap_cores(hid_m)
    ffw_o = swap_cores(tie(ffw_m, att_o, head_o, hid_o))
    lines = (frames.shape[0] // LANES, LANES)

    def own(value, size, axis):
        return lax.dynamic_slice_in_dim(value, dp_index * size, size, axis)

    old_att = own(att_m, rows, 1)
    old_ffw = own(ffw_m, rows, 1)
    old_head = own(head_bias.reshape(2, cols), cols // count, 1)
    old_hidden = own(hidden_bias, units // count, 1)
    old_vectors = own(norm_vectors, rows, 1)
    core_ref, *olds = lax.optimization_barrier(
        (core_ref, old_att, old_ffw, old_head, old_hidden, old_vectors)
    )
    old_att, old_ffw, old_head, old_hidden, old_vectors = olds
    q, k, v, augq, augk, mixed, win = attention_forward(
        core_ref, frames, segment_ids.reshape(lines), pad_mask.reshape(lines), att_m, att_o,
        head_bias, head_o,
    )
    n1, inv, out_row, gfn, ffn_m, ffn_o, sums, hidden_sums = middle(
        core_ref, frames, cotangent, mixed, att_m, att_o, ffw_m, ffw_o, hid_m, hid_o, augk,
        norm_vectors,
    )
    ffn_o = swap_cores(ffn_o)
    out_other = swap_cores(out_row)
    g1, om, oo, gm, augd = norm_backward(
        count, gfn, n1, inv, mixed, att_m, att_o, norm_vectors, sums, hidden_sums
    )
    oo = swap_cores(oo)
    ffn = Reduction(count)
    ffn.add(ffn_m, ffn_o, (0, 1, 2), units // 3)
    ffn.add(ffn_m, ffn_o, (3, 4, 5), units // 3)
    ffn.add(om, oo, (0, 1, 2), cols // 3)
    ffn.add(om, oo, (3,), LANES)
    sent = advance(place, [ffn], gm)

    def back(side, gm):
        return heads_backward(
            side, count, cols, win, core_ref, q, k, v, gm, augq, augd, augk, frames
        )

    *other, other_grad = back(1, tie(gm, sent))
    other_grad = swap_cores(other_grad)
    sent = advance(place, [ffn], other[0])
    *mine, mine_grad = back(0, tie(gm, sent))
    qkv = Reduction(count)
    qkv.add(mine_grad, other_grad, (0, 1, 2), cols)
    qkv.add(mine_grad, other_grad, (3,), LANES)
    for reduction in (qkv, ffn):
        reduction.memory = OUT
    sent = advance(place, [qkv, ffn], mine_grad)
    grad_row, layer_output = input_gradient(
        core_ref, mine, other, tie(g1, sent), att_m, att_o, out_row, out_other
    )
    grad_other = swap_cores(grad_row)
    sent = advance(place, [qkv], grad_row)
    frame_grads = widen(core_ref, tie(grad_row, sent), grad_other)
    sent = (sent, frame_grads)
    while qkv.step < bits:
        sent = advance(place, [r for r in (qkv, ffn) if r.step < bits], sent)
    while ffn.step < bits:
        sent = advance(place, [ffn], sent)
    (ffn_sum,), early = fold(tie(place, sent), [ffn], final="shared")
    (qkv_sum,), squares = fold(tie(place, early), [qkv], final="own", extra=(early, count))
    squares = lax.all_to_all(squares, ("dp", "tensor"), 0, 0, tiled=True)

    def flat(value):
        return value.reshape(-1, value.shape[-1])

    new = update(
        squares, ffn_sum, qkv_sum,
        (old_att, attention_first, attention_second),
        (old_ffw, feedforward_first, feedforward_second),
        (
            (old_head, flat(head_first), flat(head_second)),
            (old_hidden, hidden_first, hidden_second),
            (old_vectors, vector_first, vector_second),
        ),
    )
    return (
        layer_output,
        frame_grads,
        new[15].reshape(()),
        *new[:6],
        *[value.reshape(head_first.shape) for value in new[6:9]],
        *new[9:15],
    )


def solution(mesh):
    weight_spec = P(None, None, "tensor")
    shard = P(None, "dp", "tensor")
    head = P(None, "tensor", "dp")
    hidden = P("tensor", "dp")
    vector = P(None, "dp")
    row = P("dp", None)
    return jax.shard_map(
        local,
        mesh=mesh,
        in_specs=(
            row, row, P("dp"), P("dp"),
            weight_spec, weight_spec,
            P(None, "tensor", None), P("tensor", None), P(),
            shard, shard, shard, shard,
            head, head, hidden, hidden, vector, vector,
        ),
        out_specs=(
            row, row, P(),
            shard, shard, shard, shard, shard, shard,
            head, head, head, hidden, hidden, hidden, vector, vector, vector,
        ),
        check_vma=False,
    )
```

```python
import functools

import jax
import jax.numpy as jnp
from jax import lax
from jax.experimental import pallas as pl
from jax.experimental.pallas import tpu as pltpu
from jax.sharding import PartitionSpec as P

HD = 64
SEQ = 1024
STEP = 10
LANES = 128
QB = 256
BLOCKS = SEQ // QB
BIG = 1e30
LOG2E = 1.4426950408889634
LN2 = 0.6931471805599453
WINDOWS = (384, 512, 640, 768, 1024)
BF = jnp.bfloat16
F32 = jnp.float32
I32 = jnp.int32


def nn(a, b):
    return jnp.dot(a, b, preferred_element_type=F32)


def nt(a, b):
    return lax.dot_general(a, b, (((1,), (1,)), ((), ())), preferred_element_type=F32)


def ds(start, size, step):
    return pl.ds(pl.multiple_of(start, step), size)


def shape(dims, dtype):
    return jax.ShapeDtypeStruct(dims, dtype)


LONG = 100


def cost(micros):
    return pl.CostEstimate(flops=int(1.1e9 * micros), bytes_accessed=2**20, transcendentals=0)


SMEM = "smem"
HBM = "hbm"
FREE = "free"
OUT = "out"
SPACES = {SMEM: pltpu.SMEM, HBM: pltpu.HBM, FREE: pl.ANY, OUT: pltpu.VMEM}
WHOLE = 63


def call(kernel, name, ins, outs, scratch, copies, estimate, mib=WHOLE):
    args = [
        pltpu.with_memory_space_constraint(array, pltpu.HBM) if space == HBM else array
        for space, array in ins
    ]
    return pl.pallas_call(
        kernel,
        out_shape=[
            pltpu.HBM(dims, dtype) if space == HBM else shape(dims, dtype)
            for space, dims, dtype in outs
        ],
        in_specs=[pl.BlockSpec(memory_space=SPACES[space]) for space, _ in ins],
        out_specs=[pl.BlockSpec(memory_space=SPACES[space]) for space, _, _ in outs],
        scratch_shapes=[pltpu.VMEM(dims, dtype) for dims, dtype in scratch]
        + [pltpu.SemaphoreType.DMA((max(copies, 1),))],
        compiler_params=pltpu.CompilerParams(vmem_limit_bytes=mib * 2**20),
        cost_estimate=estimate,
        name=name,
    )(*args)


class Copies:
    def __init__(self, sem):
        self.sem = sem
        self.used = 0
        self.pending = {}

    def start(self, name, *pairs):
        made = []
        for source, target in pairs:
            made.append(pltpu.make_async_copy(source, target, self.sem.at[self.used]))
            made[-1].start()
            self.used += 1
        self.pending[name] = made

    def wait(self, *names):
        for name in names:
            for copy in self.pending.pop(name):
                copy.wait()

    def finish(self):
        self.wait(*list(self.pending))


def lane_row():
    return lax.broadcasted_iota(I32, (1, LANES), 1)


def half_masks():
    low = jnp.where(lane_row() < HD, 1.0, 0.0)
    return (low.astype(BF), (1.0 - low).astype(BF))


def norm_rows(value):
    center = value - jnp.mean(value, axis=-1, keepdims=True)
    inv_std = lax.rsqrt(jnp.mean(center * center, axis=-1, keepdims=True) + 1e-05)
    return center * inv_std, inv_std


def norm_back(grad, normed, inv_std, gain):
    scaled = grad * gain
    mean_one = jnp.mean(scaled, axis=-1, keepdims=True)
    mean_two = jnp.mean(scaled * normed, axis=-1, keepdims=True)
    return inv_std * (scaled - mean_one - normed * mean_two)


def col_sum(value):
    return jnp.sum(value, axis=0, keepdims=True)


def sides(refs, target, index=None):
    size = target.shape[-1] // len(refs)
    picked = [ref if index is None else ref.at[index] for ref in refs]
    return [
        (ref, target.at[:, n * size : (n + 1) * size]) for n, ref in enumerate(picked)
    ]


def by_block(vectors, width, first, lines, each, spread):
    size = vectors.shape[1]
    count = size // (each * spread)
    rows = width // count
    if spread > 1:
        vectors = jnp.broadcast_to(vectors[0:1, :], (8, size))
    tall = jnp.concatenate([vectors] * count, axis=0)
    row = lax.broadcasted_iota(I32, (8 * count, size), 0)
    col = lax.broadcasted_iota(I32, (8 * count, size), 1)
    line = row % 8
    wanted = spread * (row // 8) + (line if spread > 1 else 0)
    picked = jnp.where((col // each == wanted) & (line < lines), tall, 0.0).astype(BF)
    source = lax.broadcasted_iota(I32, (size, LANES), 0)
    lane = lax.broadcasted_iota(I32, (size, LANES), 1)
    move = jnp.where(source % each + first == lane, 1.0, 0.0).astype(BF)
    placed = nn(picked, move).astype(BF)
    target = lax.broadcasted_iota(I32, (width, 8 * count), 0)
    origin = lax.broadcasted_iota(I32, (width, 8 * count), 1)
    spot = (target // rows == origin // 8) & (target % rows == origin % 8)
    return nn(jnp.where(spot, 1.0, 0.0).astype(BF), placed)


def staged(count, *stages):
    for step in range(count + len(stages) - 1):
        for n, stage in enumerate(stages):
            if 0 <= step - n < count:
                stage(step - n)


def window_of(seg, real, i):
    begin = jnp.min(seg[2 * i : 2 * i + 1, :])
    end = jnp.max(seg[2 * i + 1 : 2 * i + 2, :])
    start = jnp.sum(jnp.where(seg < begin, 1, 0))
    stop = jnp.minimum(jnp.sum(jnp.where(seg <= end, 1, 0)), real)
    start = (start // LANES) * LANES
    need = stop - start
    kind = jnp.int32(0)
    size = jnp.int32(WINDOWS[0])
    for index, width in enumerate(WINDOWS[:-1]):
        kind = jnp.where(need > width, index + 1, kind)
        size = jnp.where(need > width, WINDOWS[index + 1], size)
    return jnp.minimum(start, SEQ - size), kind


def attention_kernel(
    core_ref, frames_ref, seg_ref, pad_ref, wm_ref, wo_ref, bm_ref, bo_ref,
    q_ref, k_ref, v_ref, augq_out, augk_out, mixed_ref, win_ref,
    x_s, w_s, q_s, k_s, v_s, vt_s, mt_s, lse_s, score_s, prob_s, mixed_s, augq_ref, augk_ref,
    small_s, seg_s, pad_s, sem,
):
    moves = Copies(sem)
    core = core_ref[0]
    lines = ds(core * (SEQ // LANES), SEQ // LANES, SEQ // LANES)
    moves.start("seg", (seg_ref.at[lines, :], seg_s), (pad_ref.at[lines, :], pad_s))
    moves.start("x", (frames_ref.at[ds(core * SEQ, SEQ, SEQ), :], x_s))
    for j in range(2):
        moves.start(("bias", j), *sides((bm_ref, bo_ref), small_s.at[j], j))
    moves.start(0, *sides((wm_ref, wo_ref), w_s.at[0], 0))
    lane = lane_row()
    moves.wait("seg")
    seg = seg_s[...]
    pad = pad_s[...]
    real = jnp.sum(pad)
    for i in range(BLOCKS):
        begin, kind = window_of(seg, real, i)
        win_ref[0, i] = begin
        win_ref[1, i] = kind
    for b in range(SEQ // LANES):
        rows = slice(b * LANES, (b + 1) * LANES)
        ids = jnp.broadcast_to(seg[b : b + 1, :].astype(F32), (LANES, LANES)).T
        shown = jnp.broadcast_to(pad[b : b + 1, :].astype(F32), (LANES, LANES)).T
        same = lane.astype(F32) == ids
        augk_ref[rows, :] = jnp.where(
            lane == 10, 1.0 - shown, jnp.where(same, 1.0, 0.0)
        ).astype(BF)
        off = jnp.where(same, 0.0, -BIG)
        augq_ref[rows, :] = jnp.where(
            lane < 10, off, jnp.where(lane == 10, -BIG, 0.0)
        ).astype(BF)
    moves.start("augk", (augk_ref, augk_out))
    moves.wait(("bias", 0), ("bias", 1), "x", 0)
    for j in (1, 2):
        moves.start(j, *sides((wm_ref, wo_ref), w_s.at[j], j))
    bias = [small_s[j] for j in range(2)]
    q_s[...] = ((nn(x_s[...], w_s[0]) + bias[0]) * (HD ** (-0.5) * LOG2E)).astype(BF)
    moves.start("q", (q_s, q_ref))
    moves.wait(1)
    k_s[...] = nn(x_s[...], w_s[1]).astype(BF)
    moves.start("k", (k_s, k_ref))
    moves.wait(2)
    v_s[...] = (nn(x_s[...], w_s[2]) + bias[1]).astype(BF)
    moves.start("v", (v_s, v_ref))
    vt_s[...] = v_s[...].T
    lse_s[...] = jnp.zeros_like(lse_s)
    heads = q_s.shape[1] // HD
    masks = half_masks()

    def block(i, carry):
        rows = ds(i * QB, QB, QB)
        begin = win_ref[0, i]
        kind = win_ref[1, i]

        def run(width):
            span = ds(begin, width, LANES)
            ones = jnp.ones((16, width), BF)

            def score(p):
                tile = slice(p * LANES, (p + 1) * LANES)
                right = jnp.concatenate([q_s[rows, tile], augq_ref[rows, :]], axis=1)
                key = k_s[span, tile]
                aug = augk_ref[span, :]
                left = [jnp.concatenate([key * mask, aug], axis=1) for mask in masks]
                score_s[p % 2, : 2 * width] = nt(jnp.concatenate(left, axis=0), right)

            def soften(p):
                for a in range(2):
                    here = slice(a * width, (a + 1) * width)
                    top = jnp.max(score_s[p % 2, here], axis=0, keepdims=True)
                    prob_s[p % 2, here] = jnp.exp2(score_s[p % 2, here] - top).astype(BF)
                    tops[2 * p + a] = top

            def mix(p):
                for a in range(2):
                    h = 2 * p + a
                    part = slice(h * HD, (h + 1) * HD)
                    left = jnp.concatenate([vt_s[part, span], ones], axis=0)
                    out = nn(left, prob_s[p % 2, a * width : (a + 1) * width])
                    total = out[HD : HD + 1, :]
                    mt_s[part, rows] = (out[:HD, :] * (1.0 / total)).astype(BF)
                    lse = tops.pop(h) + jnp.log2(total)
                    for piece in range(3):
                        lse_s[16 * (piece + 1) + h : 16 * (piece + 1) + h + 1, rows] = lse

            tops = {}
            for step in range(heads // 2 + 2):
                if step < heads // 2:
                    score(step)
                if step >= 2:
                    mix(step - 2)
                if 1 <= step <= heads // 2:
                    soften(step - 1)

        for index, width in enumerate(WINDOWS):
            pl.when(kind == index)(functools.partial(run, width))
        mixed_s[rows, :] = mt_s[:, rows].T
        return carry

    lax.fori_loop(0, BLOCKS, block, 0)
    moves.start("mixed", (mixed_s, mixed_ref))
    lse = lse_s[...].T
    high = lse.astype(BF).astype(F32)
    mid = (lse - high).astype(BF).astype(F32)
    piece = jnp.where(lane < 32, high, jnp.where(lane < 48, mid, lse - high - mid))
    augq_ref[...] = (augq_ref[...].astype(F32) - piece).astype(BF)
    moves.start("augq", (augq_ref, augq_out))
    moves.finish()


def attention_forward(core, frames, seg, pad, att_m, att_o, bias_m, bias_o):
    width = frames.shape[1]
    wide = ((SEQ, width), BF)
    thin = ((SEQ, LANES), BF)
    line = ((SEQ // LANES, LANES), I32)
    return call(
        attention_kernel,
        "attention_forward",
        [(SMEM, core)]
        + [(HBM, a) for a in (frames, seg, pad, att_m, att_o, bias_m, bias_o)],
        [(HBM, *wide)] * 3 + [(HBM, *thin)] * 2 + [(HBM, *wide), (SMEM, (2, BLOCKS), I32)],
        [
            wide, ((3, width, width), BF), wide, wide, wide, ((width, SEQ), BF),
            ((width, SEQ), BF), ((LANES, SEQ), F32), ((2, 2 * SEQ, QB), F32), ((2, 2 * SEQ, QB), BF),
            wide, thin, thin, ((2, 1, width), F32), line, line,
        ],
        19,
        cost(LONG),
    )


def gelu_pair(value):
    phi = 0.5 + 0.5 * lax.erf(value * 0.7071067811865476)
    low = value.astype(BF)
    density = jnp.exp2(low * low * BF(-0.5 * LOG2E)) * BF(0.3989422804014327)
    return (value * phi).astype(BF), phi.astype(BF) + low * density


def chunk_of(c, size):
    each = size // QB
    return c // each, ds(c % each * QB, QB, QB)


def middle_kernel(
    core_ref, frames_ref, cot_ref, mixed_ref, am_ref, ao_ref, fm_ref, fo_ref, hm_ref, ho_ref,
    augk_out, vec_out,
    n1_ref, inv_out, out_ref, gfn_ref, dm_ref, do_ref, sums_out, hsum_out,
    x_s, mixed_s, wo_s, w1_s, w2_s, cot_s, n1_s, inv_ref, low_s, g2_s, glow_s, slope_s, act_s,
    turn_s, stage_s, unit_s, ffn_s, bias_s, augk_ref, vec_ref, sum_ref, hsum_ref, sem,
):
    units = fm_ref.shape[2]
    moves = Copies(sem)
    own = ds(core_ref[0] * SEQ, SEQ, SEQ)
    moves.start("wo", *sides((am_ref, ao_ref), wo_s, 3))
    moves.start("in", (vec_out, vec_ref), (mixed_ref, mixed_s), (frames_ref.at[own, :], x_s))
    moves.start("bias", *sides((hm_ref, ho_ref), bias_s))
    moves.wait("wo", "in")
    moves.start("w1", *sides((fm_ref, fo_ref), w1_s, 0))
    sum_ref[...] = jnp.zeros_like(sum_ref)

    def project(r):
        rows = slice(r * QB, (r + 1) * QB)
        ffn_s[r % 2] = nt(mixed_s[rows, :], wo_s[...])

    def first_rows(r):
        rows = slice(r * QB, (r + 1) * QB)
        first = x_s[rows, :].astype(F32) + ffn_s[r % 2] + vec_ref[0:1, :]
        normed, inv_std = norm_rows(first)
        n1_s[rows, :] = normed
        inv_ref[rows, :] = jnp.broadcast_to(inv_std, (QB, LANES))
        low_s[rows, :] = (normed * vec_ref[1:2, :] + vec_ref[2:3, :]).astype(BF)

    staged(BLOCKS, project, first_rows)
    moves.wait("bias", "w1")
    moves.start("first", (n1_s, n1_ref), (inv_ref, inv_out))
    moves.start("cot", (cot_ref.at[own, :], cot_s), (augk_out, augk_ref))
    moves.start("w2", *sides((fm_ref, fo_ref), w2_s, 1))
    each = units // QB

    def up(c):
        unit_s[c % 2] = nn(low_s[...], w1_s[:, c * QB : (c + 1) * QB])

    def bend(c):
        spot = slice(c * QB, (c + 1) * QB)
        act, slope = gelu_pair(unit_s[c % 2] + bias_s[0:1, spot])
        act_s[:, c * QB : (c + 1) * QB] = act
        slope_s[:, c * QB : (c + 1) * QB] = slope

    staged(2 * each, up, bend)
    moves.wait("cot", "w2")

    def contract(r):
        rows = slice(r * QB, (r + 1) * QB)
        ffn_s[r % 2] = nt(act_s[rows, :], w2_s[...])

    def second(r):
        rows = slice(r * QB, (r + 1) * QB)
        first_norm = n1_s[rows, :] * vec_ref[1:2, :] + vec_ref[2:3, :]
        n2, inv_std = norm_rows(first_norm + ffn_s[r % 2] + vec_ref[3:4, :])
        valid = 1.0 - augk_ref[rows, 10:11].astype(F32)
        grad = cot_s[rows, :].astype(F32) * valid
        cot_s[rows, :] = (n2 * vec_ref[4:5, :] + vec_ref[5:6, :]).astype(BF)
        back = norm_back(grad, n2, inv_std, vec_ref[4:5, :])
        g2_s[rows, :] = back
        glow_s[rows, :] = back.astype(BF)
        sum_ref[3:4, :] += col_sum(back)
        sum_ref[4:5, :] += col_sum(grad * n2)
        sum_ref[5:6, :] += col_sum(grad)

    staged(BLOCKS, contract, second)
    moves.start("second", (cot_s, out_ref))
    size = stage_s.shape[2]
    stages = []

    def put(side, part, column, value):
        slot = len(stages) % 2
        if column == 0 and len(stages) >= 2:
            moves.wait(stages[-2])
        stage_s[slot, :, column : column + QB] = value
        if column + QB == size:
            stages.append(("part", side, part))
            moves.start(stages[-1], (stage_s.at[slot], (dm_ref, do_ref)[side].at[part]))

    turn_s[...] = glow_s[...].T
    for side in (1, 0):
        for c in range(each):
            at = side * units + c * QB
            part, column = divmod(c * QB, size)
            put(side, part, column, nn(turn_s[...], act_s[:, at : at + QB]).astype(BF))
    turn_s[...] = low_s[...].T
    order = [(side, c) for side in (1, 0) for c in range(each)]

    def columns(n):
        side, c = order[n]
        return slice(side * units + c * QB, side * units + (c + 1) * QB)

    def pull(n):
        unit_s[n % 2] = nn(glow_s[...], w2_s[:, columns(n)])

    def lean(n):
        grad = (unit_s[n % 2] * slope_s[:, columns(n)].astype(F32)).astype(BF)
        slope_s[:, columns(n)] = grad
        hsum_ref[0:1, columns(n)] = col_sum(grad.astype(F32))

    def push(n):
        side, c = order[n]
        part, column = divmod(c * QB, size)
        put(side, 3 + part, column, nn(turn_s[...], slope_s[:, columns(n)]).astype(BF))

    staged(2 * each, pull, lean, push)
    moves.start("sums", (sum_ref, sums_out), (hsum_ref, hsum_out))
    for r in range(BLOCKS):
        rows = slice(r * QB, (r + 1) * QB)
        g2_s[rows, :] += nt(slope_s[rows, :], w1_s[...])
        moves.start(("gfn", r), (g2_s.at[rows, :], gfn_ref.at[rows, :]))
    moves.finish()


def middle(core, frames, cot, mixed, att_m, att_o, ffw_m, ffw_o, hid_m, hid_o, augk, vectors):
    width = frames.shape[1]
    units = ffw_m.shape[2]
    wide = ((SEQ, width), BF)
    full = ((SEQ, width), F32)
    thin = ((SEQ, LANES), F32)
    inner = ((width, 2 * units), BF)
    outer = ((SEQ, 2 * units), BF)
    grads = ((6, width, units // 3), BF)
    ins = (frames, cot, mixed, att_m, att_o, ffw_m, ffw_o, hid_m, hid_o, augk, vectors)
    return call(
        middle_kernel,
        "middle",
        [(SMEM, core)] + [(HBM, a) for a in ins],
        [(HBM, *out) for out in (full, thin, wide, full, grads, grads)]
        + [(HBM, (8, width), F32), (HBM, (1, 2 * units), F32)],
        [
            wide, wide, ((width, width), BF), inner, inner, wide, full, thin, wide, full, wide,
            outer, outer, ((width, SEQ), BF), ((2, width, units // 3), BF), ((2, SEQ, QB), F32),
            ((2, QB, width), F32), ((1, 2 * units), F32), ((SEQ, LANES), BF),
            (vectors.shape, F32), ((8, width), F32), ((1, 2 * units), F32),
        ],
        36,
        cost(LONG),
    )


def norm_kernel(
    count, gfn_ref, n1_ref, inv_out, mixed_ref, am_ref, ao_ref, vec_out, sums_out, hsum_out,
    g1_ref, om_ref, oo_ref, gm_ref, augd_out,
    gfn_s, n1_s, inv_ref, mixed_s, wo_s, vec_ref,
    glow_s, glt_s, gm_s, augd_ref, om_s, oo_s, sum_ref, hsum_ref, sem,
):
    moves = Copies(sem)
    g1_s = gfn_s
    moves.start("sums", (sums_out, sum_ref), (hsum_out, hsum_ref))
    moves.start("vec", (vec_out, vec_ref), (inv_out, inv_ref))
    for r in range(BLOCKS):
        rows = slice(r * QB, (r + 1) * QB)
        moves.start(
            r, (gfn_ref.at[rows, :], gfn_s.at[rows, :]), (n1_ref.at[rows, :], n1_s.at[rows, :])
        )
        if r == 0:
            moves.wait("vec", "sums", 0)
    moves.start("wo", *sides((am_ref, ao_ref), wo_s, 3))
    moves.start("mixed", (mixed_ref, mixed_s))
    for r in range(BLOCKS):
        rows = slice(r * QB, (r + 1) * QB)
        if r > 0:
            moves.wait(r)
        grad = gfn_s[rows, :]
        n1 = n1_s[rows, :]
        back = norm_back(grad, n1, inv_ref[rows, 0:1], vec_ref[1:2, :])
        g1_s[rows, :] = back
        glow_s[rows, :] = back.astype(BF)
        sum_ref[0:1, :] += col_sum(back)
        sum_ref[1:2, :] += col_sum(grad * n1)
        sum_ref[2:3, :] += col_sum(grad)
    moves.start("g1", (g1_s, g1_ref))
    moves.wait("wo", "mixed")
    lane = lane_row()
    width = wo_s.shape[0]
    head = lax.broadcasted_iota(I32, (width, LANES), 0) // HD
    spot = lax.broadcasted_iota(I32, (width, LANES), 1)
    pick = jnp.where((spot == head + 16) | (spot == head + 32), 1.0, 0.0).astype(BF)
    for r in range(BLOCKS):
        rows = slice(r * QB, (r + 1) * QB)
        gm = nn(glow_s[rows, :], wo_s[...]).astype(BF)
        gm_s[rows, :] = gm
        both = gm.astype(F32) * mixed_s[rows, :].astype(F32)
        high = both.astype(BF)
        dots = nn(high, pick) + nn((both - high.astype(F32)).astype(BF), pick)
        dot_high = dots.astype(BF).astype(F32)
        augd_ref[rows, :] = (-jnp.where(lane < 32, dot_high, dots - dot_high)).astype(BF)
    moves.start("gm", (gm_s, gm_ref), (augd_ref, augd_out))
    glt_s[...] = glow_s[...].T
    size = om_s.shape[2]
    vectors = by_block(sum_ref[...], width, 0, 6, width // count, 1)
    units = hsum_ref.shape[1] // 2
    for side, target, result in ((1, oo_s, oo_ref), (0, om_s, om_ref)):
        cols = slice(side * 3 * size, (side + 1) * 3 * size)
        product = nn(glt_s[...], mixed_s[:, cols]).astype(BF)
        for part in range(3):
            target[part] = product[:, part * size : (part + 1) * size]
        hidden = hsum_ref[:, side * units : (side + 1) * units]
        hidden = by_block(hidden, width, LANES // 2, 2, units // count // 2, 2)
        target[3] = (vectors + hidden).astype(BF)
        moves.start(("o", side), (target, result))
    moves.finish()


def norm_backward(count, gfn, n1, inv, mixed, att_m, att_o, vectors, sums, hidden_sums):
    width = n1.shape[1]
    cols = att_m.shape[2]
    wide = ((SEQ, width), BF)
    full = ((SEQ, width), F32)
    thin = ((SEQ, LANES), BF)
    grads = ((4, width, cols // 3), BF)
    ins = (gfn, n1, inv, mixed, att_m, att_o, vectors, sums, hidden_sums)
    return call(
        functools.partial(norm_kernel, count),
        "norm_backward",
        [(HBM, a) for a in ins],
        [(HBM, *out) for out in (full, grads, grads, wide, thin)],
        [
            full, full, ((SEQ, LANES), F32), wide, ((width, width), BF), (vectors.shape, F32),
            wide, ((width, SEQ), BF), wide, thin, grads, grads, (sums.shape, F32),
            (hidden_sums.shape, F32),
        ],
        21,
        cost(LONG),
    )


def heads_kernel(
    first, count, shares, joins,
    win_ref, core_ref, q_ref, k_ref, v_ref, gm_ref, augq_out, augd_out, augk_out, frames_ref,
    *refs
):
    if joins:
        before_ref, refs = refs[0], refs[1:]
    dq_ref, dk_ref, dv_ref, refs = *refs[:3], refs[3:]
    grad_refs, refs = refs[: len(shares)], refs[len(shares) :]
    if not joins:
        bias_out, refs = refs[0], refs[1:]
    (
        q_s, k_s, v_s, gm_s, augq_ref, augd_ref, augk_ref, x_s, qt_s, kt_s, gt_s, dqt_s, dkt_s,
        dvt_s, xt_s, score_s, slope_s, prob_s, back_s, outs_s, grad_s, bias_ref, block_s, sem,
    ) = refs
    cols = dkt_s.shape[0]
    heads = cols // HD
    moves = Copies(sem)
    own = slice(first, first + cols)
    moves.start(
        "in",
        *[
            (ref.at[:, own], to)
            for ref, to in ((k_ref, k_s), (q_ref, q_s), (v_ref, v_s), (gm_ref, gm_s))
        ],
        (augq_out, augq_ref), (augd_out, augd_ref), (augk_out, augk_ref),
    )
    bias_ref[...] = jnp.zeros_like(bias_ref)
    dkt_s[...] = jnp.zeros_like(dkt_s)
    dvt_s[...] = jnp.zeros_like(dvt_s)
    moves.wait("in")
    moves.start("x", (frames_ref.at[ds(core_ref[0] * SEQ, SEQ, SEQ), :], x_s))
    if joins:
        moves.start("before", (before_ref, bias_ref.at[:, cols:]))
    kt_s[...] = k_s[...].T
    qt_s[...] = q_s[...].T
    gt_s[...] = gm_s[...].T
    masks = half_masks()
    lane = lane_row()

    def block(i, carry):
        rows = ds(i * QB, QB, QB)
        begin = win_ref[0, i]
        kind = win_ref[1, i]

        def run(width):
            span = ds(begin, width, LANES)

            def scores(p):
                tile = slice(p * LANES, (p + 1) * LANES)
                key = k_s[span, tile]
                value = v_s[span, tile]
                aug = augk_ref[span, :]
                keys = []
                values = []
                for a, mask in enumerate(masks):
                    at = first // HD + 2 * p + a
                    ones = jnp.where((lane == at + 16) | (lane == at + 32), 1.0, 0.0)
                    more = jnp.where(lane == at + 48, 1.0, ones).astype(BF)
                    ones = jnp.broadcast_to(ones.astype(BF), (width, LANES))
                    keys.append(jnp.concatenate([key * mask, aug + more], axis=1))
                    values.append(jnp.concatenate([value * mask, ones], axis=1))
                score_s[p % 2, : 2 * width] = nt(
                    jnp.concatenate(keys, axis=0),
                    jnp.concatenate([q_s[rows, tile], augq_ref[rows, :]], axis=1),
                )
                slope_s[p % 2, : 2 * width] = nt(
                    jnp.concatenate(values, axis=0),
                    jnp.concatenate([gm_s[rows, tile], augd_ref[rows, :]], axis=1),
                )

            def soften(p):
                probs = jnp.exp2(score_s[p % 2, : 2 * width])
                prob_s[p % 2, : 2 * width] = probs.astype(BF)
                back_s[p % 2, : 2 * width] = (probs * slope_s[p % 2, : 2 * width]).astype(BF)

            def collect(p):
                for a in range(2):
                    here = slice((2 * p + a) * HD, (2 * p + a + 1) * HD)
                    probs = prob_s[p % 2, a * width : (a + 1) * width]
                    back = back_s[p % 2, a * width : (a + 1) * width]
                    dvt_s[here, span] += nt(gt_s[here, rows], probs)
                    dkt_s[here, span] += nt(qt_s[here, rows], back)
                    dqt_s[here, rows] = nn(kt_s[here, span], back)

            for step in range(heads // 2 + 2):
                if step < heads // 2:
                    scores(step)
                if step >= 2:
                    collect(step - 2)
                if 1 <= step <= heads // 2:
                    soften(step - 1)

        for index, width in enumerate(WINDOWS):
            pl.when(kind == index)(functools.partial(run, width))
        return carry

    lax.fori_loop(0, BLOCKS, block, 0)
    outs_s[0] = (dqt_s[...] * HD ** (-0.5)).astype(BF).T
    outs_s[1] = (dkt_s[...] * LN2).astype(BF).T
    outs_s[2] = dvt_s[...].astype(BF).T
    moves.start("out", *[(outs_s.at[j], ref) for j, ref in enumerate((dq_ref, dk_ref, dv_ref))])
    moves.wait("x")
    xt_s[...] = x_s[...].T
    for j in range(3):
        grad_s[j] = nn(xt_s[...], outs_s[j]).astype(BF)
        at = 0
        for n, size in enumerate(shares):
            moves.start((j, n), (grad_s.at[j, :, at : at + size], grad_refs[n].at[j]))
            at += size
    if joins:
        moves.wait("before")
    bias_ref[0:1, :cols] = col_sum(outs_s[0].astype(F32))
    bias_ref[1:2, :cols] = col_sum(outs_s[2].astype(F32))
    width = grad_s.shape[1]
    if joins:
        side = bias_ref[...]
    else:
        side = bias_ref[:, shares[0] :]
        moves.start("bias", (bias_ref.at[:, : shares[0]], bias_out))
    block_s[...] = by_block(side, width, 0, 2, side.shape[1] // count, 1).astype(BF)
    moves.start("block", (block_s, grad_refs[-1].at[3, :, :LANES]))
    moves.finish()


def heads_backward(first, shares, count, win, core, q, k, v, gm, augq, augd, augk, frames, before=None):
    width = frames.shape[1]
    cols = sum(shares)
    joins = before is not None
    part = ((SEQ, cols), BF)
    turned = ((cols, SEQ), BF)
    thin = ((SEQ, LANES), BF)
    sums = ((cols, SEQ), F32)
    ins = (q, k, v, gm, augq, augd, augk, frames) + ((before,) if joins else ())
    grads = [(HBM, (3, width, size), BF) for size in shares[:-1]]
    grads.append((HBM, (4, width, shares[-1]), BF))
    biases = [] if joins else [(HBM, (8, shares[0]), F32)]
    total = cols + (before.shape[1] if joins else 0)
    return call(
        functools.partial(heads_kernel, first, count, shares, joins),
        "heads_backward",
        [(SMEM, win), (SMEM, core)] + [(HBM, a) for a in ins],
        [(HBM, *part)] * 3 + grads + biases,
        [
            part, part, part, part, thin, thin, thin, ((SEQ, width), BF),
            turned, turned, turned, sums, sums, sums, ((width, SEQ), BF),
            ((2, 2 * SEQ, QB), F32), ((2, 2 * SEQ, QB), F32),
            ((2, 2 * SEQ, QB), BF), ((2, 2 * SEQ, QB), BF),
            ((3, SEQ, cols), BF), ((3, width, cols), BF), ((8, total), F32), ((width, LANES), BF),
        ],
        24,
        cost(LONG),
    )


def input_kernel(
    qm_ref, km_ref, vm_ref, qo_ref, ko_ref, vo_ref, g1_ref, wm_ref, wo_ref, out_ref,
    w_s, left_s, g1_s, out_s, sem,
):
    cols = wm_ref.shape[2]
    moves = Copies(sem)
    for j in range(3):
        at = slice(2 * j * cols, 2 * (j + 1) * cols)
        moves.start(("w", j), *sides((wm_ref, wo_ref), w_s.at[:, at], j))
    places = []
    for ref in (qm_ref, qo_ref, km_ref, ko_ref, vm_ref, vo_ref):
        places.append((sum(r.shape[1] for _, r in places), ref))

    def fetch(r):
        rows = slice(r * QB, (r + 1) * QB)
        moves.start(
            r,
            (g1_ref.at[rows, :], g1_s.at[rows, :]),
            *[
                (ref.at[rows, :], left_s.at[rows, at : at + ref.shape[1]])
                for at, ref in places
            ],
        )

    fetch(0)
    moves.wait(*[("w", j) for j in range(3)])
    fetch(1)
    for r in range(BLOCKS):
        rows = slice(r * QB, (r + 1) * QB)
        moves.wait(r)
        if 0 < r < BLOCKS - 1:
            fetch(r + 1)
        out_s[rows, :] = (nt(left_s[rows, :], w_s[...]) + g1_s[rows, :]).astype(BF)
        moves.start(("out", r), (out_s.at[rows, :], out_ref.at[rows, :]))
    moves.finish()


def input_gradient(mine, other, g1, att_m, att_o):
    width = g1.shape[1]
    return call(
        input_kernel,
        "input_gradient",
        [(HBM, a) for a in (*mine, *other, g1, att_m, att_o)],
        [(HBM, (SEQ, width), BF)],
        [
            ((width, 3 * width), BF), ((SEQ, 3 * width), BF), ((SEQ, width), F32),
            ((SEQ, width), BF),
        ],
        6 + 8 * BLOCKS,
        cost(LONG),
        mib=26,
    )[0]


def join_kernel(
    core_ref, row_ref, partner_ref, grad_ref, theirs_ref, both_ref, out_ref,
    rows_s, low_s, high_s, sem,
):
    core = core_ref[0]
    moves = Copies(sem)
    size = SEQ // 2
    spots = [(half, slice(r * size, (r + 1) * size)) for half in range(2) for r in range(2)]

    def place(half, rows):
        return ds((core if half == 0 else 1 - core) * SEQ + rows.start, size, size)

    for half, rows in spots:
        ref = (grad_ref, theirs_ref)[half]
        moves.start((half, rows.start), (ref.at[rows, :], low_s.at[half, rows, :]))
    moves.start("rows", (row_ref, rows_s.at[0]), (partner_ref, rows_s.at[1]))
    for half, rows in spots:
        moves.wait((half, rows.start))
        high_s[half, rows, :] = low_s[half, rows, :].astype(F32)
        moves.start(
            ("out", half, rows.start),
            (high_s.at[half, rows, :], out_ref.at[place(half, rows), :]),
        )
    moves.wait("rows")
    for half, rows in spots:
        moves.start(
            ("both", half, rows.start),
            (rows_s.at[half, rows, :], both_ref.at[place(half, rows), :]),
        )
    moves.finish()


def join(core, row, partner, grad, theirs):
    both = (2 * SEQ, row.shape[1])
    return call(
        join_kernel,
        "join",
        [(SMEM, core)] + [(HBM, a) for a in (row, partner, grad, theirs)],
        [(HBM, both, BF), (HBM, both, F32)],
        [((2, *row.shape), BF), ((2, *row.shape), BF), ((2, *row.shape), F32)],
        14,
        cost(5),
        mib=20,
    )


def swap_cores(value):
    return lax.ppermute(value, "tensor", [(0, 1), (1, 0)])


def swap_bit(value, bit, count):
    return lax.ppermute(value, "dp", [(i, i ^ (1 << bit)) for i in range(count)])


class Reduction:
    def __init__(self, count, keep_from):
        self.count = count
        self.keep_from = keep_from
        self.memory = FREE
        self.bits = count.bit_length() - 1
        self.step = 0
        self.widths = [[], [], []]
        turn = min(self.bits, 3)
        self.orders = [
            [(n + s) % turn for s in range(turn)] + list(range(turn, self.bits)) for n in range(3)
        ]
        self.sources = [[], [], []]

    def columns(self, part):
        return sum(self.widths[part])

    def starts(self):
        return [sum(self.columns(p) for p in range(part)) for part in range(4)]

    def add(self, mine, other, leads, width, skips=(0, 0)):
        self.rows = mine.shape[1] // self.count
        every = list(range(self.bits - 1, -1, -1))
        pair = [
            value.reshape((value.shape[0],) + (2,) * self.bits + (self.rows, value.shape[2]))
            for value in (mine, other)
        ]
        for part, lead in enumerate(leads):
            for space, value, skip in zip((HBM, FREE), pair, skips):
                at = self.columns(part)
                self.sources[part].append((space, value, lead, every, skip, at, width))
            self.widths[part].append(width)

    def left(self, part, step):
        gone = self.orders[part][:step]
        return [b for b in range(self.bits - 1, -1, -1) if b not in gone]

    def jobs(self, final):
        step = self.bits if final else self.step + 1
        sent = [None if final else order[self.step] for order in self.orders]
        joined = len(set(sent)) == 1
        starts = self.starts()
        outs = []
        jobs = []
        for part in range(3):
            bits = self.left(part, step)
            dims = (2,) * len(bits) + (self.rows,)
            if joined:
                if part == 0:
                    memory = OUT if final or self.memory == OUT else HBM
                    outs.append((memory, dims + (starts[3],), F32 if final else BF))
                spot = (0, starts[part])
            else:
                memory = HBM if self.memory == FREE else OUT
                outs.append((memory, dims + (self.columns(part),), BF))
                spot = (part, 0)
            jobs.append((*spot, bits, sent[part], self.sources[part], self.widths[part]))
        if self.step >= self.keep_from and not final:
            for part in range(3):
                bits = self.left(part, step)
                dims = (2,) * len(bits) + (self.rows, self.columns(part))
                outs.append((HBM if self.memory == FREE else OUT, dims, F32))
                jobs.append(
                    (len(outs) - 1, 0, bits, None, self.sources[part], self.widths[part])
                )
        return outs, jobs

    def launch(self, values):
        turn = [order[self.step] for order in self.orders]
        kept = self.step >= self.keep_from
        sends = values[:-3] if kept else values
        if len(sends) == 1:
            got = swap_bit(sends[0], turn[0], self.count)
            moved = [(got, at) for at in self.starts()[:3]]
        else:
            moved = [(swap_bit(s, b, self.count), 0) for s, b in zip(sends, turn)]
        self.step += 1
        for part, (value, skip) in enumerate(moved):
            bits = self.left(part, self.step)
            columns = self.columns(part)
            if kept:
                own = values[part - 3]
                self.sources[part] = [(self.memory, own, None, bits, 0, 0, columns)]
            self.sources[part].append((self.memory, value, None, bits, skip, 0, columns))


def fold_kernel(jobs, spaces, spans, final, extra, place_ref, *refs):
    ins, refs = refs[: len(spaces)], refs[len(spaces) :]
    if extra:
        early_ref, refs = refs[0], refs[1:]
    results, refs = refs[: len(spans)], refs[len(spans) :]
    if final:
        squares_ref, refs = refs[0], refs[1:]
    moves = Copies(refs[-1])
    scratch = list(refs[:-1])
    outs = [ref if space == OUT else scratch.pop() for space, ref in zip(spans, results)]
    values = []
    for number, (output, column, bits, sent, sources, widths) in enumerate(jobs):
        found = []
        for which, lead, own_bits, skip, at, width in sources:
            index = [] if lead is None else [lead]
            for bit in own_bits:
                if bit in bits:
                    index.append(slice(None))
                else:
                    index.append(1 - place_ref[bit] if bit == sent else place_ref[bit])
            if spaces[which] != OUT:
                target = scratch.pop(0)
                index += [slice(None), slice(skip, skip + width)]
                moves.start((number, len(found)), (ins[which].at[tuple(index)], target))
                found.append((target, (), 0))
            else:
                found.append((ins[which], tuple(index), skip))
        values.append(found)
    squares = jnp.float32(0.0)
    for number, (output, column, bits, sent, sources, widths) in enumerate(jobs):
        total = [None for _ in widths]
        starts = [sum(widths[:n]) for n in range(len(widths))]
        for n, (which, lead, own_bits, skip, first, size) in enumerate(sources):
            if spaces[which] != OUT:
                moves.wait((number, n))
            ref, index, skip = values[number][n]
            for spot, (at, width) in enumerate(zip(starts, widths)):
                if first <= at < first + size:
                    cols = slice(skip + at - first, skip + at - first + width)
                    value = ref[(*index, Ellipsis, cols)].astype(F32)
                    total[spot] = value if total[spot] is None else total[spot] + value
        for at, width, value in zip(starts, widths, total):
            outs[output][..., column + at : column + at + width] = value.astype(
                outs[output].dtype
            )
            if final:
                squares = squares + jnp.sum(value * value)
                if number == 0 and final == "shared" and at == starts[-1]:
                    lane = lax.broadcasted_iota(I32, value.shape, 1)
                    line = lax.broadcasted_iota(I32, value.shape, 0)
                    both = jnp.where((lane < LANES // 2) & (line < 6), value, 0.0)
                    squares = squares - 0.5 * jnp.sum(both * both)
        if spans[output] != OUT:
            if output not in [job[0] for job in jobs[number + 1 :]]:
                moves.start(("out", output), (outs[output], results[output]))
    if extra:
        squares_ref[...] = jnp.full(squares_ref.shape, squares + early_ref[0, 0], F32)
    elif final:
        squares_ref[0, 0] = squares
    moves.finish()


def fold(place, reductions, final=False, extra=None):
    arrays = []
    outs = []
    jobs = []
    counts = []
    for reduction in reductions:
        shapes, todo = reduction.jobs(final)
        for output, column, bits, sent, sources, widths in todo:
            listed = []
            for space, array, *rest in sources:
                known = [n for n, (_, a) in enumerate(arrays) if a is array]
                if not known:
                    arrays.append((space, array))
                listed.append((known[0] if known else len(arrays) - 1, *rest))
            jobs.append((len(outs) + output, column, bits, sent, listed, widths))
        outs += shapes
        counts.append(len(shapes))
    scratch = []
    for output, column, bits, sent, sources, widths in jobs:
        for which, lead, own_bits, skip, at, width in sources:
            if arrays[which][0] != OUT:
                array = arrays[which][1]
                scratch.append(((2,) * len(bits) + (array.shape[-2], width), array.dtype))
    copies = len(scratch)
    for space, dims, dtype in reversed(outs):
        if space != OUT:
            scratch.append((dims, dtype))
            copies += 1

    def volume(dims):
        return 4 * functools.reduce(lambda a, b: a * b, dims)

    last = []
    if extra:
        last = [(OUT, (2 * extra[1], LANES), F32)]
    elif final:
        last = [(SMEM, (1, 1), F32)]
    size = sum(volume(dims) for dims, _ in scratch)
    size += sum(volume(a.shape) for space, a in arrays if space == OUT)
    size += sum(volume(dims) for space, dims, _ in outs if space == OUT)
    res = call(
        functools.partial(
            fold_kernel, jobs, [space for space, _ in arrays], [out[0] for out in outs], final,
            bool(extra),
        ),
        "fold",
        [(SMEM, place)] + arrays + ([(SMEM, extra[0])] if extra else []),
        outs + last,
        scratch,
        copies,
        cost(2),
        mib=4 + size // 2**20,
    )
    grouped = []
    at = 0
    for n in counts:
        grouped.append(list(res[at : at + n]))
        at += n
    return grouped + ([res[-1]] if final else [])


def tie(value, *others):
    return lax.optimization_barrier((value, others))[0]


def advance(place, reductions, after):
    values = fold(tie(place, after), reductions)
    values = lax.optimization_barrier(values)
    for reduction, value in zip(reductions, values):
        reduction.launch(value)
    return values


def update_kernel(
    squares_ref, ffn_ref, qkv_ref, aw, am, av, fw, fm, fv, *refs
):
    small, outs, norm_ref = refs[:9], refs[9:-2], refs[-2]
    norm = jnp.sqrt(col_sum(squares_ref[...])[:, 0:1])
    norm_ref[...] = norm
    factor = jnp.minimum(1.0, 1.0 / (norm + 1e-06))

    def adam(grad, weight, first, second, results, index, rate, decay):
        clipped = grad * factor
        first_new = 0.9 * first[index] + 0.1 * clipped
        second_new = 0.999 * second[index] + 0.001 * clipped * clipped
        mean_hat = first_new / (1.0 - 0.9**STEP)
        var_hat = second_new / (1.0 - 0.999**STEP)
        old = weight[index].astype(F32)
        results[0][index] = first_new
        results[1][index] = second_new
        results[2][index] = old - rate * (mean_hat / (jnp.sqrt(var_hat) + 1e-08) + decay * old)

    every = slice(None)
    each = fw.shape[2] // 3
    wide = aw.shape[2]
    rest = wide // 3
    ends = [small[3 * n].shape[1] for n in range(3)]
    here = 2 * each + rest
    lines = ffn_ref[0:6, here : here + ends[2]]
    half = ends[1] // 2
    spot = here + LANES // 2
    hidden = jnp.concatenate(
        [ffn_ref[0:1, spot : spot + half], ffn_ref[1:2, spot : spot + half]], axis=1
    )
    tails = (qkv_ref[0:2, wide : wide + ends[0]], hidden, lines)
    for j in range(3):
        at = 0 if j == 0 else LANES + j * wide
        adam(qkv_ref[:, at : at + wide], aw, am, av, outs[0:3], (j,), 0.05, 0.01)
        at = 0 if j == 0 else LANES + j * here
        cols = slice(j * rest, (j + 1) * rest)
        grad = ffn_ref[:, at + 2 * each : at + here]
        adam(grad, aw, am, av, outs[0:3], (3, every, cols), 0.05, 0.01)
        cols = slice(j * each, (j + 1) * each)
        grad = ffn_ref[:, at + each : at + 2 * each]
        adam(grad, fw, fm, fv, outs[3:6], (0, every, cols), 0.05, 0.01)
        adam(ffn_ref[:, at : at + each], fw, fm, fv, outs[3:6], (1, every, cols), 0.05, 0.01)
    for n in range(3):
        weight, first, second = small[3 * n : 3 * n + 3]
        results = outs[6 + 3 * n : 9 + 3 * n]
        adam(tails[n], weight, first, second, results, (every, every), 0.5, 0.0)


def update(squares, ffn, qkv, attention, feedforward, small):
    arrays = [squares, ffn, qkv, *attention, *feedforward]
    outs = [attention[1].shape] * 3 + [feedforward[1].shape] * 3
    for group in small:
        arrays += group
        outs += [group[0].shape] * 3
    return call(
        update_kernel,
        "update",
        [(OUT, a) for a in arrays],
        [(OUT, dims, F32) for dims in outs] + [(OUT, (1, 1), F32)],
        [],
        0,
        cost(2),
        mib=16,
    )


def local(
    frames,
    cotangent,
    segment_ids,
    pad_mask,
    attention_weight,
    feedforward_weight,
    head_bias,
    hidden_bias,
    norm_vectors,
    attention_first,
    attention_second,
    feedforward_first,
    feedforward_second,
    head_first,
    head_second,
    hidden_first,
    hidden_second,
    vector_first,
    vector_second,
):
    width = frames.shape[1]
    cols = attention_weight.shape[2]
    units = feedforward_weight.shape[2]
    count = lax.axis_size("dp")
    bits = count.bit_length() - 1
    rows = width // count
    core = lax.axis_index("tensor")
    dp_index = lax.axis_index("dp")
    core_ref = core.reshape(1).astype(I32)
    place = jnp.stack([(dp_index >> b) & 1 for b in range(bits)]).astype(I32)

    att_m, ffw_m, hid_m = attention_weight, feedforward_weight, hidden_bias
    att_o = swap_cores(att_m)
    head_o = swap_cores(head_bias)
    hid_o = swap_cores(hid_m)
    ffw_o = swap_cores(tie(ffw_m, att_o, head_o, hid_o))
    lines = (frames.shape[0] // LANES, LANES)

    q, k, v, augq, augk, mixed, win = attention_forward(
        core_ref, frames, segment_ids.reshape(lines), pad_mask.reshape(lines), att_m, att_o,
        head_bias, head_o,
    )
    n1, inv, out_row, gfn, ffn_m, ffn_o, sums, hidden_sums = middle(
        core_ref, frames, cotangent, mixed, att_m, att_o, ffw_m, ffw_o, hid_m, hid_o, augk,
        norm_vectors,
    )
    ffn_o = swap_cores(ffn_o)
    out_other = swap_cores(out_row)
    g1, om, oo, gm, augd = norm_backward(
        count, gfn, n1, inv, mixed, att_m, att_o, norm_vectors, sums, hidden_sums
    )
    oo = swap_cores(oo)
    ffn = Reduction(count, 2)
    ffn.add(ffn_m, ffn_o, (0, 1, 2), units // 3)
    ffn.add(ffn_m, ffn_o, (3, 4, 5), units // 3)
    ffn.add(om, oo, (0, 1, 2), cols // 3)
    ffn.add(om, oo, (3,), LANES)
    sent = advance(place, [ffn], gm)

    split = cols - LANES
    back = functools.partial(
        heads_backward, count=count, win=win, core=core_ref, q=q, k=k, v=v, augq=augq, augd=augd,
        augk=augk, frames=frames,
    )
    *other, last_grad, other_grad, last_bias = back(
        split, (LANES, cols), gm=tie(gm, sent)
    )
    other_grad = swap_cores(other_grad)
    sent = advance(place, [ffn], other[0])
    *mine, mine_grad = back(0, (split,), gm=tie(gm, sent), before=last_bias)
    qkv = Reduction(count, 1)
    qkv.add(mine_grad, other_grad, (0, 1, 2), split)
    qkv.add(last_grad, other_grad, (0, 1, 2), LANES, (0, split))
    qkv.add(mine_grad, other_grad, (3,), LANES)
    for reduction in (qkv, ffn):
        reduction.memory = OUT
    sent = advance(place, [qkv, ffn], mine_grad)
    grad_row = input_gradient(mine, other, tie(g1, sent), att_m, att_o)
    sent = advance(place, [r for r in (qkv, ffn) if r.step < bits], grad_row)
    grad_row = tie(grad_row, sent)
    grad_other = swap_cores(grad_row)
    dp_late = tie(dp_index, sent)

    def own(value, size, axis):
        return lax.dynamic_slice_in_dim(value, dp_late * size, size, axis)

    olds = (
        own(att_m, rows, 1), own(ffw_m, rows, 1),
        own(head_bias.reshape(2, cols), cols // count, 1),
        own(hidden_bias, units // count, 1), own(norm_vectors, rows, 1),
    )
    sent = advance(place, [r for r in (qkv, ffn) if r.step < bits], (sent, olds))
    layer_output, frame_grads = join(
        core_ref, out_row, out_other, tie(grad_row, sent), grad_other
    )
    sent = (sent, frame_grads)
    while qkv.step < bits:
        sent = advance(place, [r for r in (qkv, ffn) if r.step < bits], sent)
    old_att, old_ffw, old_head, old_hidden, old_vectors = olds
    while ffn.step < bits:
        sent = advance(place, [ffn], sent)
    (ffn_sum,), early = fold(tie(place, sent), [ffn], final="shared")
    (qkv_sum,), squares = fold(tie(place, early), [qkv], final="own", extra=(early, count))
    squares = lax.all_to_all(squares, ("dp", "tensor"), 0, 0, tiled=True)

    def flat(value):
        return value.reshape(-1, value.shape[-1])

    new = update(
        squares, ffn_sum, qkv_sum,
        (old_att, attention_first, attention_second),
        (old_ffw, feedforward_first, feedforward_second),
        (
            (old_head, flat(head_first), flat(head_second)),
            (old_hidden, hidden_first, hidden_second),
            (old_vectors, vector_first, vector_second),
        ),
    )
    return (
        layer_output,
        frame_grads,
        new[15].reshape(()),
        *new[:6],
        *[value.reshape(head_first.shape) for value in new[6:9]],
        *new[9:15],
    )


def solution(mesh):
    weight_spec = P(None, None, "tensor")
    shard = P(None, "dp", "tensor")
    head = P(None, "tensor", "dp")
    hidden = P("tensor", "dp")
    vector = P(None, "dp")
    row = P("dp", None)
    return jax.shard_map(
        local,
        mesh=mesh,
        in_specs=(
            row, row, P("dp"), P("dp"),
            weight_spec, weight_spec,
            P(None, "tensor", None), P("tensor", None), P(),
            shard, shard, shard, shard,
            head, head, hidden, hidden, vector, vector,
        ),
        out_specs=(
            row, row, P(),
            shard, shard, shard, shard, shard, shard,
            head, head, head, hidden, hidden, hidden, vector, vector, vector,
        ),
        check_vma=False,
    )
```

```python
import functools

import jax
import jax.numpy as jnp
from jax import lax
from jax.experimental import pallas as pl
from jax.experimental.pallas import tpu as pltpu
from jax.sharding import PartitionSpec as P

HD = 64
SEQ = 1024
STEP = 10
LANES = 128
QB = 256
BLOCKS = SEQ // QB
BIG = 1e30
LOG2E = 1.4426950408889634
LN2 = 0.6931471805599453
WINDOWS = (384, 512, 640, 768, 1024)
BF = jnp.bfloat16
F32 = jnp.float32
I32 = jnp.int32


def nn(a, b):
    return jnp.dot(a, b, preferred_element_type=F32)


def nt(a, b):
    return lax.dot_general(a, b, (((1,), (1,)), ((), ())), preferred_element_type=F32)


def ds(start, size, step):
    return pl.ds(pl.multiple_of(start, step), size)


def shape(dims, dtype):
    return jax.ShapeDtypeStruct(dims, dtype)


LONG = 100


def cost(micros):
    return pl.CostEstimate(flops=int(1.1e9 * micros), bytes_accessed=2**20, transcendentals=0)


SMEM = "smem"
HBM = "hbm"
FREE = "free"
OUT = "out"
SPACES = {SMEM: pltpu.SMEM, HBM: pltpu.HBM, FREE: pl.ANY, OUT: pltpu.VMEM}
WHOLE = 63


def call(kernel, name, ins, outs, scratch, copies, estimate, mib=WHOLE):
    args = [
        pltpu.with_memory_space_constraint(array, pltpu.HBM) if space == HBM else array
        for space, array in ins
    ]
    return pl.pallas_call(
        kernel,
        out_shape=[
            pltpu.HBM(dims, dtype) if space == HBM else shape(dims, dtype)
            for space, dims, dtype in outs
        ],
        in_specs=[pl.BlockSpec(memory_space=SPACES[space]) for space, _ in ins],
        out_specs=[pl.BlockSpec(memory_space=SPACES[space]) for space, _, _ in outs],
        scratch_shapes=[pltpu.VMEM(dims, dtype) for dims, dtype in scratch]
        + [pltpu.SemaphoreType.DMA((max(copies, 1),))],
        compiler_params=pltpu.CompilerParams(vmem_limit_bytes=mib * 2**20),
        cost_estimate=estimate,
        name=name,
    )(*args)


class Copies:
    def __init__(self, sem):
        self.sem = sem
        self.used = 0
        self.pending = {}

    def start(self, name, *pairs):
        made = []
        for source, target in pairs:
            made.append(pltpu.make_async_copy(source, target, self.sem.at[self.used]))
            made[-1].start()
            self.used += 1
        self.pending[name] = made

    def wait(self, *names):
        for name in names:
            for copy in self.pending.pop(name):
                copy.wait()

    def finish(self):
        self.wait(*list(self.pending))


def lane_row():
    return lax.broadcasted_iota(I32, (1, LANES), 1)


def half_masks():
    low = jnp.where(lane_row() < HD, 1.0, 0.0)
    return (low.astype(BF), (1.0 - low).astype(BF))


def norm_rows(value):
    center = value - jnp.mean(value, axis=-1, keepdims=True)
    inv_std = lax.rsqrt(jnp.mean(center * center, axis=-1, keepdims=True) + 1e-05)
    return center * inv_std, inv_std


def norm_back(grad, normed, inv_std, gain):
    scaled = grad * gain
    mean_one = jnp.mean(scaled, axis=-1, keepdims=True)
    mean_two = jnp.mean(scaled * normed, axis=-1, keepdims=True)
    return inv_std * (scaled - mean_one - normed * mean_two)


def col_sum(value):
    return jnp.sum(value, axis=0, keepdims=True)


def sides(refs, target, index=None):
    size = target.shape[-1] // len(refs)
    picked = [ref if index is None else ref.at[index] for ref in refs]
    return [
        (ref, target.at[:, n * size : (n + 1) * size]) for n, ref in enumerate(picked)
    ]


def by_block(vectors, width, first, lines, each, spread):
    size = vectors.shape[1]
    count = size // (each * spread)
    rows = width // count
    if spread > 1:
        vectors = jnp.broadcast_to(vectors[0:1, :], (8, size))
    tall = jnp.concatenate([vectors] * count, axis=0)
    row = lax.broadcasted_iota(I32, (8 * count, size), 0)
    col = lax.broadcasted_iota(I32, (8 * count, size), 1)
    line = row % 8
    wanted = spread * (row // 8) + (line if spread > 1 else 0)
    picked = jnp.where((col // each == wanted) & (line < lines), tall, 0.0).astype(BF)
    source = lax.broadcasted_iota(I32, (size, LANES), 0)
    lane = lax.broadcasted_iota(I32, (size, LANES), 1)
    move = jnp.where(source % each + first == lane, 1.0, 0.0).astype(BF)
    placed = nn(picked, move).astype(BF)
    target = lax.broadcasted_iota(I32, (width, 8 * count), 0)
    origin = lax.broadcasted_iota(I32, (width, 8 * count), 1)
    spot = (target // rows == origin // 8) & (target % rows == origin % 8)
    return nn(jnp.where(spot, 1.0, 0.0).astype(BF), placed)


def staged(count, *stages):
    for step in range(count + len(stages) - 1):
        for n, stage in enumerate(stages):
            if 0 <= step - n < count:
                stage(step - n)


def window_of(seg, real, i):
    begin = jnp.min(seg[2 * i : 2 * i + 1, :])
    end = jnp.max(seg[2 * i + 1 : 2 * i + 2, :])
    start = jnp.sum(jnp.where(seg < begin, 1, 0))
    stop = jnp.minimum(jnp.sum(jnp.where(seg <= end, 1, 0)), real)
    start = (start // LANES) * LANES
    need = stop - start
    kind = jnp.int32(0)
    size = jnp.int32(WINDOWS[0])
    for index, width in enumerate(WINDOWS[:-1]):
        kind = jnp.where(need > width, index + 1, kind)
        size = jnp.where(need > width, WINDOWS[index + 1], size)
    return jnp.minimum(start, SEQ - size), kind


def attention_kernel(
    core_ref, frames_ref, seg_ref, pad_ref, wm_ref, wo_ref, bm_ref, bo_ref,
    q_ref, k_ref, v_ref, augq_out, augk_out, mixed_ref, win_ref,
    x_s, w_s, q_s, k_s, v_s, vt_s, mt_s, lse_s, score_s, prob_s, mixed_s, augq_ref, augk_ref,
    small_s, seg_s, pad_s, sem,
):
    moves = Copies(sem)
    core = core_ref[0]
    lines = ds(core * (SEQ // LANES), SEQ // LANES, SEQ // LANES)
    moves.start("seg", (seg_ref.at[lines, :], seg_s), (pad_ref.at[lines, :], pad_s))
    moves.start("x", (frames_ref.at[ds(core * SEQ, SEQ, SEQ), :], x_s))
    for j in range(2):
        moves.start(("bias", j), *sides((bm_ref, bo_ref), small_s.at[j], j))
    moves.start(0, *sides((wm_ref, wo_ref), w_s.at[0], 0))
    lane = lane_row()
    moves.wait("seg")
    seg = seg_s[...]
    pad = pad_s[...]
    real = jnp.sum(pad)
    for i in range(BLOCKS):
        begin, kind = window_of(seg, real, i)
        win_ref[0, i] = begin
        win_ref[1, i] = kind
    for b in range(SEQ // LANES):
        rows = slice(b * LANES, (b + 1) * LANES)
        ids = jnp.broadcast_to(seg[b : b + 1, :].astype(F32), (LANES, LANES)).T
        shown = jnp.broadcast_to(pad[b : b + 1, :].astype(F32), (LANES, LANES)).T
        same = lane.astype(F32) == ids
        augk_ref[rows, :] = jnp.where(
            lane == 10, 1.0 - shown, jnp.where(same, 1.0, 0.0)
        ).astype(BF)
        off = jnp.where(same, 0.0, -BIG)
        augq_ref[rows, :] = jnp.where(
            lane < 10, off, jnp.where(lane == 10, -BIG, 0.0)
        ).astype(BF)
    moves.start("augk", (augk_ref, augk_out))
    moves.wait(("bias", 0), ("bias", 1), "x", 0)
    for j in (1, 2):
        moves.start(j, *sides((wm_ref, wo_ref), w_s.at[j], j))
    bias = [small_s[j] for j in range(2)]
    q_s[...] = ((nn(x_s[...], w_s[0]) + bias[0]) * (HD ** (-0.5) * LOG2E)).astype(BF)
    moves.start("q", (q_s, q_ref))
    moves.wait(1)
    k_s[...] = nn(x_s[...], w_s[1]).astype(BF)
    moves.start("k", (k_s, k_ref))
    moves.wait(2)
    v_s[...] = (nn(x_s[...], w_s[2]) + bias[1]).astype(BF)
    moves.start("v", (v_s, v_ref))
    vt_s[...] = v_s[...].T
    lse_s[...] = jnp.zeros_like(lse_s)
    heads = q_s.shape[1] // HD
    masks = half_masks()

    def block(i, carry):
        rows = ds(i * QB, QB, QB)
        begin = win_ref[0, i]
        kind = win_ref[1, i]

        def run(width):
            span = ds(begin, width, LANES)
            ones = jnp.ones((16, width), BF)

            def score(p):
                tile = slice(p * LANES, (p + 1) * LANES)
                right = jnp.concatenate([q_s[rows, tile], augq_ref[rows, :]], axis=1)
                key = k_s[span, tile]
                aug = augk_ref[span, :]
                left = [jnp.concatenate([key * mask, aug], axis=1) for mask in masks]
                score_s[p % 2, : 2 * width] = nt(jnp.concatenate(left, axis=0), right)

            def soften(p):
                for a in range(2):
                    here = slice(a * width, (a + 1) * width)
                    top = jnp.max(score_s[p % 2, here], axis=0, keepdims=True)
                    prob_s[p % 2, here] = jnp.exp2(score_s[p % 2, here] - top).astype(BF)
                    tops[2 * p + a] = top

            def mix(p):
                for a in range(2):
                    h = 2 * p + a
                    part = slice(h * HD, (h + 1) * HD)
                    left = jnp.concatenate([vt_s[part, span], ones], axis=0)
                    out = nn(left, prob_s[p % 2, a * width : (a + 1) * width])
                    total = out[HD : HD + 1, :]
                    mt_s[part, rows] = (out[:HD, :] * (1.0 / total)).astype(BF)
                    lse = tops.pop(h) + jnp.log2(total)
                    for piece in range(3):
                        lse_s[16 * (piece + 1) + h : 16 * (piece + 1) + h + 1, rows] = lse

            tops = {}
            for step in range(heads // 2 + 2):
                if step < heads // 2:
                    score(step)
                if step >= 2:
                    mix(step - 2)
                if 1 <= step <= heads // 2:
                    soften(step - 1)

        for index, width in enumerate(WINDOWS):
            pl.when(kind == index)(functools.partial(run, width))
        mixed_s[rows, :] = mt_s[:, rows].T
        return carry

    lax.fori_loop(0, BLOCKS, block, 0)
    moves.start("mixed", (mixed_s, mixed_ref))
    lse = lse_s[...].T
    high = lse.astype(BF).astype(F32)
    mid = (lse - high).astype(BF).astype(F32)
    piece = jnp.where(lane < 32, high, jnp.where(lane < 48, mid, lse - high - mid))
    augq_ref[...] = (augq_ref[...].astype(F32) - piece).astype(BF)
    moves.start("augq", (augq_ref, augq_out))
    moves.finish()


def attention_forward(core, frames, seg, pad, att_m, att_o, bias_m, bias_o):
    width = frames.shape[1]
    wide = ((SEQ, width), BF)
    thin = ((SEQ, LANES), BF)
    line = ((SEQ // LANES, LANES), I32)
    return call(
        attention_kernel,
        "attention_forward",
        [(SMEM, core)]
        + [(HBM, a) for a in (frames, seg, pad, att_m, att_o, bias_m, bias_o)],
        [(HBM, *wide)] * 3 + [(HBM, *thin)] * 2 + [(HBM, *wide), (SMEM, (2, BLOCKS), I32)],
        [
            wide, ((3, width, width), BF), wide, wide, wide, ((width, SEQ), BF),
            ((width, SEQ), BF), ((LANES, SEQ), F32), ((2, 2 * SEQ, QB), F32), ((2, 2 * SEQ, QB), BF),
            wide, thin, thin, ((2, 1, width), F32), line, line,
        ],
        19,
        cost(LONG),
    )


def gelu_pair(value):
    phi = 0.5 + 0.5 * lax.erf(value * 0.7071067811865476)
    low = value.astype(BF)
    density = jnp.exp2(low * low * BF(-0.5 * LOG2E)) * BF(0.3989422804014327)
    return (value * phi).astype(BF), phi.astype(BF) + low * density


def chunk_of(c, size):
    each = size // QB
    return c // each, ds(c % each * QB, QB, QB)


def middle_kernel(
    core_ref, frames_ref, cot_ref, mixed_ref, am_ref, ao_ref, fm_ref, fo_ref, hm_ref, ho_ref,
    augk_out, vec_out,
    n1_ref, inv_out, out_ref, gfn_ref, dm_ref, do_ref, sums_out, hsum_out,
    x_s, mixed_s, wo_s, w1_s, w2_s, cot_s, n1_s, inv_ref, low_s, g2_s, glow_s, slope_s, act_s,
    turn_s, stage_s, unit_s, ffn_s, bias_s, augk_ref, vec_ref, sum_ref, hsum_ref, sem,
):
    units = fm_ref.shape[2]
    moves = Copies(sem)
    own = ds(core_ref[0] * SEQ, SEQ, SEQ)
    moves.start("wo", *sides((am_ref, ao_ref), wo_s, 3))
    moves.start("in", (vec_out, vec_ref), (mixed_ref, mixed_s), (frames_ref.at[own, :], x_s))
    moves.start("bias", *sides((hm_ref, ho_ref), bias_s))
    halves = sides((fm_ref, fo_ref), w1_s, 0)
    moves.wait("wo", "in")
    moves.start("w1", halves[0])
    sum_ref[...] = jnp.zeros_like(sum_ref)

    def project(r):
        rows = slice(r * QB, (r + 1) * QB)
        ffn_s[r % 2] = nt(mixed_s[rows, :], wo_s[...])

    def first_rows(r):
        rows = slice(r * QB, (r + 1) * QB)
        first = x_s[rows, :].astype(F32) + ffn_s[r % 2] + vec_ref[0:1, :]
        normed, inv_std = norm_rows(first)
        n1_s[rows, :] = normed
        inv_ref[rows, :] = jnp.broadcast_to(inv_std, (QB, LANES))
        low_s[rows, :] = (normed * vec_ref[1:2, :] + vec_ref[2:3, :]).astype(BF)

    staged(BLOCKS, project, first_rows)
    moves.wait("bias", "w1")
    moves.start("w1", halves[1])
    each = units // QB

    def up(c):
        if c == each:
            moves.wait("w1")
            moves.start("first", (n1_s, n1_ref), (inv_ref, inv_out))
            moves.start("cot", (cot_ref.at[own, :], cot_s), (augk_out, augk_ref))
            moves.start("w2", *sides((fm_ref, fo_ref), w2_s, 1))
        unit_s[c % 2] = nn(low_s[...], w1_s[:, c * QB : (c + 1) * QB])

    def bend(c):
        spot = slice(c * QB, (c + 1) * QB)
        act, slope = gelu_pair(unit_s[c % 2] + bias_s[0:1, spot])
        act_s[:, c * QB : (c + 1) * QB] = act
        slope_s[:, c * QB : (c + 1) * QB] = slope

    staged(2 * each, up, bend)
    moves.wait("cot", "w2")

    def contract(r):
        rows = slice(r * QB, (r + 1) * QB)
        ffn_s[r % 2] = nt(act_s[rows, :], w2_s[...])

    def second(r):
        rows = slice(r * QB, (r + 1) * QB)
        first_norm = n1_s[rows, :] * vec_ref[1:2, :] + vec_ref[2:3, :]
        n2, inv_std = norm_rows(first_norm + ffn_s[r % 2] + vec_ref[3:4, :])
        valid = 1.0 - augk_ref[rows, 10:11].astype(F32)
        grad = cot_s[rows, :].astype(F32) * valid
        cot_s[rows, :] = (n2 * vec_ref[4:5, :] + vec_ref[5:6, :]).astype(BF)
        back = norm_back(grad, n2, inv_std, vec_ref[4:5, :])
        g2_s[rows, :] = back
        glow_s[rows, :] = back.astype(BF)
        sum_ref[3:4, :] += col_sum(back)
        sum_ref[4:5, :] += col_sum(grad * n2)
        sum_ref[5:6, :] += col_sum(grad)

    staged(BLOCKS, contract, second)
    moves.start("second", (cot_s, out_ref))
    size = stage_s.shape[2]
    stages = []

    def put(side, part, column, value):
        slot = len(stages) % 2
        if column == 0 and len(stages) >= 2:
            moves.wait(stages[-2])
        stage_s[slot, :, column : column + QB] = value
        if column + QB == size:
            stages.append(("part", side, part))
            moves.start(stages[-1], (stage_s.at[slot], (dm_ref, do_ref)[side].at[part]))

    turn_s[...] = glow_s[...].T
    for side in (1, 0):
        for c in range(each):
            at = side * units + c * QB
            part, column = divmod(c * QB, size)
            put(side, part, column, nn(turn_s[...], act_s[:, at : at + QB]).astype(BF))
    turn_s[...] = low_s[...].T
    order = [(side, c) for side in (1, 0) for c in range(each)]

    def columns(n):
        side, c = order[n]
        return slice(side * units + c * QB, side * units + (c + 1) * QB)

    def pull(n):
        unit_s[n % 2] = nn(glow_s[...], w2_s[:, columns(n)])

    def lean(n):
        grad = (unit_s[n % 2] * slope_s[:, columns(n)].astype(F32)).astype(BF)
        slope_s[:, columns(n)] = grad
        hsum_ref[0:1, columns(n)] = col_sum(grad.astype(F32))

    def push(n):
        side, c = order[n]
        part, column = divmod(c * QB, size)
        put(side, 3 + part, column, nn(turn_s[...], slope_s[:, columns(n)]).astype(BF))

    staged(2 * each, pull, lean, push)
    moves.start("sums", (sum_ref, sums_out), (hsum_ref, hsum_out))
    for r in range(BLOCKS):
        rows = slice(r * QB, (r + 1) * QB)
        g2_s[rows, :] += nt(slope_s[rows, :], w1_s[...])
        moves.start(("gfn", r), (g2_s.at[rows, :], gfn_ref.at[rows, :]))
    moves.finish()


def middle(core, frames, cot, mixed, att_m, att_o, ffw_m, ffw_o, hid_m, hid_o, augk, vectors):
    width = frames.shape[1]
    units = ffw_m.shape[2]
    wide = ((SEQ, width), BF)
    full = ((SEQ, width), F32)
    thin = ((SEQ, LANES), F32)
    inner = ((width, 2 * units), BF)
    outer = ((SEQ, 2 * units), BF)
    grads = ((6, width, units // 3), BF)
    ins = (frames, cot, mixed, att_m, att_o, ffw_m, ffw_o, hid_m, hid_o, augk, vectors)
    return call(
        middle_kernel,
        "middle",
        [(SMEM, core)] + [(HBM, a) for a in ins],
        [(HBM, *out) for out in (full, thin, wide, full, grads, grads)]
        + [(HBM, (8, width), F32), (HBM, (1, 2 * units), F32)],
        [
            wide, wide, ((width, width), BF), inner, inner, wide, full, thin, wide, full, wide,
            outer, outer, ((width, SEQ), BF), ((2, width, units // 3), BF), ((2, SEQ, QB), F32),
            ((2, QB, width), F32), ((1, 2 * units), F32), ((SEQ, LANES), BF),
            (vectors.shape, F32), ((8, width), F32), ((1, 2 * units), F32),
        ],
        36,
        cost(LONG),
    )


def norm_kernel(
    count, gfn_ref, n1_ref, inv_out, mixed_ref, am_ref, ao_ref, vec_out, sums_out, hsum_out,
    g1_ref, om_ref, oo_ref, gm_ref, augd_out,
    gfn_s, n1_s, inv_ref, mixed_s, wo_s, vec_ref,
    glow_s, glt_s, gm_s, augd_ref, om_s, oo_s, sum_ref, hsum_ref, sem,
):
    moves = Copies(sem)
    g1_s = gfn_s
    moves.start("sums", (sums_out, sum_ref), (hsum_out, hsum_ref))
    moves.start("vec", (vec_out, vec_ref), (inv_out, inv_ref))
    for r in range(BLOCKS):
        rows = slice(r * QB, (r + 1) * QB)
        moves.start(
            r, (gfn_ref.at[rows, :], gfn_s.at[rows, :]), (n1_ref.at[rows, :], n1_s.at[rows, :])
        )
        if r == 0:
            moves.wait("vec", "sums", 0)
    moves.start("wo", *sides((am_ref, ao_ref), wo_s, 3))
    moves.start("mixed", (mixed_ref, mixed_s))
    for r in range(BLOCKS):
        rows = slice(r * QB, (r + 1) * QB)
        if r > 0:
            moves.wait(r)
        grad = gfn_s[rows, :]
        n1 = n1_s[rows, :]
        back = norm_back(grad, n1, inv_ref[rows, 0:1], vec_ref[1:2, :])
        g1_s[rows, :] = back
        glow_s[rows, :] = back.astype(BF)
        sum_ref[0:1, :] += col_sum(back)
        sum_ref[1:2, :] += col_sum(grad * n1)
        sum_ref[2:3, :] += col_sum(grad)
    moves.start("g1", (g1_s, g1_ref))
    moves.wait("wo", "mixed")
    lane = lane_row()
    width = wo_s.shape[0]
    head = lax.broadcasted_iota(I32, (width, LANES), 0) // HD
    spot = lax.broadcasted_iota(I32, (width, LANES), 1)
    pick = jnp.where((spot == head + 16) | (spot == head + 32), 1.0, 0.0).astype(BF)
    for r in range(BLOCKS):
        rows = slice(r * QB, (r + 1) * QB)
        gm = nn(glow_s[rows, :], wo_s[...]).astype(BF)
        gm_s[rows, :] = gm
        both = gm.astype(F32) * mixed_s[rows, :].astype(F32)
        high = both.astype(BF)
        dots = nn(high, pick) + nn((both - high.astype(F32)).astype(BF), pick)
        dot_high = dots.astype(BF).astype(F32)
        augd_ref[rows, :] = (-jnp.where(lane < 32, dot_high, dots - dot_high)).astype(BF)
    moves.start("gm", (gm_s, gm_ref), (augd_ref, augd_out))
    glt_s[...] = glow_s[...].T
    size = om_s.shape[2]
    vectors = by_block(sum_ref[...], width, 0, 6, width // count, 1)
    units = hsum_ref.shape[1] // 2
    for side, target, result in ((1, oo_s, oo_ref), (0, om_s, om_ref)):
        cols = slice(side * 3 * size, (side + 1) * 3 * size)
        product = nn(glt_s[...], mixed_s[:, cols]).astype(BF)
        for part in range(3):
            target[part] = product[:, part * size : (part + 1) * size]
        hidden = hsum_ref[:, side * units : (side + 1) * units]
        hidden = by_block(hidden, width, LANES // 2, 2, units // count // 2, 2)
        target[3] = (vectors + hidden).astype(BF)
        moves.start(("o", side), (target, result))
    moves.finish()


def norm_backward(count, gfn, n1, inv, mixed, att_m, att_o, vectors, sums, hidden_sums):
    width = n1.shape[1]
    cols = att_m.shape[2]
    wide = ((SEQ, width), BF)
    full = ((SEQ, width), F32)
    thin = ((SEQ, LANES), BF)
    grads = ((4, width, cols // 3), BF)
    ins = (gfn, n1, inv, mixed, att_m, att_o, vectors, sums, hidden_sums)
    return call(
        functools.partial(norm_kernel, count),
        "norm_backward",
        [(HBM, a) for a in ins],
        [(HBM, *out) for out in (full, grads, grads, wide, thin)],
        [
            full, full, ((SEQ, LANES), F32), wide, ((width, width), BF), (vectors.shape, F32),
            wide, ((width, SEQ), BF), wide, thin, grads, grads, (sums.shape, F32),
            (hidden_sums.shape, F32),
        ],
        21,
        cost(LONG),
    )


def heads_kernel(
    first, count, shares, joins,
    win_ref, core_ref, q_ref, k_ref, v_ref, gm_ref, augq_out, augd_out, augk_out, frames_ref,
    *refs
):
    if joins:
        before_ref, row_ref, partner_ref, refs = *refs[:3], refs[3:]
    dq_ref, dk_ref, dv_ref, refs = *refs[:3], refs[3:]
    grad_refs, refs = refs[: len(shares)], refs[len(shares) :]
    extra_ref, refs = refs[0], refs[1:]
    if joins:
        *refs, rows_s, sem = refs
        refs = (*refs, sem)
    else:
        bias_out = extra_ref
    (
        q_s, k_s, v_s, gm_s, augq_ref, augd_ref, augk_ref, x_s, kt_s, dqt_s, dk_s, dv_s, xt_s, score_s, slope_s, prob_s, back_s, outs_s, grad_s, bias_ref, block_s, sem,
    ) = refs
    cols = dk_s.shape[1]
    heads = cols // HD
    moves = Copies(sem)
    own = slice(first, first + cols)
    moves.start("k", (k_ref.at[:, own], k_s))
    moves.start(
        "in",
        *[(ref.at[:, own], to) for ref, to in ((q_ref, q_s), (v_ref, v_s), (gm_ref, gm_s))],
        (augq_out, augq_ref), (augd_out, augd_ref), (augk_out, augk_ref),
    )
    bias_ref[...] = jnp.zeros_like(bias_ref)
    dk_s[...] = jnp.zeros_like(dk_s)
    dv_s[...] = jnp.zeros_like(dv_s)
    moves.wait("k")
    kt_s[...] = k_s[...].T
    moves.wait("in")
    moves.start("x", (frames_ref.at[ds(core_ref[0] * SEQ, SEQ, SEQ), :], x_s))
    if joins:
        moves.start("before", (before_ref, bias_ref.at[:, cols:]))
        moves.start("rows", (row_ref, rows_s.at[0]), (partner_ref, rows_s.at[1]))
    masks = half_masks()
    lane = lane_row()

    def block(i, carry):
        rows = ds(i * QB, QB, QB)
        begin = win_ref[0, i]
        kind = win_ref[1, i]

        def run(width):
            span = ds(begin, width, LANES)

            def scores(p):
                tile = slice(p * LANES, (p + 1) * LANES)
                key = k_s[span, tile]
                value = v_s[span, tile]
                aug = augk_ref[span, :]
                keys = []
                values = []
                for a, mask in enumerate(masks):
                    at = first // HD + 2 * p + a
                    ones = jnp.where((lane == at + 16) | (lane == at + 32), 1.0, 0.0)
                    more = jnp.where(lane == at + 48, 1.0, ones).astype(BF)
                    ones = jnp.broadcast_to(ones.astype(BF), (width, LANES))
                    keys.append(jnp.concatenate([key * mask, aug + more], axis=1))
                    values.append(jnp.concatenate([value * mask, ones], axis=1))
                score_s[p % 2, : 2 * width] = nt(
                    jnp.concatenate(keys, axis=0),
                    jnp.concatenate([q_s[rows, tile], augq_ref[rows, :]], axis=1),
                )
                slope_s[p % 2, : 2 * width] = nt(
                    jnp.concatenate(values, axis=0),
                    jnp.concatenate([gm_s[rows, tile], augd_ref[rows, :]], axis=1),
                )

            def soften(p):
                probs = jnp.exp2(score_s[p % 2, : 2 * width])
                prob_s[p % 2, : 2 * width] = probs.astype(BF)
                back_s[p % 2, : 2 * width] = (probs * slope_s[p % 2, : 2 * width]).astype(BF)

            def collect(p):
                tile = slice(p * LANES, (p + 1) * LANES)
                query = q_s[rows, tile]
                out_grad = gm_s[rows, tile]
                values = []
                keys = []
                for a, mask in enumerate(masks):
                    here = slice((2 * p + a) * HD, (2 * p + a + 1) * HD)
                    probs = prob_s[p % 2, a * width : (a + 1) * width]
                    back = back_s[p % 2, a * width : (a + 1) * width]
                    values.append(nn(probs, out_grad * mask))
                    keys.append(nn(back, query * mask))
                    dqt_s[here, rows] = nn(kt_s[here, span], back)
                dv_s[span, tile] += values[0] + values[1]
                dk_s[span, tile] += keys[0] + keys[1]

            for step in range(heads // 2 + 2):
                if step < heads // 2:
                    scores(step)
                if step >= 2:
                    collect(step - 2)
                if 1 <= step <= heads // 2:
                    soften(step - 1)

        for index, width in enumerate(WINDOWS):
            pl.when(kind == index)(functools.partial(run, width))
        return carry

    lax.fori_loop(0, BLOCKS, block, 0)
    if joins:
        moves.wait("rows")
        place = core_ref[0] * SEQ
        moves.start(
            "both",
            (rows_s.at[0], extra_ref.at[ds(place, SEQ, SEQ), :]),
            (rows_s.at[1], extra_ref.at[ds(SEQ - place, SEQ, SEQ), :]),
        )
    outs_s[0] = (dqt_s[...] * HD ** (-0.5)).astype(BF).T
    outs_s[1] = (dk_s[...] * LN2).astype(BF)
    outs_s[2] = dv_s[...].astype(BF)
    moves.start("out", *[(outs_s.at[j], ref) for j, ref in enumerate((dq_ref, dk_ref, dv_ref))])
    moves.wait("x")
    xt_s[...] = x_s[...].T
    for j in range(3):
        grad_s[j] = nn(xt_s[...], outs_s[j]).astype(BF)
        at = 0
        for n, size in enumerate(shares):
            moves.start((j, n), (grad_s.at[j, :, at : at + size], grad_refs[n].at[j]))
            at += size
    if joins:
        moves.wait("before")
    bias_ref[0:1, :cols] = col_sum(outs_s[0].astype(F32))
    bias_ref[1:2, :cols] = col_sum(outs_s[2].astype(F32))
    width = grad_s.shape[1]
    if joins:
        side = bias_ref[...]
    else:
        side = bias_ref[:, shares[0] :]
        moves.start("bias", (bias_ref.at[:, : shares[0]], bias_out))
    block_s[...] = by_block(side, width, 0, 2, side.shape[1] // count, 1).astype(BF)
    moves.start("block", (block_s, grad_refs[-1].at[3, :, :LANES]))
    moves.finish()


def heads_backward(
    first, shares, count, win, core, q, k, v, gm, augq, augd, augk, frames, before=None
):
    width = frames.shape[1]
    cols = sum(shares)
    joins = before is not None
    part = ((SEQ, cols), BF)
    turned = ((cols, SEQ), BF)
    thin = ((SEQ, LANES), BF)
    sums = ((SEQ, cols), F32)
    ins = (q, k, v, gm, augq, augd, augk, frames) + (before if joins else ())
    grads = [(HBM, (3, width, size), BF) for size in shares[:-1]]
    grads.append((HBM, (4, width, shares[-1]), BF))
    more = [(HBM, (2 * SEQ, width), BF) if joins else (HBM, (8, shares[0]), F32)]
    total = cols + (before[0].shape[1] if joins else 0)
    return call(
        functools.partial(heads_kernel, first, count, shares, joins),
        "heads_backward",
        [(SMEM, win), (SMEM, core)] + [(HBM, a) for a in ins],
        [(HBM, *part)] * 3 + grads + more,
        [
            part, part, part, part, thin, thin, thin, ((SEQ, width), BF),
            turned, ((cols, SEQ), F32), sums, sums, ((width, SEQ), BF),
            ((2, 2 * SEQ, QB), F32), ((2, 2 * SEQ, QB), F32),
            ((2, 2 * SEQ, QB), BF), ((2, 2 * SEQ, QB), BF),
            ((3, SEQ, cols), BF), ((3, width, cols), BF), ((8, total), F32), ((width, LANES), BF),
        ]
        + ([((2, SEQ, width), BF)] if joins else []),
        24,
        cost(LONG),
    )


def input_kernel(
    qm_ref, km_ref, vm_ref, qo_ref, ko_ref, vo_ref, g1_ref, wm_ref, wo_ref, out_ref,
    w_s, left_s, g1_s, out_s, sem,
):
    cols = wm_ref.shape[2]
    moves = Copies(sem)
    for j in range(3):
        at = slice(2 * j * cols, 2 * (j + 1) * cols)
        moves.start(("w", j), *sides((wm_ref, wo_ref), w_s.at[:, at], j))
    places = []
    for ref in (qm_ref, qo_ref, km_ref, ko_ref, vm_ref, vo_ref):
        places.append((sum(r.shape[1] for _, r in places), ref))

    def fetch(r):
        rows = slice(r * QB, (r + 1) * QB)
        moves.start(
            r,
            (g1_ref.at[rows, :], g1_s.at[rows, :]),
            *[
                (ref.at[rows, :], left_s.at[rows, at : at + ref.shape[1]])
                for at, ref in places
            ],
        )

    fetch(0)
    moves.wait(*[("w", j) for j in range(3)])
    fetch(1)
    for r in range(BLOCKS):
        rows = slice(r * QB, (r + 1) * QB)
        moves.wait(r)
        if 0 < r < BLOCKS - 1:
            fetch(r + 1)
        out_s[rows, :] = (nt(left_s[rows, :], w_s[...]) + g1_s[rows, :]).astype(BF)
        moves.start(("out", r), (out_s.at[rows, :], out_ref.at[rows, :]))
    moves.finish()


def input_gradient(mine, other, g1, att_m, att_o):
    width = g1.shape[1]
    return call(
        input_kernel,
        "input_gradient",
        [(HBM, a) for a in (*mine, *other, g1, att_m, att_o)],
        [(HBM, (SEQ, width), BF)],
        [
            ((width, 3 * width), BF), ((SEQ, 3 * width), BF), ((SEQ, width), F32),
            ((SEQ, width), BF),
        ],
        6 + 8 * BLOCKS,
        cost(LONG),
        mib=26,
    )[0]


def widen_kernel(core_ref, row_ref, partner_ref, out_ref, low_s, high_s, sem):
    core = core_ref[0]
    moves = Copies(sem)
    size = SEQ // 2
    spots = [(half, slice(r * size, (r + 1) * size)) for half in range(2) for r in range(2)]
    for half, rows in spots:
        ref = (row_ref, partner_ref)[half]
        moves.start((half, rows.start), (ref.at[rows, :], low_s.at[half, rows, :]))
    for half, rows in spots:
        moves.wait((half, rows.start))
        high_s[half, rows, :] = low_s[half, rows, :].astype(F32)
        place = (core if half == 0 else 1 - core) * SEQ + rows.start
        moves.start(
            ("out", half, rows.start),
            (high_s.at[half, rows, :], out_ref.at[ds(place, size, size), :]),
        )
    moves.finish()


def widen(core, row, partner):
    return call(
        widen_kernel,
        "widen",
        [(SMEM, core), (HBM, row), (HBM, partner)],
        [(HBM, (2 * SEQ, row.shape[1]), F32)],
        [((2, *row.shape), BF), ((2, *row.shape), F32)],
        8,
        cost(5),
        mib=16,
    )[0]


def swap_cores(value):
    return lax.ppermute(value, "tensor", [(0, 1), (1, 0)])


def swap_bit(value, bit, count):
    return lax.ppermute(value, "dp", [(i, i ^ (1 << bit)) for i in range(count)])


class Reduction:
    def __init__(self, count, keep_from):
        self.count = count
        self.keep_from = keep_from
        self.memory = FREE
        self.bits = count.bit_length() - 1
        self.step = 0
        self.widths = [[], [], []]
        turn = min(self.bits, 3)
        self.orders = [
            [(n + s) % turn for s in range(turn)] + list(range(turn, self.bits)) for n in range(3)
        ]
        self.sources = [[], [], []]

    def columns(self, part):
        return sum(self.widths[part])

    def starts(self):
        return [sum(self.columns(p) for p in range(part)) for part in range(4)]

    def add(self, mine, other, leads, width, skips=(0, 0)):
        self.rows = mine.shape[1] // self.count
        every = list(range(self.bits - 1, -1, -1))
        pair = [
            value.reshape((value.shape[0],) + (2,) * self.bits + (self.rows, value.shape[2]))
            for value in (mine, other)
        ]
        for part, lead in enumerate(leads):
            for space, value, skip in zip((HBM, FREE), pair, skips):
                at = self.columns(part)
                self.sources[part].append((space, value, lead, every, skip, at, width))
            self.widths[part].append(width)

    def left(self, part, step):
        gone = self.orders[part][:step]
        return [b for b in range(self.bits - 1, -1, -1) if b not in gone]

    def jobs(self, final):
        step = self.bits if final else self.step + 1
        sent = [None if final else order[self.step] for order in self.orders]
        joined = len(set(sent)) == 1
        starts = self.starts()
        outs = []
        jobs = []
        for part in range(3):
            bits = self.left(part, step)
            dims = (2,) * len(bits) + (self.rows,)
            if joined:
                if part == 0:
                    memory = OUT if final or self.memory == OUT else HBM
                    outs.append((memory, dims + (starts[3],), F32 if final else BF))
                spot = (0, starts[part])
            else:
                memory = HBM if self.memory == FREE else OUT
                outs.append((memory, dims + (self.columns(part),), BF))
                spot = (part, 0)
            jobs.append((*spot, bits, sent[part], self.sources[part], self.widths[part]))
        if self.step >= self.keep_from and not final:
            for part in range(3):
                bits = self.left(part, step)
                dims = (2,) * len(bits) + (self.rows, self.columns(part))
                outs.append((HBM if self.memory == FREE else OUT, dims, F32))
                jobs.append(
                    (len(outs) - 1, 0, bits, None, self.sources[part], self.widths[part])
                )
        return outs, jobs

    def launch(self, values):
        turn = [order[self.step] for order in self.orders]
        kept = self.step >= self.keep_from
        sends = values[:-3] if kept else values
        if len(sends) == 1:
            got = swap_bit(sends[0], turn[0], self.count)
            moved = [(got, at) for at in self.starts()[:3]]
        else:
            moved = [(swap_bit(s, b, self.count), 0) for s, b in zip(sends, turn)]
        self.step += 1
        for part, (value, skip) in enumerate(moved):
            bits = self.left(part, self.step)
            columns = self.columns(part)
            if kept:
                own = values[part - 3]
                self.sources[part] = [(self.memory, own, None, bits, 0, 0, columns)]
            self.sources[part].append((self.memory, value, None, bits, skip, 0, columns))


def fold_kernel(jobs, spaces, spans, final, extra, place_ref, *refs):
    ins, refs = refs[: len(spaces)], refs[len(spaces) :]
    if extra:
        early_ref, refs = refs[0], refs[1:]
    results, refs = refs[: len(spans)], refs[len(spans) :]
    if final:
        squares_ref, refs = refs[0], refs[1:]
    moves = Copies(refs[-1])
    scratch = list(refs[:-1])
    outs = [ref if space == OUT else scratch.pop() for space, ref in zip(spans, results)]
    values = []
    for number, (output, column, bits, sent, sources, widths) in enumerate(jobs):
        found = []
        for which, lead, own_bits, skip, at, width in sources:
            index = [] if lead is None else [lead]
            for bit in own_bits:
                if bit in bits:
                    index.append(slice(None))
                else:
                    index.append(1 - place_ref[bit] if bit == sent else place_ref[bit])
            if spaces[which] != OUT:
                target = scratch.pop(0)
                index += [slice(None), slice(skip, skip + width)]
                moves.start((number, len(found)), (ins[which].at[tuple(index)], target))
                found.append((target, (), 0))
            else:
                found.append((ins[which], tuple(index), skip))
        values.append(found)
    squares = jnp.float32(0.0)
    for number, (output, column, bits, sent, sources, widths) in enumerate(jobs):
        total = [None for _ in widths]
        starts = [sum(widths[:n]) for n in range(len(widths))]
        for n, (which, lead, own_bits, skip, first, size) in enumerate(sources):
            if spaces[which] != OUT:
                moves.wait((number, n))
            ref, index, skip = values[number][n]
            for spot, (at, width) in enumerate(zip(starts, widths)):
                if first <= at < first + size:
                    cols = slice(skip + at - first, skip + at - first + width)
                    value = ref[(*index, Ellipsis, cols)].astype(F32)
                    total[spot] = value if total[spot] is None else total[spot] + value
        for at, width, value in zip(starts, widths, total):
            outs[output][..., column + at : column + at + width] = value.astype(
                outs[output].dtype
            )
            if final:
                squares = squares + jnp.sum(value * value)
                if number == 0 and final == "shared" and at == starts[-1]:
                    lane = lax.broadcasted_iota(I32, value.shape, 1)
                    line = lax.broadcasted_iota(I32, value.shape, 0)
                    both = jnp.where((lane < LANES // 2) & (line < 6), value, 0.0)
                    squares = squares - 0.5 * jnp.sum(both * both)
        if spans[output] != OUT:
            if output not in [job[0] for job in jobs[number + 1 :]]:
                moves.start(("out", output), (outs[output], results[output]))
    if extra:
        squares_ref[...] = jnp.full(squares_ref.shape, squares + early_ref[0, 0], F32)
    elif final:
        squares_ref[0, 0] = squares
    moves.finish()


def fold(place, reductions, final=False, extra=None):
    arrays = []
    outs = []
    jobs = []
    counts = []
    for reduction in reductions:
        shapes, todo = reduction.jobs(final)
        for output, column, bits, sent, sources, widths in todo:
            listed = []
            for space, array, *rest in sources:
                known = [n for n, (_, a) in enumerate(arrays) if a is array]
                if not known:
                    arrays.append((space, array))
                listed.append((known[0] if known else len(arrays) - 1, *rest))
            jobs.append((len(outs) + output, column, bits, sent, listed, widths))
        outs += shapes
        counts.append(len(shapes))
    scratch = []
    for output, column, bits, sent, sources, widths in jobs:
        for which, lead, own_bits, skip, at, width in sources:
            if arrays[which][0] != OUT:
                array = arrays[which][1]
                scratch.append(((2,) * len(bits) + (array.shape[-2], width), array.dtype))
    copies = len(scratch)
    for space, dims, dtype in reversed(outs):
        if space != OUT:
            scratch.append((dims, dtype))
            copies += 1

    def volume(dims):
        return 4 * functools.reduce(lambda a, b: a * b, dims)

    last = []
    if extra:
        last = [(OUT, (2 * extra[1], LANES), F32)]
    elif final:
        last = [(SMEM, (1, 1), F32)]
    size = sum(volume(dims) for dims, _ in scratch)
    size += sum(volume(a.shape) for space, a in arrays if space == OUT)
    size += sum(volume(dims) for space, dims, _ in outs if space == OUT)
    res = call(
        functools.partial(
            fold_kernel, jobs, [space for space, _ in arrays], [out[0] for out in outs], final,
            bool(extra),
        ),
        "fold",
        [(SMEM, place)] + arrays + ([(SMEM, extra[0])] if extra else []),
        outs + last,
        scratch,
        copies,
        cost(2),
        mib=4 + size // 2**20,
    )
    grouped = []
    at = 0
    for n in counts:
        grouped.append(list(res[at : at + n]))
        at += n
    return grouped + ([res[-1]] if final else [])


def tie(value, *others):
    return lax.optimization_barrier((value, others))[0]


def advance(place, reductions, after):
    values = fold(tie(place, after), reductions)
    values = lax.optimization_barrier(values)
    for reduction, value in zip(reductions, values):
        reduction.launch(value)
    return values


def update_kernel(
    squares_ref, ffn_ref, qkv_ref, aw, am, av, fw, fm, fv, *refs
):
    small, outs, norm_ref = refs[:9], refs[9:-2], refs[-2]
    norm = jnp.sqrt(col_sum(squares_ref[...])[:, 0:1])
    norm_ref[...] = norm
    factor = jnp.minimum(1.0, 1.0 / (norm + 1e-06))

    def adam(grad, weight, first, second, results, index, rate, decay):
        clipped = grad * factor
        first_new = 0.9 * first[index] + 0.1 * clipped
        second_new = 0.999 * second[index] + 0.001 * clipped * clipped
        mean_hat = first_new / (1.0 - 0.9**STEP)
        var_hat = second_new / (1.0 - 0.999**STEP)
        old = weight[index].astype(F32)
        results[0][index] = first_new
        results[1][index] = second_new
        results[2][index] = old - rate * (mean_hat / (jnp.sqrt(var_hat) + 1e-08) + decay * old)

    every = slice(None)
    each = fw.shape[2] // 3
    wide = aw.shape[2]
    rest = wide // 3
    ends = [small[3 * n].shape[1] for n in range(3)]
    here = 2 * each + rest
    lines = ffn_ref[0:6, here : here + ends[2]]
    half = ends[1] // 2
    spot = here + LANES // 2
    hidden = jnp.concatenate(
        [ffn_ref[0:1, spot : spot + half], ffn_ref[1:2, spot : spot + half]], axis=1
    )
    tails = (qkv_ref[0:2, wide : wide + ends[0]], hidden, lines)
    for j in range(3):
        at = 0 if j == 0 else LANES + j * wide
        adam(qkv_ref[:, at : at + wide], aw, am, av, outs[0:3], (j,), 0.05, 0.01)
        at = 0 if j == 0 else LANES + j * here
        cols = slice(j * rest, (j + 1) * rest)
        grad = ffn_ref[:, at + 2 * each : at + here]
        adam(grad, aw, am, av, outs[0:3], (3, every, cols), 0.05, 0.01)
        cols = slice(j * each, (j + 1) * each)
        grad = ffn_ref[:, at + each : at + 2 * each]
        adam(grad, fw, fm, fv, outs[3:6], (0, every, cols), 0.05, 0.01)
        adam(ffn_ref[:, at : at + each], fw, fm, fv, outs[3:6], (1, every, cols), 0.05, 0.01)
    for n in range(3):
        weight, first, second = small[3 * n : 3 * n + 3]
        results = outs[6 + 3 * n : 9 + 3 * n]
        adam(tails[n], weight, first, second, results, (every, every), 0.5, 0.0)


def update(squares, ffn, qkv, attention, feedforward, small):
    arrays = [squares, ffn, qkv, *attention, *feedforward]
    outs = [attention[1].shape] * 3 + [feedforward[1].shape] * 3
    for group in small:
        arrays += group
        outs += [group[0].shape] * 3
    return call(
        update_kernel,
        "update",
        [(OUT, a) for a in arrays],
        [(OUT, dims, F32) for dims in outs] + [(OUT, (1, 1), F32)],
        [],
        0,
        cost(2),
        mib=16,
    )


def local(
    frames,
    cotangent,
    segment_ids,
    pad_mask,
    attention_weight,
    feedforward_weight,
    head_bias,
    hidden_bias,
    norm_vectors,
    attention_first,
    attention_second,
    feedforward_first,
    feedforward_second,
    head_first,
    head_second,
    hidden_first,
    hidden_second,
    vector_first,
    vector_second,
):
    width = frames.shape[1]
    cols = attention_weight.shape[2]
    units = feedforward_weight.shape[2]
    count = lax.axis_size("dp")
    bits = count.bit_length() - 1
    rows = width // count
    core = lax.axis_index("tensor")
    dp_index = lax.axis_index("dp")
    core_ref = core.reshape(1).astype(I32)
    place = jnp.stack([(dp_index >> b) & 1 for b in range(bits)]).astype(I32)

    att_m, ffw_m, hid_m = attention_weight, feedforward_weight, hidden_bias
    att_o = swap_cores(att_m)
    head_o = swap_cores(head_bias)
    hid_o = swap_cores(hid_m)
    ffw_o = swap_cores(tie(ffw_m, att_o, head_o, hid_o))
    lines = (frames.shape[0] // LANES, LANES)

    q, k, v, augq, augk, mixed, win = attention_forward(
        core_ref, frames, segment_ids.reshape(lines), pad_mask.reshape(lines), att_m, att_o,
        head_bias, head_o,
    )
    n1, inv, out_row, gfn, ffn_m, ffn_o, sums, hidden_sums = middle(
        core_ref, frames, cotangent, mixed, att_m, att_o, ffw_m, ffw_o, hid_m, hid_o, augk,
        norm_vectors,
    )
    ffn_o = swap_cores(ffn_o)
    out_other = swap_cores(out_row)
    g1, om, oo, gm, augd = norm_backward(
        count, gfn, n1, inv, mixed, att_m, att_o, norm_vectors, sums, hidden_sums
    )
    oo = swap_cores(oo)
    ffn = Reduction(count, 2)
    ffn.add(ffn_m, ffn_o, (0, 1, 2), units // 3)
    ffn.add(ffn_m, ffn_o, (3, 4, 5), units // 3)
    ffn.add(om, oo, (0, 1, 2), cols // 3)
    ffn.add(om, oo, (3,), LANES)
    sent = advance(place, [ffn], gm)

    split = cols - LANES
    back = functools.partial(
        heads_backward, count=count, win=win, core=core_ref, q=q, k=k, v=v, augq=augq, augd=augd,
        augk=augk, frames=frames,
    )
    *other, last_grad, other_grad, last_bias = back(
        split, (LANES, cols), gm=tie(gm, sent)
    )
    other_grad = swap_cores(other_grad)
    sent = advance(place, [ffn], other[0])
    *mine, mine_grad, layer_output = back(
        0, (split,), gm=tie(gm, sent), before=(last_bias, out_row, out_other)
    )
    qkv = Reduction(count, 1)
    qkv.add(mine_grad, other_grad, (0, 1, 2), split)
    qkv.add(last_grad, other_grad, (0, 1, 2), LANES, (0, split))
    qkv.add(mine_grad, other_grad, (3,), LANES)
    for reduction in (qkv, ffn):
        reduction.memory = OUT
    sent = advance(place, [qkv, ffn], mine_grad)
    grad_row = input_gradient(mine, other, tie(g1, sent), att_m, att_o)
    sent = advance(place, [r for r in (qkv, ffn) if r.step < bits], grad_row)
    grad_row = tie(grad_row, sent)
    grad_other = swap_cores(grad_row)
    dp_late = tie(dp_index, sent)

    def own(value, size, axis):
        return lax.dynamic_slice_in_dim(value, dp_late * size, size, axis)

    olds = (
        own(att_m, rows, 1), own(ffw_m, rows, 1),
        own(head_bias.reshape(2, cols), cols // count, 1),
        own(hidden_bias, units // count, 1), own(norm_vectors, rows, 1),
    )
    sent = advance(place, [r for r in (qkv, ffn) if r.step < bits], (sent, olds))
    frame_grads = widen(core_ref, tie(grad_row, sent), grad_other)
    sent = (sent, frame_grads)
    while qkv.step < bits:
        sent = advance(place, [r for r in (qkv, ffn) if r.step < bits], sent)
    old_att, old_ffw, old_head, old_hidden, old_vectors = olds
    while ffn.step < bits:
        sent = advance(place, [ffn], sent)
    (ffn_sum,), early = fold(tie(place, sent), [ffn], final="shared")
    (qkv_sum,), squares = fold(tie(place, early), [qkv], final="own", extra=(early, count))
    squares = lax.all_to_all(squares, ("dp", "tensor"), 0, 0, tiled=True)

    def flat(value):
        return value.reshape(-1, value.shape[-1])

    new = update(
        squares, ffn_sum, qkv_sum,
        (old_att, attention_first, attention_second),
        (old_ffw, feedforward_first, feedforward_second),
        (
            (old_head, flat(head_first), flat(head_second)),
            (old_hidden, hidden_first, hidden_second),
            (old_vectors, vector_first, vector_second),
        ),
    )
    return (
        layer_output,
        frame_grads,
        new[15].reshape(()),
        *new[:6],
        *[value.reshape(head_first.shape) for value in new[6:9]],
        *new[9:15],
    )


def solution(mesh):
    weight_spec = P(None, None, "tensor")
    shard = P(None, "dp", "tensor")
    head = P(None, "tensor", "dp")
    hidden = P("tensor", "dp")
    vector = P(None, "dp")
    row = P("dp", None)
    return jax.shard_map(
        local,
        mesh=mesh,
        in_specs=(
            row, row, P("dp"), P("dp"),
            weight_spec, weight_spec,
            P(None, "tensor", None), P("tensor", None), P(),
            shard, shard, shard, shard,
            head, head, hidden, hidden, vector, vector,
        ),
        out_specs=(
            row, row, P(),
            shard, shard, shard, shard, shard, shard,
            head, head, head, hidden, hidden, hidden, vector, vector, vector,
        ),
        check_vma=False,
    )
```

```python
import functools

import jax
import jax.numpy as jnp
from jax import lax
from jax.experimental import pallas as pl
from jax.experimental.pallas import tpu as pltpu
from jax.sharding import PartitionSpec as P

HD = 64
SEQ = 1024
STEP = 10
LANES = 128
QB = 256
BLOCKS = SEQ // QB
BIG = 1e30
LOG2E = 1.4426950408889634
LN2 = 0.6931471805599453
WINDOWS = (384, 512, 640, 768, 1024)
BF = jnp.bfloat16
F32 = jnp.float32
I32 = jnp.int32


def nn(a, b):
    return jnp.dot(a, b, preferred_element_type=F32)


def nt(a, b):
    return lax.dot_general(a, b, (((1,), (1,)), ((), ())), preferred_element_type=F32)


def ds(start, size, step):
    return pl.ds(pl.multiple_of(start, step), size)


def shape(dims, dtype):
    return jax.ShapeDtypeStruct(dims, dtype)


LONG = 100


def cost(micros):
    return pl.CostEstimate(flops=int(1.1e9 * micros), bytes_accessed=2**20, transcendentals=0)


SMEM = "smem"
HBM = "hbm"
FREE = "free"
OUT = "out"
SPACES = {SMEM: pltpu.SMEM, HBM: pltpu.HBM, FREE: pl.ANY, OUT: pltpu.VMEM}
WHOLE = 63


def call(kernel, name, ins, outs, scratch, copies, estimate, mib=WHOLE):
    args = [
        pltpu.with_memory_space_constraint(array, pltpu.HBM) if space == HBM else array
        for space, array in ins
    ]
    return pl.pallas_call(
        kernel,
        out_shape=[
            pltpu.HBM(dims, dtype) if space == HBM else shape(dims, dtype)
            for space, dims, dtype in outs
        ],
        in_specs=[pl.BlockSpec(memory_space=SPACES[space]) for space, _ in ins],
        out_specs=[pl.BlockSpec(memory_space=SPACES[space]) for space, _, _ in outs],
        scratch_shapes=[pltpu.VMEM(dims, dtype) for dims, dtype in scratch]
        + [pltpu.SemaphoreType.DMA((max(copies, 1),))],
        compiler_params=pltpu.CompilerParams(vmem_limit_bytes=mib * 2**20),
        cost_estimate=estimate,
        name=name,
    )(*args)


class Copies:
    def __init__(self, sem):
        self.sem = sem
        self.used = 0
        self.pending = {}

    def start(self, name, *pairs):
        made = []
        for source, target in pairs:
            made.append(pltpu.make_async_copy(source, target, self.sem.at[self.used]))
            made[-1].start()
            self.used += 1
        self.pending[name] = made

    def wait(self, *names):
        for name in names:
            for copy in self.pending.pop(name):
                copy.wait()

    def finish(self):
        self.wait(*list(self.pending))


def lane_row():
    return lax.broadcasted_iota(I32, (1, LANES), 1)


def half_masks():
    low = jnp.where(lane_row() < HD, 1.0, 0.0)
    return (low.astype(BF), (1.0 - low).astype(BF))


def norm_rows(value):
    center = value - jnp.mean(value, axis=-1, keepdims=True)
    inv_std = lax.rsqrt(jnp.mean(center * center, axis=-1, keepdims=True) + 1e-05)
    return center * inv_std, inv_std


def norm_back(grad, normed, inv_std, gain):
    scaled = grad * gain
    mean_one = jnp.mean(scaled, axis=-1, keepdims=True)
    mean_two = jnp.mean(scaled * normed, axis=-1, keepdims=True)
    return inv_std * (scaled - mean_one - normed * mean_two)


def col_sum(value):
    return jnp.sum(value, axis=0, keepdims=True)


def sides(refs, target, index=None):
    size = target.shape[-1] // len(refs)
    picked = [ref if index is None else ref.at[index] for ref in refs]
    return [
        (ref, target.at[:, n * size : (n + 1) * size]) for n, ref in enumerate(picked)
    ]


def by_block(vectors, width, first, lines, each, spread):
    size = vectors.shape[1]
    count = size // (each * spread)
    rows = width // count
    if spread > 1:
        vectors = jnp.broadcast_to(vectors[0:1, :], (8, size))
    tall = jnp.concatenate([vectors] * count, axis=0)
    row = lax.broadcasted_iota(I32, (8 * count, size), 0)
    col = lax.broadcasted_iota(I32, (8 * count, size), 1)
    line = row % 8
    wanted = spread * (row // 8) + (line if spread > 1 else 0)
    picked = jnp.where((col // each == wanted) & (line < lines), tall, 0.0).astype(BF)
    source = lax.broadcasted_iota(I32, (size, LANES), 0)
    lane = lax.broadcasted_iota(I32, (size, LANES), 1)
    move = jnp.where(source % each + first == lane, 1.0, 0.0).astype(BF)
    placed = nn(picked, move).astype(BF)
    target = lax.broadcasted_iota(I32, (width, 8 * count), 0)
    origin = lax.broadcasted_iota(I32, (width, 8 * count), 1)
    spot = (target // rows == origin // 8) & (target % rows == origin % 8)
    return nn(jnp.where(spot, 1.0, 0.0).astype(BF), placed)


def staged(count, *stages):
    for step in range(count + len(stages) - 1):
        for n, stage in enumerate(stages):
            if 0 <= step - n < count:
                stage(step - n)


def window_of(seg, real, i):
    begin = jnp.min(seg[2 * i : 2 * i + 1, :])
    end = jnp.max(seg[2 * i + 1 : 2 * i + 2, :])
    start = jnp.sum(jnp.where(seg < begin, 1, 0))
    stop = jnp.minimum(jnp.sum(jnp.where(seg <= end, 1, 0)), real)
    start = (start // LANES) * LANES
    need = stop - start
    kind = jnp.int32(0)
    size = jnp.int32(WINDOWS[0])
    for index, width in enumerate(WINDOWS[:-1]):
        kind = jnp.where(need > width, index + 1, kind)
        size = jnp.where(need > width, WINDOWS[index + 1], size)
    return jnp.minimum(start, SEQ - size), kind


def attention_kernel(
    core_ref, frames_ref, seg_ref, pad_ref, wm_ref, wo_ref, bm_ref, bo_ref,
    q_ref, k_ref, v_ref, augq_out, augk_out, mixed_ref, win_ref,
    x_s, w_s, q_s, k_s, v_s, vt_s, mt_s, lse_s, score_s, prob_s, mixed_s, augq_ref, augk_ref,
    small_s, seg_s, pad_s, sem,
):
    moves = Copies(sem)
    core = core_ref[0]
    lines = ds(core * (SEQ // LANES), SEQ // LANES, SEQ // LANES)
    moves.start("seg", (seg_ref.at[lines, :], seg_s), (pad_ref.at[lines, :], pad_s))
    moves.start("x", (frames_ref.at[ds(core * SEQ, SEQ, SEQ), :], x_s))
    for j in range(2):
        moves.start(("bias", j), *sides((bm_ref, bo_ref), small_s.at[j], j))
    moves.start(0, *sides((wm_ref, wo_ref), w_s.at[0], 0))
    lane = lane_row()
    moves.wait("seg")
    seg = seg_s[...]
    pad = pad_s[...]
    real = jnp.sum(pad)
    for i in range(BLOCKS):
        begin, kind = window_of(seg, real, i)
        win_ref[0, i] = begin
        win_ref[1, i] = kind
    for b in range(SEQ // LANES):
        rows = slice(b * LANES, (b + 1) * LANES)
        ids = jnp.broadcast_to(seg[b : b + 1, :].astype(F32), (LANES, LANES)).T
        shown = jnp.broadcast_to(pad[b : b + 1, :].astype(F32), (LANES, LANES)).T
        same = lane.astype(F32) == ids
        augk_ref[rows, :] = jnp.where(
            lane == 10, 1.0 - shown, jnp.where(same, 1.0, 0.0)
        ).astype(BF)
        off = jnp.where(same, 0.0, -BIG)
        augq_ref[rows, :] = jnp.where(
            lane < 10, off, jnp.where(lane == 10, -BIG, 0.0)
        ).astype(BF)
    moves.start("augk", (augk_ref, augk_out))
    moves.wait(("bias", 0), ("bias", 1), "x", 0)
    for j in (1, 2):
        moves.start(j, *sides((wm_ref, wo_ref), w_s.at[j], j))
    bias = [small_s[j] for j in range(2)]
    q_s[...] = ((nn(x_s[...], w_s[0]) + bias[0]) * (HD ** (-0.5) * LOG2E)).astype(BF)
    moves.start("q", (q_s, q_ref))
    moves.wait(1)
    k_s[...] = nn(x_s[...], w_s[1]).astype(BF)
    moves.start("k", (k_s, k_ref))
    moves.wait(2)
    v_s[...] = (nn(x_s[...], w_s[2]) + bias[1]).astype(BF)
    moves.start("v", (v_s, v_ref))
    vt_s[...] = v_s[...].T
    lse_s[...] = jnp.zeros_like(lse_s)
    heads = q_s.shape[1] // HD
    masks = half_masks()

    def block(i, carry):
        rows = ds(i * QB, QB, QB)
        begin = win_ref[0, i]
        kind = win_ref[1, i]

        def run(width):
            span = ds(begin, width, LANES)
            ones = jnp.ones((16, width), BF)

            def score(p):
                tile = slice(p * LANES, (p + 1) * LANES)
                right = jnp.concatenate([q_s[rows, tile], augq_ref[rows, :]], axis=1)
                key = k_s[span, tile]
                aug = augk_ref[span, :]
                left = [jnp.concatenate([key * mask, aug], axis=1) for mask in masks]
                score_s[p % 2, : 2 * width] = nt(jnp.concatenate(left, axis=0), right)

            def soften(p):
                for a in range(2):
                    here = slice(a * width, (a + 1) * width)
                    top = jnp.max(score_s[p % 2, here], axis=0, keepdims=True)
                    prob_s[p % 2, here] = jnp.exp2(score_s[p % 2, here] - top).astype(BF)
                    tops[2 * p + a] = top

            def mix(p):
                for a in range(2):
                    h = 2 * p + a
                    part = slice(h * HD, (h + 1) * HD)
                    left = jnp.concatenate([vt_s[part, span], ones], axis=0)
                    out = nn(left, prob_s[p % 2, a * width : (a + 1) * width])
                    total = out[HD : HD + 1, :]
                    mt_s[part, rows] = (out[:HD, :] * (1.0 / total)).astype(BF)
                    lse = tops.pop(h) + jnp.log2(total)
                    for piece in range(3):
                        lse_s[16 * (piece + 1) + h : 16 * (piece + 1) + h + 1, rows] = lse

            tops = {}
            for step in range(heads // 2 + 2):
                if step < heads // 2:
                    score(step)
                if step >= 2:
                    mix(step - 2)
                if 1 <= step <= heads // 2:
                    soften(step - 1)

        for index, width in enumerate(WINDOWS):
            pl.when(kind == index)(functools.partial(run, width))
        mixed_s[rows, :] = mt_s[:, rows].T
        return carry

    lax.fori_loop(0, BLOCKS, block, 0)
    moves.start("mixed", (mixed_s, mixed_ref))
    lse = lse_s[...].T
    high = lse.astype(BF).astype(F32)
    mid = (lse - high).astype(BF).astype(F32)
    piece = jnp.where(lane < 32, high, jnp.where(lane < 48, mid, lse - high - mid))
    augq_ref[...] = (augq_ref[...].astype(F32) - piece).astype(BF)
    moves.start("augq", (augq_ref, augq_out))
    moves.finish()


def attention_forward(core, frames, seg, pad, att_m, att_o, bias_m, bias_o):
    width = frames.shape[1]
    wide = ((SEQ, width), BF)
    thin = ((SEQ, LANES), BF)
    line = ((SEQ // LANES, LANES), I32)
    return call(
        attention_kernel,
        "attention_forward",
        [(SMEM, core)]
        + [(HBM, a) for a in (frames, seg, pad, att_m, att_o, bias_m, bias_o)],
        [(HBM, *wide)] * 3 + [(HBM, *thin)] * 2 + [(HBM, *wide), (SMEM, (2, BLOCKS), I32)],
        [
            wide, ((3, width, width), BF), wide, wide, wide, ((width, SEQ), BF),
            ((width, SEQ), BF), ((LANES, SEQ), F32), ((2, 2 * SEQ, QB), F32), ((2, 2 * SEQ, QB), BF),
            wide, thin, thin, ((2, 1, width), F32), line, line,
        ],
        19,
        cost(LONG),
    )


def gelu_pair(value):
    phi = 0.5 + 0.5 * lax.erf(value * 0.7071067811865476)
    low = value.astype(BF)
    density = jnp.exp2(low * low * BF(-0.5 * LOG2E)) * BF(0.3989422804014327)
    return (value * phi).astype(BF), phi.astype(BF) + low * density


def chunk_of(c, size):
    each = size // QB
    return c // each, ds(c % each * QB, QB, QB)


def middle_kernel(
    core_ref, frames_ref, cot_ref, mixed_ref, am_ref, ao_ref, fm_ref, fo_ref, hm_ref, ho_ref,
    augk_out, vec_out,
    n1_ref, inv_out, out_ref, gfn_ref, dm_ref, do_ref, sums_out, hsum_out,
    x_s, mixed_s, wo_s, w1_s, w2_s, cot_s, n1_s, inv_ref, low_s, g2_s, glow_s, slope_s, act_s,
    turn_s, stage_s, unit_s, ffn_s, bias_s, augk_ref, vec_ref, sum_ref, hsum_ref, sem,
):
    units = fm_ref.shape[2]
    moves = Copies(sem)
    own = ds(core_ref[0] * SEQ, SEQ, SEQ)
    moves.start("wo", *sides((am_ref, ao_ref), wo_s, 3))
    moves.start("in", (vec_out, vec_ref), (mixed_ref, mixed_s), (frames_ref.at[own, :], x_s))
    moves.start("bias", *sides((hm_ref, ho_ref), bias_s))
    halves = sides((fm_ref, fo_ref), w1_s, 0)
    moves.wait("wo", "in")
    moves.start("w1", halves[0])
    sum_ref[...] = jnp.zeros_like(sum_ref)

    def project(r):
        rows = slice(r * QB, (r + 1) * QB)
        ffn_s[r % 2] = nt(mixed_s[rows, :], wo_s[...])

    def first_rows(r):
        rows = slice(r * QB, (r + 1) * QB)
        first = x_s[rows, :].astype(F32) + ffn_s[r % 2] + vec_ref[0:1, :]
        normed, inv_std = norm_rows(first)
        n1_s[rows, :] = normed
        inv_ref[rows, :] = jnp.broadcast_to(inv_std, (QB, LANES))
        low_s[rows, :] = (normed * vec_ref[1:2, :] + vec_ref[2:3, :]).astype(BF)

    staged(BLOCKS, project, first_rows)
    moves.wait("bias", "w1")
    moves.start("w1", halves[1])
    each = units // QB

    def up(c):
        if c == each:
            moves.wait("w1")
            moves.start("first", (n1_s, n1_ref), (inv_ref, inv_out))
            moves.start("cot", (cot_ref.at[own, :], cot_s), (augk_out, augk_ref))
            moves.start("w2", *sides((fm_ref, fo_ref), w2_s, 1))
        unit_s[c % 2] = nn(low_s[...], w1_s[:, c * QB : (c + 1) * QB])

    def bend(c):
        spot = slice(c * QB, (c + 1) * QB)
        act, slope = gelu_pair(unit_s[c % 2] + bias_s[0:1, spot])
        act_s[:, c * QB : (c + 1) * QB] = act
        slope_s[:, c * QB : (c + 1) * QB] = slope

    staged(2 * each, up, bend)
    moves.wait("cot", "w2")

    def contract(r):
        rows = slice(r * QB, (r + 1) * QB)
        ffn_s[r % 2] = nt(act_s[rows, :], w2_s[...])

    def second(r):
        rows = slice(r * QB, (r + 1) * QB)
        first_norm = n1_s[rows, :] * vec_ref[1:2, :] + vec_ref[2:3, :]
        n2, inv_std = norm_rows(first_norm + ffn_s[r % 2] + vec_ref[3:4, :])
        valid = 1.0 - augk_ref[rows, 10:11].astype(F32)
        grad = cot_s[rows, :].astype(F32) * valid
        cot_s[rows, :] = (n2 * vec_ref[4:5, :] + vec_ref[5:6, :]).astype(BF)
        back = norm_back(grad, n2, inv_std, vec_ref[4:5, :])
        g2_s[rows, :] = back
        glow_s[rows, :] = back.astype(BF)
        sum_ref[3:4, :] += col_sum(back)
        sum_ref[4:5, :] += col_sum(grad * n2)
        sum_ref[5:6, :] += col_sum(grad)

    staged(BLOCKS, contract, second)
    moves.start("second", (cot_s, out_ref))
    size = stage_s.shape[2]
    stages = []

    def put(side, part, column, value):
        slot = len(stages) % 2
        if column == 0 and len(stages) >= 2:
            moves.wait(stages[-2])
        stage_s[slot, :, column : column + QB] = value
        if column + QB == size:
            stages.append(("part", side, part))
            moves.start(stages[-1], (stage_s.at[slot], (dm_ref, do_ref)[side].at[part]))

    turn_s[...] = glow_s[...].T
    for side in (1, 0):
        for c in range(each):
            at = side * units + c * QB
            part, column = divmod(c * QB, size)
            put(side, part, column, nn(turn_s[...], act_s[:, at : at + QB]).astype(BF))
    turn_s[...] = low_s[...].T
    order = [(side, c) for side in (1, 0) for c in range(each)]

    def columns(n):
        side, c = order[n]
        return slice(side * units + c * QB, side * units + (c + 1) * QB)

    def pull(n):
        unit_s[n % 2] = nn(glow_s[...], w2_s[:, columns(n)])

    def lean(n):
        grad = (unit_s[n % 2] * slope_s[:, columns(n)].astype(F32)).astype(BF)
        slope_s[:, columns(n)] = grad
        hsum_ref[0:1, columns(n)] = col_sum(grad.astype(F32))

    def push(n):
        side, c = order[n]
        part, column = divmod(c * QB, size)
        put(side, 3 + part, column, nn(turn_s[...], slope_s[:, columns(n)]).astype(BF))

    staged(2 * each, pull, lean, push)
    moves.start("sums", (sum_ref, sums_out), (hsum_ref, hsum_out))
    for r in range(BLOCKS):
        rows = slice(r * QB, (r + 1) * QB)
        g2_s[rows, :] += nt(slope_s[rows, :], w1_s[...])
        moves.start(("gfn", r), (g2_s.at[rows, :], gfn_ref.at[rows, :]))
    moves.finish()


def middle(core, frames, cot, mixed, att_m, att_o, ffw_m, ffw_o, hid_m, hid_o, augk, vectors):
    width = frames.shape[1]
    units = ffw_m.shape[2]
    wide = ((SEQ, width), BF)
    full = ((SEQ, width), F32)
    thin = ((SEQ, LANES), F32)
    inner = ((width, 2 * units), BF)
    outer = ((SEQ, 2 * units), BF)
    grads = ((6, width, units // 3), BF)
    ins = (frames, cot, mixed, att_m, att_o, ffw_m, ffw_o, hid_m, hid_o, augk, vectors)
    return call(
        middle_kernel,
        "middle",
        [(SMEM, core)] + [(HBM, a) for a in ins],
        [(HBM, *out) for out in (full, thin, wide, full, grads, grads)]
        + [(HBM, (8, width), F32), (HBM, (1, 2 * units), F32)],
        [
            wide, wide, ((width, width), BF), inner, inner, wide, full, thin, wide, full, wide,
            outer, outer, ((width, SEQ), BF), ((2, width, units // 3), BF), ((2, SEQ, QB), F32),
            ((2, QB, width), F32), ((1, 2 * units), F32), ((SEQ, LANES), BF),
            (vectors.shape, F32), ((8, width), F32), ((1, 2 * units), F32),
        ],
        36,
        cost(LONG),
    )


def norm_kernel(
    count, gfn_ref, n1_ref, inv_out, mixed_ref, am_ref, ao_ref, vec_out, sums_out, hsum_out,
    g1_ref, om_ref, oo_ref, gm_ref, augd_out,
    gfn_s, n1_s, inv_ref, mixed_s, wo_s, vec_ref,
    glow_s, glt_s, gm_s, augd_ref, om_s, oo_s, sum_ref, hsum_ref, sem,
):
    moves = Copies(sem)
    g1_s = gfn_s
    moves.start("sums", (sums_out, sum_ref), (hsum_out, hsum_ref))
    moves.start("vec", (vec_out, vec_ref), (inv_out, inv_ref))
    for r in range(BLOCKS):
        rows = slice(r * QB, (r + 1) * QB)
        moves.start(
            r, (gfn_ref.at[rows, :], gfn_s.at[rows, :]), (n1_ref.at[rows, :], n1_s.at[rows, :])
        )
        if r == 0:
            moves.wait("vec", "sums", 0)
            moves.start("wo", *sides((am_ref, ao_ref), wo_s, 3))
    moves.start("mixed", (mixed_ref, mixed_s))
    lane = lane_row()
    width = wo_s.shape[0]
    head = lax.broadcasted_iota(I32, (width, LANES), 0) // HD
    spot = lax.broadcasted_iota(I32, (width, LANES), 1)
    pick = jnp.where((spot == head + 16) | (spot == head + 32), 1.0, 0.0).astype(BF)

    def first_rows(r):
        rows = slice(r * QB, (r + 1) * QB)
        if r > 0:
            moves.wait(r)
        grad = gfn_s[rows, :]
        n1 = n1_s[rows, :]
        back = norm_back(grad, n1, inv_ref[rows, 0:1], vec_ref[1:2, :])
        g1_s[rows, :] = back
        glow_s[rows, :] = back.astype(BF)
        sum_ref[0:1, :] += col_sum(back)
        sum_ref[1:2, :] += col_sum(grad * n1)
        sum_ref[2:3, :] += col_sum(grad)

    def mix_rows(r):
        rows = slice(r * QB, (r + 1) * QB)
        if r == 0:
            moves.wait("wo")
        gm_s[rows, :] = nn(glow_s[rows, :], wo_s[...]).astype(BF)

    def dot_rows(r):
        rows = slice(r * QB, (r + 1) * QB)
        if r == 0:
            moves.wait("mixed")
        both = gm_s[rows, :].astype(F32) * mixed_s[rows, :].astype(F32)
        high = both.astype(BF)
        dots = nn(high, pick) + nn((both - high.astype(F32)).astype(BF), pick)
        dot_high = dots.astype(BF).astype(F32)
        augd_ref[rows, :] = (-jnp.where(lane < 32, dot_high, dots - dot_high)).astype(BF)

    staged(BLOCKS, first_rows, mix_rows, dot_rows)
    moves.start("g1", (g1_s, g1_ref))
    moves.start("gm", (gm_s, gm_ref), (augd_ref, augd_out))
    glt_s[...] = glow_s[...].T
    size = om_s.shape[2]
    vectors = by_block(sum_ref[...], width, 0, 6, width // count, 1)
    units = hsum_ref.shape[1] // 2
    for side, target, result in ((1, oo_s, oo_ref), (0, om_s, om_ref)):
        cols = slice(side * 3 * size, (side + 1) * 3 * size)
        product = nn(glt_s[...], mixed_s[:, cols]).astype(BF)
        for part in range(3):
            target[part] = product[:, part * size : (part + 1) * size]
        hidden = hsum_ref[:, side * units : (side + 1) * units]
        hidden = by_block(hidden, width, LANES // 2, 2, units // count // 2, 2)
        target[3] = (vectors + hidden).astype(BF)
        moves.start(("o", side), (target, result))
    moves.finish()


def norm_backward(count, gfn, n1, inv, mixed, att_m, att_o, vectors, sums, hidden_sums):
    width = n1.shape[1]
    cols = att_m.shape[2]
    wide = ((SEQ, width), BF)
    full = ((SEQ, width), F32)
    thin = ((SEQ, LANES), BF)
    grads = ((4, width, cols // 3), BF)
    ins = (gfn, n1, inv, mixed, att_m, att_o, vectors, sums, hidden_sums)
    return call(
        functools.partial(norm_kernel, count),
        "norm_backward",
        [(HBM, a) for a in ins],
        [(HBM, *out) for out in (full, grads, grads, wide, thin)],
        [
            full, full, ((SEQ, LANES), F32), wide, ((width, width), BF), (vectors.shape, F32),
            wide, ((width, SEQ), BF), wide, thin, grads, grads, (sums.shape, F32),
            (hidden_sums.shape, F32),
        ],
        21,
        cost(LONG),
    )


def heads_kernel(
    first, count, shares, joins,
    win_ref, core_ref, q_ref, k_ref, v_ref, gm_ref, augq_out, augd_out, augk_out, frames_ref,
    *refs
):
    if joins:
        before_ref, row_ref, partner_ref, refs = *refs[:3], refs[3:]
    dq_ref, dk_ref, dv_ref, refs = *refs[:3], refs[3:]
    grad_refs, refs = refs[: len(shares)], refs[len(shares) :]
    extra_ref, refs = refs[0], refs[1:]
    if joins:
        *refs, rows_s, sem = refs
        refs = (*refs, sem)
    else:
        bias_out = extra_ref
    (
        q_s, k_s, v_s, gm_s, augq_ref, augd_ref, augk_ref, x_s, kt_s, dqt_s, dk_s, dv_s, xt_s, score_s, slope_s, prob_s, back_s, outs_s, grad_s, bias_ref, block_s, sem,
    ) = refs
    cols = dk_s.shape[1]
    heads = cols // HD
    moves = Copies(sem)
    own = slice(first, first + cols)
    moves.start("k", (k_ref.at[:, own], k_s))
    moves.start(
        "in",
        *[(ref.at[:, own], to) for ref, to in ((q_ref, q_s), (v_ref, v_s), (gm_ref, gm_s))],
        (augq_out, augq_ref), (augd_out, augd_ref), (augk_out, augk_ref),
    )
    bias_ref[...] = jnp.zeros_like(bias_ref)
    dk_s[...] = jnp.zeros_like(dk_s)
    dv_s[...] = jnp.zeros_like(dv_s)
    moves.wait("k")
    kt_s[...] = k_s[...].T
    moves.wait("in")
    moves.start("x", (frames_ref.at[ds(core_ref[0] * SEQ, SEQ, SEQ), :], x_s))
    if joins:
        moves.start("before", (before_ref, bias_ref.at[:, cols:]))
        moves.start("rows", (row_ref, rows_s.at[0]), (partner_ref, rows_s.at[1]))
    masks = half_masks()
    lane = lane_row()

    def block(i, carry):
        rows = ds(i * QB, QB, QB)
        begin = win_ref[0, i]
        kind = win_ref[1, i]

        def run(width):
            span = ds(begin, width, LANES)

            def scores(p):
                tile = slice(p * LANES, (p + 1) * LANES)
                key = k_s[span, tile]
                value = v_s[span, tile]
                aug = augk_ref[span, :]
                keys = []
                values = []
                for a, mask in enumerate(masks):
                    at = first // HD + 2 * p + a
                    ones = jnp.where((lane == at + 16) | (lane == at + 32), 1.0, 0.0)
                    more = jnp.where(lane == at + 48, 1.0, ones).astype(BF)
                    ones = jnp.broadcast_to(ones.astype(BF), (width, LANES))
                    keys.append(jnp.concatenate([key * mask, aug + more], axis=1))
                    values.append(jnp.concatenate([value * mask, ones], axis=1))
                score_s[p % 2, : 2 * width] = nt(
                    jnp.concatenate(keys, axis=0),
                    jnp.concatenate([q_s[rows, tile], augq_ref[rows, :]], axis=1),
                )
                slope_s[p % 2, : 2 * width] = nt(
                    jnp.concatenate(values, axis=0),
                    jnp.concatenate([gm_s[rows, tile], augd_ref[rows, :]], axis=1),
                )

            def soften(p):
                probs = jnp.exp2(score_s[p % 2, : 2 * width])
                prob_s[p % 2, : 2 * width] = probs.astype(BF)
                back_s[p % 2, : 2 * width] = (probs * slope_s[p % 2, : 2 * width]).astype(BF)

            def collect(p):
                tile = slice(p * LANES, (p + 1) * LANES)
                query = q_s[rows, tile]
                out_grad = gm_s[rows, tile]
                values = []
                keys = []
                for a, mask in enumerate(masks):
                    here = slice((2 * p + a) * HD, (2 * p + a + 1) * HD)
                    probs = prob_s[p % 2, a * width : (a + 1) * width]
                    back = back_s[p % 2, a * width : (a + 1) * width]
                    values.append(nn(probs, out_grad * mask))
                    keys.append(nn(back, query * mask))
                    dqt_s[here, rows] = nn(kt_s[here, span], back)
                dv_s[span, tile] += values[0] + values[1]
                dk_s[span, tile] += keys[0] + keys[1]

            for step in range(heads // 2 + 2):
                if step < heads // 2:
                    scores(step)
                if step >= 2:
                    collect(step - 2)
                if 1 <= step <= heads // 2:
                    soften(step - 1)

        for index, width in enumerate(WINDOWS):
            pl.when(kind == index)(functools.partial(run, width))
        return carry

    lax.fori_loop(0, BLOCKS, block, 0)
    if joins:
        moves.wait("rows")
        place = core_ref[0] * SEQ
        moves.start(
            "both",
            (rows_s.at[0], extra_ref.at[ds(place, SEQ, SEQ), :]),
            (rows_s.at[1], extra_ref.at[ds(SEQ - place, SEQ, SEQ), :]),
        )
    outs_s[0] = (dqt_s[...] * HD ** (-0.5)).astype(BF).T
    outs_s[1] = (dk_s[...] * LN2).astype(BF)
    outs_s[2] = dv_s[...].astype(BF)
    moves.start("out", *[(outs_s.at[j], ref) for j, ref in enumerate((dq_ref, dk_ref, dv_ref))])
    moves.wait("x")
    xt_s[...] = x_s[...].T
    for j in range(3):
        grad_s[j] = nn(xt_s[...], outs_s[j]).astype(BF)
        at = 0
        for n, size in enumerate(shares):
            moves.start((j, n), (grad_s.at[j, :, at : at + size], grad_refs[n].at[j]))
            at += size
    if joins:
        moves.wait("before")
    bias_ref[0:1, :cols] = col_sum(outs_s[0].astype(F32))
    bias_ref[1:2, :cols] = col_sum(outs_s[2].astype(F32))
    width = grad_s.shape[1]
    if joins:
        side = bias_ref[...]
    else:
        side = bias_ref[:, shares[0] :]
        moves.start("bias", (bias_ref.at[:, : shares[0]], bias_out))
    block_s[...] = by_block(side, width, 0, 2, side.shape[1] // count, 1).astype(BF)
    moves.start("block", (block_s, grad_refs[-1].at[3, :, :LANES]))
    moves.finish()


def heads_backward(
    first, shares, count, win, core, q, k, v, gm, augq, augd, augk, frames, before=None
):
    width = frames.shape[1]
    cols = sum(shares)
    joins = before is not None
    part = ((SEQ, cols), BF)
    turned = ((cols, SEQ), BF)
    thin = ((SEQ, LANES), BF)
    sums = ((SEQ, cols), F32)
    ins = (q, k, v, gm, augq, augd, augk, frames) + (before if joins else ())
    grads = [(HBM, (3, width, size), BF) for size in shares[:-1]]
    grads.append((HBM, (4, width, shares[-1]), BF))
    more = [(HBM, (2 * SEQ, width), BF) if joins else (HBM, (8, shares[0]), F32)]
    total = cols + (before[0].shape[1] if joins else 0)
    return call(
        functools.partial(heads_kernel, first, count, shares, joins),
        "heads_backward",
        [(SMEM, win), (SMEM, core)] + [(HBM, a) for a in ins],
        [(HBM, *part)] * 3 + grads + more,
        [
            part, part, part, part, thin, thin, thin, ((SEQ, width), BF),
            turned, ((cols, SEQ), F32), sums, sums, ((width, SEQ), BF),
            ((2, 2 * SEQ, QB), F32), ((2, 2 * SEQ, QB), F32),
            ((2, 2 * SEQ, QB), BF), ((2, 2 * SEQ, QB), BF),
            ((3, SEQ, cols), BF), ((3, width, cols), BF), ((8, total), F32), ((width, LANES), BF),
        ]
        + ([((2, SEQ, width), BF)] if joins else []),
        24,
        cost(LONG),
    )


def input_kernel(
    qm_ref, km_ref, vm_ref, qo_ref, ko_ref, vo_ref, g1_ref, wm_ref, wo_ref, out_ref,
    w_s, left_s, g1_s, out_s, sem,
):
    cols = wm_ref.shape[2]
    moves = Copies(sem)
    for j in range(3):
        at = slice(2 * j * cols, 2 * (j + 1) * cols)
        moves.start(("w", j), *sides((wm_ref, wo_ref), w_s.at[:, at], j))
    places = []
    for ref in (qm_ref, qo_ref, km_ref, ko_ref, vm_ref, vo_ref):
        places.append((sum(r.shape[1] for _, r in places), ref))

    def fetch(r):
        rows = slice(r * QB, (r + 1) * QB)
        moves.start(
            r,
            (g1_ref.at[rows, :], g1_s.at[rows, :]),
            *[
                (ref.at[rows, :], left_s.at[rows, at : at + ref.shape[1]])
                for at, ref in places
            ],
        )

    fetch(0)
    moves.wait(*[("w", j) for j in range(3)])
    fetch(1)
    for r in range(BLOCKS):
        rows = slice(r * QB, (r + 1) * QB)
        moves.wait(r)
        if 0 < r < BLOCKS - 1:
            fetch(r + 1)
        out_s[rows, :] = (nt(left_s[rows, :], w_s[...]) + g1_s[rows, :]).astype(BF)
        moves.start(("out", r), (out_s.at[rows, :], out_ref.at[rows, :]))
    moves.finish()


def input_gradient(mine, other, g1, att_m, att_o):
    width = g1.shape[1]
    return call(
        input_kernel,
        "input_gradient",
        [(HBM, a) for a in (*mine, *other, g1, att_m, att_o)],
        [(HBM, (SEQ, width), BF)],
        [
            ((width, 3 * width), BF), ((SEQ, 3 * width), BF), ((SEQ, width), F32),
            ((SEQ, width), BF),
        ],
        6 + 8 * BLOCKS,
        cost(LONG),
        mib=26,
    )[0]


def widen_kernel(core_ref, row_ref, partner_ref, out_ref, low_s, high_s, sem):
    core = core_ref[0]
    moves = Copies(sem)
    size = SEQ // 2
    spots = [(half, slice(r * size, (r + 1) * size)) for half in range(2) for r in range(2)]
    for half, rows in spots:
        ref = (row_ref, partner_ref)[half]
        moves.start((half, rows.start), (ref.at[rows, :], low_s.at[half, rows, :]))
    for half, rows in spots:
        moves.wait((half, rows.start))
        high_s[half, rows, :] = low_s[half, rows, :].astype(F32)
        place = (core if half == 0 else 1 - core) * SEQ + rows.start
        moves.start(
            ("out", half, rows.start),
            (high_s.at[half, rows, :], out_ref.at[ds(place, size, size), :]),
        )
    moves.finish()


def widen(core, row, partner):
    return call(
        widen_kernel,
        "widen",
        [(SMEM, core), (HBM, row), (HBM, partner)],
        [(HBM, (2 * SEQ, row.shape[1]), F32)],
        [((2, *row.shape), BF), ((2, *row.shape), F32)],
        8,
        cost(5),
        mib=16,
    )[0]


def swap_cores(value):
    return lax.ppermute(value, "tensor", [(0, 1), (1, 0)])


def swap_bit(value, bit, count):
    return lax.ppermute(value, "dp", [(i, i ^ (1 << bit)) for i in range(count)])


class Reduction:
    def __init__(self, count, keep_from):
        self.count = count
        self.keep_from = keep_from
        self.memory = FREE
        self.bits = count.bit_length() - 1
        self.step = 0
        self.widths = [[], [], []]
        turn = min(self.bits, 3)
        self.orders = [
            [(n + s) % turn for s in range(turn)] + list(range(turn, self.bits)) for n in range(3)
        ]
        self.sources = [[], [], []]

    def columns(self, part):
        return sum(self.widths[part])

    def starts(self):
        return [sum(self.columns(p) for p in range(part)) for part in range(4)]

    def add(self, mine, other, leads, width, skips=(0, 0)):
        self.rows = mine.shape[1] // self.count
        every = list(range(self.bits - 1, -1, -1))
        pair = [
            value.reshape((value.shape[0],) + (2,) * self.bits + (self.rows, value.shape[2]))
            for value in (mine, other)
        ]
        for part, lead in enumerate(leads):
            for space, value, skip in zip((HBM, FREE), pair, skips):
                at = self.columns(part)
                self.sources[part].append((space, value, lead, every, skip, at, width))
            self.widths[part].append(width)

    def left(self, part, step):
        gone = self.orders[part][:step]
        return [b for b in range(self.bits - 1, -1, -1) if b not in gone]

    def jobs(self, final):
        step = self.bits if final else self.step + 1
        sent = [None if final else order[self.step] for order in self.orders]
        joined = len(set(sent)) == 1
        starts = self.starts()
        outs = []
        jobs = []
        for part in range(3):
            bits = self.left(part, step)
            dims = (2,) * len(bits) + (self.rows,)
            if joined:
                if part == 0:
                    memory = OUT if final or self.memory == OUT else HBM
                    outs.append((memory, dims + (starts[3],), F32 if final else BF))
                spot = (0, starts[part])
            else:
                memory = HBM if self.memory == FREE else OUT
                outs.append((memory, dims + (self.columns(part),), BF))
                spot = (part, 0)
            jobs.append((*spot, bits, sent[part], self.sources[part], self.widths[part]))
        if self.step >= self.keep_from and not final:
            for part in range(3):
                bits = self.left(part, step)
                dims = (2,) * len(bits) + (self.rows, self.columns(part))
                outs.append((HBM if self.memory == FREE else OUT, dims, F32))
                jobs.append(
                    (len(outs) - 1, 0, bits, None, self.sources[part], self.widths[part])
                )
        return outs, jobs

    def launch(self, values):
        turn = [order[self.step] for order in self.orders]
        kept = self.step >= self.keep_from
        sends = values[:-3] if kept else values
        if len(sends) == 1:
            got = swap_bit(sends[0], turn[0], self.count)
            moved = [(got, at) for at in self.starts()[:3]]
        else:
            moved = [(swap_bit(s, b, self.count), 0) for s, b in zip(sends, turn)]
        self.step += 1
        for part, (value, skip) in enumerate(moved):
            bits = self.left(part, self.step)
            columns = self.columns(part)
            if kept:
                own = values[part - 3]
                self.sources[part] = [(self.memory, own, None, bits, 0, 0, columns)]
            self.sources[part].append((self.memory, value, None, bits, skip, 0, columns))


def fold_kernel(jobs, spaces, spans, final, extra, place_ref, *refs):
    ins, refs = refs[: len(spaces)], refs[len(spaces) :]
    if extra:
        early_ref, refs = refs[0], refs[1:]
    results, refs = refs[: len(spans)], refs[len(spans) :]
    if final:
        squares_ref, refs = refs[0], refs[1:]
    moves = Copies(refs[-1])
    scratch = list(refs[:-1])
    outs = [ref if space == OUT else scratch.pop() for space, ref in zip(spans, results)]
    values = []
    for number, (output, column, bits, sent, sources, widths) in enumerate(jobs):
        found = []
        for which, lead, own_bits, skip, at, width in sources:
            index = [] if lead is None else [lead]
            for bit in own_bits:
                if bit in bits:
                    index.append(slice(None))
                else:
                    index.append(1 - place_ref[bit] if bit == sent else place_ref[bit])
            if spaces[which] != OUT:
                target = scratch.pop(0)
                index += [slice(None), slice(skip, skip + width)]
                moves.start((number, len(found)), (ins[which].at[tuple(index)], target))
                found.append((target, (), 0))
            else:
                found.append((ins[which], tuple(index), skip))
        values.append(found)
    squares = jnp.float32(0.0)
    for number, (output, column, bits, sent, sources, widths) in enumerate(jobs):
        total = [None for _ in widths]
        starts = [sum(widths[:n]) for n in range(len(widths))]
        for n, (which, lead, own_bits, skip, first, size) in enumerate(sources):
            if spaces[which] != OUT:
                moves.wait((number, n))
            ref, index, skip = values[number][n]
            for spot, (at, width) in enumerate(zip(starts, widths)):
                if first <= at < first + size:
                    cols = slice(skip + at - first, skip + at - first + width)
                    value = ref[(*index, Ellipsis, cols)].astype(F32)
                    total[spot] = value if total[spot] is None else total[spot] + value
        for at, width, value in zip(starts, widths, total):
            outs[output][..., column + at : column + at + width] = value.astype(
                outs[output].dtype
            )
            if final:
                squares = squares + jnp.sum(value * value)
                if number == 0 and final == "shared" and at == starts[-1]:
                    lane = lax.broadcasted_iota(I32, value.shape, 1)
                    line = lax.broadcasted_iota(I32, value.shape, 0)
                    both = jnp.where((lane < LANES // 2) & (line < 6), value, 0.0)
                    squares = squares - 0.5 * jnp.sum(both * both)
        if spans[output] != OUT:
            if output not in [job[0] for job in jobs[number + 1 :]]:
                moves.start(("out", output), (outs[output], results[output]))
    if extra:
        squares_ref[...] = jnp.full(squares_ref.shape, squares + early_ref[0, 0], F32)
    elif final:
        squares_ref[0, 0] = squares
    moves.finish()


def fold(place, reductions, final=False, extra=None):
    arrays = []
    outs = []
    jobs = []
    counts = []
    for reduction in reductions:
        shapes, todo = reduction.jobs(final)
        for output, column, bits, sent, sources, widths in todo:
            listed = []
            for space, array, *rest in sources:
                known = [n for n, (_, a) in enumerate(arrays) if a is array]
                if not known:
                    arrays.append((space, array))
                listed.append((known[0] if known else len(arrays) - 1, *rest))
            jobs.append((len(outs) + output, column, bits, sent, listed, widths))
        outs += shapes
        counts.append(len(shapes))
    scratch = []
    for output, column, bits, sent, sources, widths in jobs:
        for which, lead, own_bits, skip, at, width in sources:
            if arrays[which][0] != OUT:
                array = arrays[which][1]
                scratch.append(((2,) * len(bits) + (array.shape[-2], width), array.dtype))
    copies = len(scratch)
    for space, dims, dtype in reversed(outs):
        if space != OUT:
            scratch.append((dims, dtype))
            copies += 1

    def volume(dims):
        return 4 * functools.reduce(lambda a, b: a * b, dims)

    last = []
    if extra:
        last = [(OUT, (2 * extra[1], LANES), F32)]
    elif final:
        last = [(SMEM, (1, 1), F32)]
    size = sum(volume(dims) for dims, _ in scratch)
    size += sum(volume(a.shape) for space, a in arrays if space == OUT)
    size += sum(volume(dims) for space, dims, _ in outs if space == OUT)
    res = call(
        functools.partial(
            fold_kernel, jobs, [space for space, _ in arrays], [out[0] for out in outs], final,
            bool(extra),
        ),
        "fold",
        [(SMEM, place)] + arrays + ([(SMEM, extra[0])] if extra else []),
        outs + last,
        scratch,
        copies,
        cost(2),
        mib=4 + size // 2**20,
    )
    grouped = []
    at = 0
    for n in counts:
        grouped.append(list(res[at : at + n]))
        at += n
    return grouped + ([res[-1]] if final else [])


def tie(value, *others):
    return lax.optimization_barrier((value, others))[0]


def advance(place, reductions, after):
    values = fold(tie(place, after), reductions)
    values = lax.optimization_barrier(values)
    for reduction, value in zip(reductions, values):
        reduction.launch(value)
    return values


def update_kernel(
    squares_ref, ffn_ref, qkv_ref, aw, am, av, fw, fm, fv, *refs
):
    small, outs, norm_ref = refs[:9], refs[9:-2], refs[-2]
    norm = jnp.sqrt(col_sum(squares_ref[...])[:, 0:1])
    norm_ref[...] = norm
    factor = jnp.minimum(1.0, 1.0 / (norm + 1e-06))

    def adam(grad, weight, first, second, results, index, rate, decay):
        clipped = grad * factor
        first_new = 0.9 * first[index] + 0.1 * clipped
        second_new = 0.999 * second[index] + 0.001 * clipped * clipped
        mean_hat = first_new / (1.0 - 0.9**STEP)
        var_hat = second_new / (1.0 - 0.999**STEP)
        old = weight[index].astype(F32)
        results[0][index] = first_new
        results[1][index] = second_new
        results[2][index] = old - rate * (mean_hat / (jnp.sqrt(var_hat) + 1e-08) + decay * old)

    every = slice(None)
    each = fw.shape[2] // 3
    wide = aw.shape[2]
    rest = wide // 3
    ends = [small[3 * n].shape[1] for n in range(3)]
    here = 2 * each + rest
    lines = ffn_ref[0:6, here : here + ends[2]]
    half = ends[1] // 2
    spot = here + LANES // 2
    hidden = jnp.concatenate(
        [ffn_ref[0:1, spot : spot + half], ffn_ref[1:2, spot : spot + half]], axis=1
    )
    tails = (qkv_ref[0:2, wide : wide + ends[0]], hidden, lines)
    for j in range(3):
        at = 0 if j == 0 else LANES + j * wide
        adam(qkv_ref[:, at : at + wide], aw, am, av, outs[0:3], (j,), 0.05, 0.01)
        at = 0 if j == 0 else LANES + j * here
        cols = slice(j * rest, (j + 1) * rest)
        grad = ffn_ref[:, at + 2 * each : at + here]
        adam(grad, aw, am, av, outs[0:3], (3, every, cols), 0.05, 0.01)
        cols = slice(j * each, (j + 1) * each)
        grad = ffn_ref[:, at + each : at + 2 * each]
        adam(grad, fw, fm, fv, outs[3:6], (0, every, cols), 0.05, 0.01)
        adam(ffn_ref[:, at : at + each], fw, fm, fv, outs[3:6], (1, every, cols), 0.05, 0.01)
    for n in range(3):
        weight, first, second = small[3 * n : 3 * n + 3]
        results = outs[6 + 3 * n : 9 + 3 * n]
        adam(tails[n], weight, first, second, results, (every, every), 0.5, 0.0)


def update(squares, ffn, qkv, attention, feedforward, small):
    arrays = [squares, ffn, qkv, *attention, *feedforward]
    outs = [attention[1].shape] * 3 + [feedforward[1].shape] * 3
    for group in small:
        arrays += group
        outs += [group[0].shape] * 3
    return call(
        update_kernel,
        "update",
        [(OUT, a) for a in arrays],
        [(OUT, dims, F32) for dims in outs] + [(OUT, (1, 1), F32)],
        [],
        0,
        cost(2),
        mib=16,
    )


def local(
    frames,
    cotangent,
    segment_ids,
    pad_mask,
    attention_weight,
    feedforward_weight,
    head_bias,
    hidden_bias,
    norm_vectors,
    attention_first,
    attention_second,
    feedforward_first,
    feedforward_second,
    head_first,
    head_second,
    hidden_first,
    hidden_second,
    vector_first,
    vector_second,
):
    width = frames.shape[1]
    cols = attention_weight.shape[2]
    units = feedforward_weight.shape[2]
    count = lax.axis_size("dp")
    bits = count.bit_length() - 1
    rows = width // count
    core = lax.axis_index("tensor")
    dp_index = lax.axis_index("dp")
    core_ref = core.reshape(1).astype(I32)
    place = jnp.stack([(dp_index >> b) & 1 for b in range(bits)]).astype(I32)

    att_m, ffw_m, hid_m = attention_weight, feedforward_weight, hidden_bias
    att_o = swap_cores(att_m)
    head_o = swap_cores(head_bias)
    hid_o = swap_cores(hid_m)
    ffw_o = swap_cores(tie(ffw_m, att_o, head_o, hid_o))
    lines = (frames.shape[0] // LANES, LANES)

    q, k, v, augq, augk, mixed, win = attention_forward(
        core_ref, frames, segment_ids.reshape(lines), pad_mask.reshape(lines), att_m, att_o,
        head_bias, head_o,
    )
    n1, inv, out_row, gfn, ffn_m, ffn_o, sums, hidden_sums = middle(
        core_ref, frames, cotangent, mixed, att_m, att_o, ffw_m, ffw_o, hid_m, hid_o, augk,
        norm_vectors,
    )
    ffn_o = swap_cores(ffn_o)
    out_other = swap_cores(out_row)
    g1, om, oo, gm, augd = norm_backward(
        count, gfn, n1, inv, mixed, att_m, att_o, norm_vectors, sums, hidden_sums
    )
    oo = swap_cores(oo)
    ffn = Reduction(count, 2)
    ffn.add(ffn_m, ffn_o, (0, 1, 2), units // 3)
    ffn.add(ffn_m, ffn_o, (3, 4, 5), units // 3)
    ffn.add(om, oo, (0, 1, 2), cols // 3)
    ffn.add(om, oo, (3,), LANES)
    sent = advance(place, [ffn], gm)

    split = cols - LANES
    back = functools.partial(
        heads_backward, count=count, win=win, core=core_ref, q=q, k=k, v=v, augq=augq, augd=augd,
        augk=augk, frames=frames,
    )
    *other, last_grad, other_grad, last_bias = back(
        split, (LANES, cols), gm=tie(gm, sent)
    )
    other_grad = swap_cores(other_grad)
    sent = advance(place, [ffn], other[0])
    *mine, mine_grad, layer_output = back(
        0, (split,), gm=tie(gm, sent), before=(last_bias, out_row, out_other)
    )
    qkv = Reduction(count, 1)
    qkv.add(mine_grad, other_grad, (0, 1, 2), split)
    qkv.add(last_grad, other_grad, (0, 1, 2), LANES, (0, split))
    qkv.add(mine_grad, other_grad, (3,), LANES)
    for reduction in (qkv, ffn):
        reduction.memory = OUT
    sent = advance(place, [qkv, ffn], mine_grad)
    grad_row = input_gradient(mine, other, tie(g1, sent), att_m, att_o)
    sent = advance(place, [r for r in (qkv, ffn) if r.step < bits], grad_row)
    grad_row = tie(grad_row, sent)
    grad_other = swap_cores(grad_row)
    dp_late = tie(dp_index, sent)

    def own(value, size, axis):
        return lax.dynamic_slice_in_dim(value, dp_late * size, size, axis)

    olds = (
        own(att_m, rows, 1), own(ffw_m, rows, 1),
        own(head_bias.reshape(2, cols), cols // count, 1),
        own(hidden_bias, units // count, 1), own(norm_vectors, rows, 1),
    )
    sent = advance(place, [r for r in (qkv, ffn) if r.step < bits], (sent, olds))
    frame_grads = widen(core_ref, tie(grad_row, sent), grad_other)
    sent = (sent, frame_grads)
    while qkv.step < bits:
        sent = advance(place, [r for r in (qkv, ffn) if r.step < bits], sent)
    old_att, old_ffw, old_head, old_hidden, old_vectors = olds
    while ffn.step < bits:
        sent = advance(place, [ffn], sent)
    (ffn_sum,), early = fold(tie(place, sent), [ffn], final="shared")
    (qkv_sum,), squares = fold(tie(place, early), [qkv], final="own", extra=(early, count))
    squares = lax.all_to_all(squares, ("dp", "tensor"), 0, 0, tiled=True)

    def flat(value):
        return value.reshape(-1, value.shape[-1])

    new = update(
        squares, ffn_sum, qkv_sum,
        (old_att, attention_first, attention_second),
        (old_ffw, feedforward_first, feedforward_second),
        (
            (old_head, flat(head_first), flat(head_second)),
            (old_hidden, hidden_first, hidden_second),
            (old_vectors, vector_first, vector_second),
        ),
    )
    return (
        layer_output,
        frame_grads,
        new[15].reshape(()),
        *new[:6],
        *[value.reshape(head_first.shape) for value in new[6:9]],
        *new[9:15],
    )


def solution(mesh):
    weight_spec = P(None, None, "tensor")
    shard = P(None, "dp", "tensor")
    head = P(None, "tensor", "dp")
    hidden = P("tensor", "dp")
    vector = P(None, "dp")
    row = P("dp", None)
    return jax.shard_map(
        local,
        mesh=mesh,
        in_specs=(
            row, row, P("dp"), P("dp"),
            weight_spec, weight_spec,
            P(None, "tensor", None), P("tensor", None), P(),
            shard, shard, shard, shard,
            head, head, hidden, hidden, vector, vector,
        ),
        out_specs=(
            row, row, P(),
            shard, shard, shard, shard, shard, shard,
            head, head, head, hidden, hidden, hidden, vector, vector, vector,
        ),
        check_vma=False,
    )
```
